256 devices in a mesh: box: 128 (over z, y, x), slab: 2 (over core).
Axes of the slice: x: 4, y: 4, z: 8, core: 2. Of those that a mesh axis runs over, the one named last changes fastest.
Arguments:
- pressure_guess: float32 [16, 4096, 256], P('slab', 'box'), may hold values from -3 to 3
- right_side: float32 [16, 4096, 256], P('slab', 'box'), may hold values from -4 to 4
- coefficient: float32 [16, 4096, 256], P('slab', 'box'), may hold values from 0.2 to 5
Outputs:
- solution: float32 [16, 4096, 256], P('slab', 'box')
- residual: float32 [16, 4096, 256], P('slab', 'box')
The draws below stay inside these ranges and needn't reach their ends.
All inputs are finite; a program needn't handle non-finite values.
Results may differ from the reference program's by a relative error of at most 0.0003.
Values sent between devices are 32-bit elements; how exact they have to be, the bound alone decides.
No kernel may reach another device: no remote copies, remote signals or barrier semaphores. Data moves between devices by JAX's collectives and lax.ppermute only.
A program may use at most 192 MiB of HBM per device.

```python
import math
import jax
import jax.numpy as jnp
from jax import lax

LEVELS = 4
NU = 2
COARSE_ITERS = 8
NZ = 16
NX = 4096
NY = 256


def draw_right_side(key, part):
    key = jax.random.fold_in(key, 11)
    extent = (NZ, NX, NY)
    values = jax.random.truncated_normal(key, -4.0, 4.0, extent, jnp.float32)
    return values.astype(jnp.float32)


def block_scale(rng, dims, pieces, smallest, largest):
    gain, own = 1.0, jax.random.fold_in(rng, 6)
    for axis_at, shards_of in pieces:
        steps = jnp.exp(jax.random.uniform(jax.random.fold_in(own, axis_at), (shards_of,), jnp.float32, smallest / len(pieces), largest / len(pieces)))
        gain = gain * jnp.repeat(steps, dims[axis_at] // shards_of).reshape([-1 if axis == axis_at else 1 for axis in range(len(dims))])
    return gain


def noise(stream_key, dims, scale, bound, cuts=(), dtype=jnp.bfloat16):
    loudness = block_scale(stream_key, dims, cuts, -0.22, 0.18) if cuts else 1.0
    values = jax.random.normal(stream_key, dims, jnp.float32) * scale * loudness
    return jnp.minimum(jnp.maximum(values, -bound), bound).astype(dtype)


def setup_inputs(seed: int = 0) -> dict:
    arg_keys = jax.random.split(jax.random.key(seed), 4)
    pressure_guess = noise(arg_keys[0], (NZ, NX, NY), 0.5, 3.0, ((0, 2), (1, 128)), jnp.float32)
    right_side = draw_right_side(jax.random.fold_in(arg_keys[3], 71), 0)
    coefficient = jnp.clip(jnp.exp(math.log(5.0) - 3.218876 * jax.random.uniform(arg_keys[2], (NZ, NX, NY), jnp.float32) ** block_scale(arg_keys[2], (NZ, NX, NY), ((0, 2), (1, 128)), -0.2, 0.2)), 0.2, 5.0)
    return dict(pressure_guess=pressure_guess, right_side=right_side, coefficient=coefficient)


def face_terms(coefficient_padded, factor):
    along_first = 0.5 * (coefficient_padded[1:, 1:-1, 1:-1] + coefficient_padded[:-1, 1:-1, 1:-1]) * factor
    along_second = 0.5 * (coefficient_padded[1:-1, 1:, 1:-1] + coefficient_padded[1:-1, :-1, 1:-1]) * factor
    along_third = 0.5 * (coefficient_padded[1:-1, 1:-1, 1:] + coefficient_padded[1:-1, 1:-1, :-1]) * factor
    center = (along_first[1:] + along_first[:-1]) + (along_second[:, 1:] + along_second[:, :-1]) + (along_third[:, :, 1:] + along_third[:, :, :-1])
    return along_first, along_second, along_third, center


def neighbour_sum(padded, face_set):
    along_first, along_second, along_third, center = face_set
    summed = along_first[1:] * padded[2:, 1:-1, 1:-1] + along_first[:-1] * padded[:-2, 1:-1, 1:-1]
    summed = summed + (along_second[:, 1:] * padded[1:-1, 2:, 1:-1] + along_second[:, :-1] * padded[1:-1, :-2, 1:-1])
    summed = summed + (along_third[:, :, 1:] * padded[1:-1, 1:-1, 2:] + along_third[:, :, :-1] * padded[1:-1, 1:-1, :-2])
    return summed


def colour_cells(extent, parity):
    summed = lax.broadcasted_iota(jnp.int32, extent, 0) + lax.broadcasted_iota(jnp.int32, extent, 1) + lax.broadcasted_iota(jnp.int32, extent, 2)
    return summed % 2 == parity


def zero_pad(values):
    return jnp.pad(values, 1)


def smooth_half(solution, source, face_set, cells, pad_cells):
    updated = (source + neighbour_sum(pad_cells(solution), face_set)) / face_set[3]
    return jnp.where(cells, updated, solution)


def first_half(source, face_set, cells):
    return jnp.where(cells, source / face_set[3], jnp.zeros_like(source))


def residual_of(solution, source, face_set, pad_cells):
    return source - (face_set[3] * solution - neighbour_sum(pad_cells(solution), face_set))


def coarse_solve(source, face_set):
    solution = jnp.zeros_like(source)
    remainder = source
    direction = source
    norm_now = jnp.sum(remainder * remainder)
    for repeat_index in range(COARSE_ITERS):
        image = face_set[3] * direction - neighbour_sum(zero_pad(direction), face_set)
        alpha = norm_now / jnp.sum(direction * image)
        solution = solution + alpha * direction
        remainder = remainder - alpha * image
        norm_next = jnp.sum(remainder * remainder)
        direction = remainder + (norm_next / norm_now) * direction
        norm_now = norm_next
    return solution


def coarsen(values):
    grouped = values.reshape(values.shape[0] // 2, 2, values.shape[1] // 2, 2, values.shape[2] // 2, 2)
    return jnp.sum(grouped, axis=(1, 3, 5)) * 0.125


def refine(values):
    return jnp.repeat(jnp.repeat(jnp.repeat(values, 2, axis=0), 2, axis=1), 2, axis=2)


def cycle(level_index, initial, source, coefficient):
    face_set = face_terms(zero_pad(coefficient), 0.25 ** level_index)
    red_cells = colour_cells(source.shape, 0)
    black_cells = colour_cells(source.shape, 1)
    if level_index == LEVELS - 1:
        return coarse_solve(source, face_set), face_set
    if level_index == 0:
        solution = smooth_half(initial, source, face_set, red_cells, zero_pad)
    else:
        solution = first_half(source, face_set, red_cells)
    solution = smooth_half(solution, source, face_set, black_cells, zero_pad)
    for repeat_index in range(NU - 1):
        solution = smooth_half(solution, source, face_set, red_cells, zero_pad)
        solution = smooth_half(solution, source, face_set, black_cells, zero_pad)
    residual = residual_of(solution, source, face_set, zero_pad)
    correction, unused = cycle(level_index + 1, None, coarsen(residual), coarsen(coefficient))
    solution = solution + refine(correction)
    for repeat_index in range(NU):
        solution = smooth_half(solution, source, face_set, red_cells, zero_pad)
        solution = smooth_half(solution, source, face_set, black_cells, zero_pad)
    return solution, face_set


def reference(pressure_guess, right_side, coefficient):
    solution, face_set = cycle(0, pressure_guess, right_side, coefficient)
    return solution, residual_of(solution, right_side, face_set, zero_pad)
```

```python
import functools

import jax
import jax.numpy as jnp
from jax import lax
from jax.experimental import pallas as pl
from jax.experimental.pallas import tpu as pltpu
from jax.sharding import PartitionSpec as P

ITERS = 8
F32 = jnp.float32
BF16 = jnp.bfloat16

H0 = 9
H1 = 12
N0 = 32 + 2 * H0
N1 = 16 + 2 * (H1 + 1)
N2 = 24
ROWS = 20
EDGE = 184
SEND1 = H1 + (H1 + 1) + 8


def matmul(x, m):
    high = x.astype(BF16)
    rest = x - high.astype(F32)
    mid = rest.astype(BF16)
    low = (rest - mid.astype(F32)).astype(BF16)
    dot = functools.partial(jnp.dot, preferred_element_type=F32)
    return dot(high, m) + (dot(mid, m) + dot(low, m))


def one_hot(shape, rule):
    i = lax.broadcasted_iota(jnp.int32, shape, 0)
    j = lax.broadcasted_iota(jnp.int32, shape, 1)
    return rule(i, j).astype(F32).astype(BF16)


def iota(shape, axis):
    return lax.broadcasted_iota(jnp.int32, shape, axis)


def up(v, axis):
    return pltpu.roll(v, v.shape[axis] - 1, axis)


def down(v, axis):
    return pltpu.roll(v, 1, axis)


def slab_rows(x, half, odd):
    return pl.ds((x // 8) * 16 + half * 8 + x % 8 + 64 * odd, 4, stride=128)


def pack_kernel(g, r, c, low, high):
    even_y = (iota((4, 128), 1) & 1) == 0
    odd_y = jnp.logical_not(even_y)
    for x in range(32):
        out, base = (low, x * ROWS) if x < 16 else (high, (x - 16) * ROWS)
        p0 = even_y if x % 2 == 0 else odd_y
        for half in range(2):
            lanes = slice(128 * half, 128 * half + 128)
            even, odd = slab_rows(x, half, 0), slab_rows(x, half, 1)
            out[base : base + 4, lanes] = c[even, :]
            out[base + 4 : base + 8, lanes] = c[odd, :]
            fe, fo = r[even, :], r[odd, :]
            out[base + 8 : base + 12, lanes] = jnp.where(p0, fe, fo)
            out[base + 12 : base + 16, lanes] = jnp.where(p0, fo, fe)
            out[base + 16 : base + 20, lanes] = jnp.where(p0, g[odd, :], g[even, :])


def parity(i, shape, shift):
    return ((iota(shape, 1) + i + shift) & 1) == 0


def nsum_packed(lv, v, xa, xb, ya, yb, i, p):
    here = v[i]
    t = xa[i] * v[i + 1] + xb[i - 1] * v[i - 1]
    t = t + (ya[i] * up(here, 1) + down(yb[i] * here, 1))
    cross = lv["c"][i]
    z = jnp.where(p, down(cross * here, 0), cross * up(here, 0))
    return t + (lv["s"][i] * here + z)


def sweep_packed(lv, red, first, last):
    def body(i, carry):
        p = parity(i, (8, 256), 1)
        if red:
            n = nsum_packed(lv, lv["vB"], lv["xR"], lv["xB"], lv["yR"], lv["yB"], i, p)
            lv["vR"][i] = (lv["fR"][i] + n) * lv["iR"][i]
        else:
            p = jnp.logical_not(p)
            n = nsum_packed(lv, lv["vR"], lv["xB"], lv["xR"], lv["yB"], lv["yR"], i, p)
            lv["vB"][i] = (lv["fB"][i] + n) * lv["iB"][i]
        return carry

    lax.fori_loop(first, last, body, 0, unroll=6)


def residual_packed(lv, i):
    p = parity(i, (8, 256), 1)
    n = nsum_packed(lv, lv["vB"], lv["xR"], lv["xB"], lv["yR"], lv["yB"], i, p)
    r_red = lv["fR"][i] - (lv["cR"][i] * lv["vR"][i] - n)
    q = jnp.logical_not(p)
    n = nsum_packed(lv, lv["vR"], lv["xB"], lv["xR"], lv["yB"], lv["yR"], i, q)
    r_black = lv["fB"][i] - (lv["cB"][i] * lv["vB"][i] - n)
    return r_red, r_black, p


PACKED = ("vB", "fR", "fB", "xR", "xB", "yR", "yB", "s", "c", "iR", "iB", "cR", "cB")


def fine_kernel(place, lo, hi, halo, *refs):
    outs = dict(zip(PACKED, refs))
    own, send, bottom = refs[len(PACKED) : len(PACKED) + 3]
    vR, bE, bO, pair_r, pair_b, tmp = refs[len(PACKED) + 3 :]
    lv = dict(outs, vR=vR)
    slab, box, boxes = place[0], place[1], place[2]

    def source(t, i):
        if i < H0:
            return halo.at[t, 0], i * ROWS + (EDGE - H0 * ROWS)
        if i >= H0 + 32:
            return halo.at[t, 1], (i - H0 - 32) * ROWS
        x = i - H0
        return (lo.at[t], x * ROWS) if x < 16 else (hi.at[t], (x - 16) * ROWS)

    for i in range(N0):
        for t in range(2):
            ref, base = source(t, i)
            for k, out in enumerate((bE, bO, lv["fR"], lv["fB"], lv["vB"])):
                out[i, 4 * t : 4 * t + 4, :] = ref[base + 4 * k : base + 4 * k + 4, :]

    row, lane = iota((8, 256), 0), iota((8, 256), 1)
    top, bot = row == 7, row == 0
    end, begin = lane == 255, lane == 0

    def faces(i, carry):
        p = parity(i, (8, 256), 1)
        e, o = bE[i], bO[i]
        fxe, fxo = 0.5 * (e + bE[i + 1]), 0.5 * (o + bO[i + 1])
        lv["xR"][i] = jnp.where(p, fxe, fxo)
        lv["xB"][i] = jnp.where(p, fxo, fxe)
        fye = 0.5 * (e + jnp.where(end, 0.0, up(e, 1)))
        fyo = 0.5 * (o + jnp.where(end, 0.0, up(o, 1)))
        gye = 0.5 * (e + jnp.where(begin, 0.0, down(e, 1)))
        gyo = 0.5 * (o + jnp.where(begin, 0.0, down(o, 1)))
        yr, yb = jnp.where(p, fye, fyo), jnp.where(p, fyo, fye)
        lv["yR"][i] = jnp.where(end, 0.0, yr)
        lv["yB"][i] = jnp.where(end, 0.0, yb)
        s = 0.5 * (e + o)
        above = 0.5 * (o + jnp.where(top, 0.0, up(e, 0)))
        below = 0.5 * (e + jnp.where(bot, 0.0, down(o, 0)))
        lv["s"][i] = s
        lv["c"][i] = jnp.where(top, 0.0, above)
        ze, zo = fye + gye + (s + below), fyo + gyo + (s + above)
        lv["cR"][i] = jnp.where(p, ze, zo)
        lv["cB"][i] = jnp.where(p, zo, ze)
        return carry

    lax.fori_loop(0, N0 - 1, faces, 0, unroll=7)

    def inverses(i, carry):
        x = box * 32 - H0 + i
        inside = jnp.logical_and(x >= 0, x < boxes * 32)
        cr = lv["cR"][i] + (lv["xR"][i] + lv["xB"][i - 1])
        cb = lv["cB"][i] + (lv["xB"][i] + lv["xR"][i - 1])
        lv["cR"][i] = cr
        lv["cB"][i] = cb
        lv["iR"][i] = jnp.where(inside, 1.0 / cr, 0.0)
        lv["iB"][i] = jnp.where(inside, 1.0 / cb, 0.0)
        return carry

    lax.fori_loop(1, N0 - 1, inverses, 0, unroll=6)

    for k in range(2):
        sweep_packed(lv, True, 1 + 2 * k, N0 - 1 - 2 * k)
        sweep_packed(lv, False, 2 + 2 * k, N0 - 2 - 2 * k)

    def restrict(j, carry):
        a, b, _ = residual_packed(lv, H0 + 2 * j)
        c, d, _ = residual_packed(lv, H0 + 1 + 2 * j)
        i = H0 + 2 * j
        pair_r[j] = (a + b) + (c + d)
        pair_b[j] = (bE[i] + bO[i]) + (bE[i + 1] + bO[i + 1])
        return carry

    lax.fori_loop(0, 16, restrict, 0, unroll=4)

    halve = one_hot((256, 128), lambda i, j: (i >> 1) == j)
    f1 = 0.125 * matmul(pair_r[...].reshape(128, 256), halve)
    b1 = 0.125 * matmul(pair_b[...].reshape(128, 256), halve)
    own[0:16] = f1.reshape(16, 8, 128)
    own[16:32] = b1.reshape(16, 8, 128)

    for k in range(8):
        tmp[8 * k : 8 * k + 8, :] = own[16 + 2 * k] + own[17 + 2 * k]
    summed = tmp[pl.ds(0, 32, stride=2), :] + tmp[pl.ds(1, 32, stride=2), :]
    halve = one_hot((128, 128), lambda i, j: (i >> 1) == j)
    b2 = 0.125 * matmul(summed, halve)
    own[32:40] = jnp.zeros((8, 8, 128), F32)
    for k in range(8):
        own[32 + k, 0:4, :] = b2[4 * k : 4 * k + 4]
    bottom[...] = bottom_row([own[32 + 2 * k] + own[33 + 2 * k] for k in range(4)], slab)

    first = jnp.where(slab == 0, 1, 0)
    send[0:H1] = own[pl.ds(first * (16 - H1), H1)]
    send[H1 : 2 * H1 + 1] = own[pl.ds(16 + first * (15 - H1), H1 + 1)]
    send[2 * H1 + 1 :] = own[32:40]


def bottom_row(pairs, slab):
    total = None
    for k, plane in enumerate(pairs):
        spread = one_hot((128, 128), lambda i, j, k=k: jnp.logical_and((i >> 1) + 32 * k == j, i < 64))
        part = matmul(plane, spread)
        total = part if total is None else total + part
    low, high = total[0:1] + total[1:2], total[2:3] + total[3:4]
    row = 0.125 * jnp.where(slab == 0, low, high)
    return jnp.broadcast_to(row, (8, 128))


def level_faces(b, ax, ay, az, inv, n, factor, depth, width, inside):
    row, lane = iota((8, 128), 0), iota((8, 128), 1)
    top, bot = row == depth - 1, row == 0
    end, begin = lane == width - 1, lane == 0
    cell = jnp.logical_and(row < depth, lane < width)
    for i in range(n - 1):
        ax[i] = factor * (b[i] + b[i + 1])
    for i in range(1, n - 1):
        v = b[i]
        fy = factor * (v + jnp.where(end, 0.0, up(v, 1)))
        gy = factor * (v + jnp.where(begin, 0.0, down(v, 1)))
        fz = factor * (v + jnp.where(top, 0.0, up(v, 0)))
        gz = factor * (v + jnp.where(bot, 0.0, down(v, 0)))
        ay[i] = jnp.where(end, 0.0, fy)
        az[i] = jnp.where(top, 0.0, fz)
        center = (fz + gz) + (ax[i] + ax[i - 1]) + (fy + gy)
        inv[i] = jnp.where(jnp.logical_and(cell, inside(i)), 1.0 / center, 0.0)


def nsum_plain(v, ax, ay, az, i):
    here = v[i]
    t = ax[i] * v[i + 1] + ax[i - 1] * v[i - 1]
    t = t + (ay[i] * up(here, 1) + down(ay[i] * here, 1))
    return t + (az[i] * up(here, 0) + down(az[i] * here, 0))


def sweep_plain(v, f, ax, ay, az, inv, odd, shift, first, last):
    row, lane = iota((8, 128), 0), iota((8, 128), 1)
    even = ((row + lane) & 1) == 0
    masks = (even, jnp.logical_not(even))
    for i in range(first, last):
        cells = masks[(i + shift + odd) % 2]
        v[i] = jnp.where(cells, (f[i] + nsum_plain(v, ax, ay, az, i)) * inv[i], v[i])


def first_plain(v, f, inv, shift, first, last):
    row, lane = iota((8, 128), 0), iota((8, 128), 1)
    even = ((row + lane) & 1) == 0
    masks = (even, jnp.logical_not(even))
    for i in range(first, last):
        v[i] = jnp.where(masks[(i + shift) % 2], f[i] * inv[i], 0.0)


def residual_plain(v, f, ax, ay, az, inv, center, i):
    return f[i] - (center * v[i] - nsum_plain(v, ax, ay, az, i))


def center_plain(b, ax, i, factor, depth, width):
    row, lane = iota((8, 128), 0), iota((8, 128), 1)
    v = b[i]
    fy = jnp.where(lane == width - 1, 0.0, up(v, 1)) + jnp.where(lane == 0, 0.0, down(v, 1))
    fz = jnp.where(row == depth - 1, 0.0, up(v, 0)) + jnp.where(row == 0, 0.0, down(v, 0))
    return factor * (4.0 * v + fy + fz) + (ax[i] + ax[i - 1])


def middle_kernel(place, own, halo, bottom, v1, f1, ax1, ay1, az1, inv1, ax2, ay2, az2, inv2, send, message, b1, b2, v2, f2, tmp):
    slab, box, boxes = place[0], place[1], place[2]
    w = H1 + 1
    b1[0:w] = halo[0, H1 : H1 + w]
    b1[w : w + 16] = own[16:32]
    b1[w + 16 :] = halo[1, H1 : H1 + w]
    f1[0:1] = jnp.zeros((1, 8, 128), F32)
    f1[1 : 1 + H1] = halo[0, 0:H1]
    f1[w : w + 16] = own[0:16]
    f1[w + 16 : w + 16 + H1] = halo[1, 0:H1]
    f1[N1 - 1 :] = jnp.zeros((1, 8, 128), F32)
    b2[0:8] = halo[0, H1 + w :]
    b2[8:16] = own[32:40]
    b2[16:24] = halo[1, H1 + w :]
    v1[...] = jnp.zeros(v1.shape, F32)
    v2[...] = jnp.zeros(v2.shape, F32)
    f2[...] = jnp.zeros(f2.shape, F32)

    def within(size, width):
        def inside(i):
            x = box * size - width + i
            return jnp.logical_and(x >= 0, x < boxes * size)

        return inside

    k1, k2 = 0.5 * 0.25, 0.5 * 0.25**2
    level_faces(b1, ax1, ay1, az1, inv1, N1, k1, 8, 128, within(16, w))
    level_faces(b2, ax2, ay2, az2, inv2, N2, k2, 4, 64, within(8, 8))

    one = (f1, ax1, ay1, az1, inv1)
    first_plain(v1, f1, inv1, 1, 1, N1 - 1)
    sweep_plain(v1, *one, 1, 1, 2, N1 - 2)
    sweep_plain(v1, *one, 0, 1, 3, N1 - 3)
    sweep_plain(v1, *one, 1, 1, 4, N1 - 4)
    for j in range(16):
        parts = [
            residual_plain(v1, *one, center_plain(b1, ax1, i, k1, 8, 128), i)
            for i in (5 + 2 * j, 6 + 2 * j)
        ]
        tmp[8 * j : 8 * j + 8, :] = parts[0] + parts[1]
    summed = tmp[pl.ds(0, 64, stride=2), :] + tmp[pl.ds(1, 64, stride=2), :]
    coarse = 0.125 * matmul(summed, one_hot((128, 128), lambda i, j: (i >> 1) == j))
    for j in range(16):
        f2[4 + j, 0:4, :] = coarse[4 * j : 4 * j + 4]

    two = (f2, ax2, ay2, az2, inv2)
    first_plain(v2, f2, inv2, 0, 4, 20)
    sweep_plain(v2, *two, 1, 0, 5, 19)
    sweep_plain(v2, *two, 0, 0, 6, 18)
    sweep_plain(v2, *two, 1, 0, 7, 17)
    pairs = []
    for k in range(4):
        parts = [
            residual_plain(v2, *two, center_plain(b2, ax2, i, k2, 4, 64), i)
            for i in (8 + 2 * k, 9 + 2 * k)
        ]
        pairs.append(parts[0] + parts[1])
    source = bottom_row(pairs, slab)
    send[0:8] = v2[8:16]
    send[8:16] = f2[8:16]
    rows = jnp.where((iota((8, 128), 0) & 1) == 0, source, bottom[...])
    count = message.shape[0] // 8

    def spread(k, carry):
        message[pl.ds(pl.multiple_of(8 * k, 8), 8), :] = rows
        return carry

    lax.fori_loop(0, count, spread, 0, unroll=4)


def coarse_solve(n, source, coefficient, dref, qref, eref):
    row, lane = iota((n, 128), 0), iota((n, 128), 1)
    factor = 0.5 * 0.25**3
    last = jnp.logical_and(row == n - 1, lane >= 96)
    first = jnp.logical_and(row == 0, lane < 32)
    inner_hi, inner_lo = lane < 96, lane >= 32
    end, begin = (lane & 31) == 31, (lane & 31) == 0

    def xp(v):
        a = pltpu.roll(v, 96, 1)
        return jnp.where(inner_hi, a, up(a, 0))

    def xm(v):
        a = pltpu.roll(v, 32, 1)
        return jnp.where(inner_lo, a, down(a, 0))

    ax, ay, center = [], [], []
    az = factor * (coefficient[0] + coefficient[1])
    for b in coefficient:
        fx = factor * (b + jnp.where(last, 0.0, xp(b)))
        gx = factor * (b + jnp.where(first, 0.0, xm(b)))
        fy = factor * (b + jnp.where(end, 0.0, up(b, 1)))
        gy = factor * (b + jnp.where(begin, 0.0, down(b, 1)))
        ax.append(jnp.where(last, 0.0, fx))
        ay.append(jnp.where(end, 0.0, fy))
        center.append((factor * b + az) + (fx + gx) + (fy + gy))

    def total(u, w):
        s = u[0] * w[0] + u[1] * w[1]
        return jnp.sum(jnp.sum(s, axis=0, keepdims=True), axis=1, keepdims=True)

    for t in range(2):
        dref[t] = source[t]
        qref[t] = source[t]
        eref[t, 8 : 8 + n] = jnp.zeros((n, 128), F32)
        eref[t, 0:8] = jnp.zeros((8, 128), F32)
        eref[t, 8 + n :] = jnp.zeros((8, 128), F32)

    def iterate(k, now):
        d = (dref[0], dref[1])
        w = []
        for t in range(2):
            v = d[t]
            s = ax[t] * xp(v) + xm(ax[t] * v)
            s = s + (ay[t] * up(v, 1) + down(ay[t] * v, 1))
            w.append(center[t] * v - (s + az * d[1 - t]))
        alpha = now / total(d, w)
        q = []
        for t in range(2):
            eref[t, 8 : 8 + n] = eref[t, 8 : 8 + n] + alpha * d[t]
            q.append(qref[t] - alpha * w[t])
            qref[t] = q[t]
        later = total(q, q)
        beta = later / now
        for t in range(2):
            dref[t] = q[t] + beta * d[t]
        return later

    lax.fori_loop(0, ITERS, iterate, total(source, source))


def last_kernel(boxes, place, *refs):
    names = ("all", "own2", "v1", "f1", "ax1", "ay1", "az1", "inv1", "ax2", "ay2", "az2", "inv2")
    given = dict(zip(names, refs))
    refs = refs[len(names) :]
    level0 = dict(zip(PACKED, refs))
    refs = refs[len(PACKED) :]
    out_v, out_r, vR, vB, v1, v2, f2, dref, qref, eref, wide, e0 = refs
    slab, box = place[0], place[1]
    gathered = given["all"]

    source = [gathered[t, pl.ds(0, boxes, stride=2), :] for t in range(2)]
    coefficient = [gathered[t, pl.ds(1, boxes, stride=2), :] for t in range(2)]
    coarse_solve(boxes, source, coefficient, dref, qref, eref)

    base = 2 * boxes
    for side, at in ((0, 0), (1, 16)):
        for k in range(8):
            v2[at + k] = gathered[side, base + 8 * k : base + 8 * k + 8, :]
            f2[at + k] = gathered[side, base + 64 + 8 * k : base + 64 + 8 * k + 8, :]
    v2[8:16] = given["own2"][0:8]
    f2[8:16] = given["own2"][8:16]
    near = [eref[t, pl.ds(7 + box, 8), :] for t in range(2)]
    spread = one_hot((128, 512), lambda i, j: jnp.logical_and(((j >> 7) * 32) + ((j & 127) >> 1) == i, (j & 127) < 64))
    fine = [matmul(e, spread) for e in near]
    row = iota((8, 128), 0)
    for i in range(N2):
        cell, k = (i // 2) // 4, (i // 2) % 4
        low, high = (f[cell : cell + 1, 128 * k : 128 * k + 128] for f in fine)
        v2[i] = v2[i] + jnp.where(row < 2, low, jnp.where(row < 4, high, 0.0))
    two = (f2, given["ax2"], given["ay2"], given["az2"], given["inv2"])
    for k in range(2):
        sweep_plain(v2, *two, 0, 0, 1 + 2 * k, N2 - 1 - 2 * k)
        sweep_plain(v2, *two, 1, 0, 2 + 2 * k, N2 - 2 - 2 * k)

    packed = jnp.concatenate([v2[4 + j, 0:4, :] for j in range(16)], axis=0)
    fine = matmul(packed, one_hot((128, 128), lambda i, j: (j >> 1) == i))
    wide[pl.ds(0, 64, stride=2), :] = fine
    wide[pl.ds(1, 64, stride=2), :] = fine
    for i in range(6, N1 - 6):
        j = (i + 3) // 2 - 4
        v1[i] = given["v1"][i] + wide[8 * j : 8 * j + 8, :]
    one = (given["f1"], given["ax1"], given["ay1"], given["az1"], given["inv1"])
    for k in range(2):
        sweep_plain(v1, *one, 0, 1, 7 + 2 * k, N1 - 7 - 2 * k)
        sweep_plain(v1, *one, 1, 1, 8 + 2 * k, N1 - 8 - 2 * k)

    double = one_hot((128, 256), lambda i, j: (j >> 1) == i)
    e0[...] = matmul(v1[10:32].reshape(176, 128), double).reshape(22, 8, 256)
    lv = dict(level0, vR=vR, vB=vB)

    def correct(j, carry):
        e = e0[j]
        vB[3 + 2 * j] = level0["vB"][3 + 2 * j] + e
        vB[4 + 2 * j] = level0["vB"][4 + 2 * j] + e
        return carry

    lax.fori_loop(0, 22, correct, 0, unroll=2)
    for k in range(2):
        sweep_packed(lv, True, 5 + 2 * k, N0 - 5 - 2 * k)
        sweep_packed(lv, False, 6 + 2 * k, N0 - 6 - 2 * k)

    for x in range(32):
        i = H0 + x
        red, black, p = residual_packed(lv, i)
        for out, a, b in ((out_v, vR[i], vB[i]), (out_r, red, black)):
            even, odd = jnp.where(p, a, b), jnp.where(p, b, a)
            even = jnp.where(slab == 0, even[0:4], even[4:8])
            odd = jnp.where(slab == 0, odd[0:4], odd[4:8])
            for half in range(2):
                lanes = slice(128 * half, 128 * half + 128)
                out[slab_rows(x, half, 0), :] = even[:, lanes]
                out[slab_rows(x, half, 1), :] = odd[:, lanes]


def call(kernel, outs, scratch, *args, scalars=0):
    vmem = pl.BlockSpec(memory_space=pltpu.VMEM)
    smem = pl.BlockSpec(memory_space=pltpu.SMEM)
    shapes = [jax.ShapeDtypeStruct(s, F32) for s in outs]
    return pl.pallas_call(
        kernel,
        out_shape=shapes,
        in_specs=[smem] * scalars + [vmem] * (len(args) - scalars),
        out_specs=[vmem] * len(shapes),
        scratch_shapes=[pltpu.VMEM(s, F32) for s in scratch],
        compiler_params=pltpu.CompilerParams(vmem_limit_bytes=40 * 1024 * 1024),
    )(*args)


def by_tiles(a):
    return a.reshape(8, 4, 8, 2, 128).transpose(0, 1, 3, 2, 4).reshape(512, 128)


def from_tiles(a):
    return a.reshape(8, 4, 2, 8, 128).transpose(0, 1, 3, 2, 4).reshape(8, 32, 256)


def body(pressure_guess, right_side, coefficient):
    boxes = lax.axis_size("box")
    slab, box = lax.axis_index("slab"), lax.axis_index("box")
    place = jnp.stack([slab, box, jnp.int32(boxes), jnp.int32(0)]).astype(jnp.int32)
    rightward = [(i, i + 1) for i in range(boxes - 1)]
    leftward = [(i + 1, i) for i in range(boxes - 1)]
    both = [(2 * i, 2 * i + 2) for i in range(boxes - 1)] + [(2 * i + 3, 2 * i + 1) for i in range(boxes - 1)]

    flat = [by_tiles(a) for a in (pressure_guess, right_side, coefficient)]
    low, high = call(pack_kernel, [(16 * ROWS, 256)] * 2, [], *flat)
    from_left = lax.ppermute(high[16 * ROWS - EDGE :], "box", rightward)
    from_right = lax.ppermute(low[:EDGE], "box", leftward)
    low, high = lax.all_gather(low, "slab"), lax.all_gather(high, "slab")
    halo = lax.all_gather(jnp.stack([from_left, from_right]), "slab")

    plane = (N0, 8, 256)
    fine = call(
        fine_kernel,
        [plane] * len(PACKED) + [(40, 8, 128), (SEND1, 8, 128), (8, 128)],
        [plane] * 3 + [(16, 8, 256)] * 2 + [(64, 128)],
        place,
        low,
        high,
        halo,
        scalars=1,
    )
    level0 = fine[: len(PACKED)]
    own, send, bottom = fine[len(PACKED) :]
    halo = lax.all_gather(lax.ppermute(send, ("box", "slab"), both), "slab")

    one, two = (N1, 8, 128), (N2, 8, 128)
    *levels, send, message = call(
        middle_kernel,
        [one] * 6 + [two] * 4 + [(16, 8, 128), (2 * boxes, 128)],
        [one, two, two, two, (128, 128)],
        place,
        own,
        halo,
        bottom,
        scalars=1,
    )
    beside = lax.ppermute(send, ("box", "slab"), both)
    spread = lax.all_to_all(message.reshape(boxes, 2, 128), "box", 0, 0)
    both_parts = jnp.concatenate([spread.reshape(2 * boxes, 128), beside.reshape(128, 128)], axis=0)
    gathered = lax.all_gather(both_parts, "slab")

    flat_out = [(512, 128)] * 2
    pressure, residual = call(
        functools.partial(last_kernel, boxes),
        flat_out,
        [plane, plane, one, two, two, (2, boxes, 128), (2, boxes, 128), (2, boxes + 16, 128), (128, 128), (22, 8, 256)],
        place,
        gathered,
        send,
        *levels,
        *level0,
        scalars=1,
    )
    return from_tiles(pressure), from_tiles(residual)


def solution(mesh):
    split = P("slab", "box", None)
    return jax.shard_map(body, mesh=mesh, in_specs=(split,) * 3, out_specs=(split,) * 2, check_vma=False)
```

```python
import functools

import jax
import jax.numpy as jnp
from jax import lax
from jax.experimental import pallas as pl
from jax.experimental.pallas import tpu as pltpu
from jax.sharding import PartitionSpec as P

ITERS = 8
F32 = jnp.float32
BF16 = jnp.bfloat16

H0 = 9
H1 = 12
N0 = 32 + 2 * H0
N1 = 16 + 2 * (H1 + 1)
N2 = 24
ROWS = 20
EDGE = 184
SEND1 = H1 + (H1 + 1) + 8


def matmul(x, m):
    high = x.astype(BF16)
    rest = x - high.astype(F32)
    mid = rest.astype(BF16)
    low = (rest - mid.astype(F32)).astype(BF16)
    dot = functools.partial(jnp.dot, preferred_element_type=F32)
    return dot(high, m) + (dot(mid, m) + dot(low, m))


def one_hot(shape, rule):
    i = lax.broadcasted_iota(jnp.int32, shape, 0)
    j = lax.broadcasted_iota(jnp.int32, shape, 1)
    return rule(i, j).astype(F32).astype(BF16)


def iota(shape, axis):
    return lax.broadcasted_iota(jnp.int32, shape, axis)


def up(v, axis):
    return pltpu.roll(v, v.shape[axis] - 1, axis)


def down(v, axis):
    return pltpu.roll(v, 1, axis)


def slab_rows(x, half, odd):
    return pl.ds((x // 8) * 16 + half * 8 + x % 8 + 64 * odd, 4, stride=128)


def pack_kernel(g_hbm, r_hbm, c_hbm, low, high, g, r, c, sem):
    copies = [pltpu.make_async_copy(a, b, sem.at[k]) for k, (a, b) in enumerate(((g_hbm, g), (r_hbm, r), (c_hbm, c)))]
    for copy in copies:
        copy.start()
    for copy in copies:
        copy.wait()
    even_y = (iota((4, 128), 1) & 1) == 0
    odd_y = jnp.logical_not(even_y)
    for x in range(32):
        out, base = (low, x * ROWS) if x < 16 else (high, (x - 16) * ROWS)
        p0 = even_y if x % 2 == 0 else odd_y
        for half in range(2):
            lanes = slice(128 * half, 128 * half + 128)
            even, odd = slab_rows(x, half, 0), slab_rows(x, half, 1)
            out[base : base + 4, lanes] = c[even, :]
            out[base + 4 : base + 8, lanes] = c[odd, :]
            fe, fo = r[even, :], r[odd, :]
            out[base + 8 : base + 12, lanes] = jnp.where(p0, fe, fo)
            out[base + 12 : base + 16, lanes] = jnp.where(p0, fo, fe)
            out[base + 16 : base + 20, lanes] = jnp.where(p0, g[odd, :], g[even, :])


def parity(i, shape, shift):
    return ((iota(shape, 1) + i + shift) & 1) == 0


def nsum_packed(lv, v, xa, xb, ya, yb, i, p):
    here = v[i]
    t = xa[i] * v[i + 1] + xb[i - 1] * v[i - 1]
    t = t + (ya[i] * up(here, 1) + down(yb[i] * here, 1))
    cross = lv["c"][i]
    z = jnp.where(p, down(cross * here, 0), cross * up(here, 0))
    return t + (lv["s"][i] * here + z)


def sweep_packed(lv, red, first, last):
    def body(i, carry):
        p = parity(i, (8, 256), 1)
        if red:
            n = nsum_packed(lv, lv["vB"], lv["xR"], lv["xB"], lv["yR"], lv["yB"], i, p)
            lv["vR"][i] = (lv["fR"][i] + n) * lv["iR"][i]
        else:
            p = jnp.logical_not(p)
            n = nsum_packed(lv, lv["vR"], lv["xB"], lv["xR"], lv["yB"], lv["yR"], i, p)
            lv["vB"][i] = (lv["fB"][i] + n) * lv["iB"][i]
        return carry

    lax.fori_loop(first, last, body, 0, unroll=6)


def residual_packed(lv, i):
    p = parity(i, (8, 256), 1)
    n = nsum_packed(lv, lv["vB"], lv["xR"], lv["xB"], lv["yR"], lv["yB"], i, p)
    r_red = lv["fR"][i] - (lv["cR"][i] * lv["vR"][i] - n)
    q = jnp.logical_not(p)
    n = nsum_packed(lv, lv["vR"], lv["xB"], lv["xR"], lv["yB"], lv["yR"], i, q)
    r_black = lv["fB"][i] - (lv["cB"][i] * lv["vB"][i] - n)
    return r_red, r_black, p


PACKED = ("vB", "fR", "fB", "xR", "xB", "yR", "yB", "s", "c", "iR", "iB", "cR", "cB")


def fine_kernel(place, lo, hi, halo, *refs):
    outs = dict(zip(PACKED, refs))
    own, send, bottom = refs[len(PACKED) : len(PACKED) + 3]
    vR, bE, bO, pair_r, pair_b, tmp = refs[len(PACKED) + 3 :]
    lv = dict(outs, vR=vR)
    slab, box, boxes = place[0], place[1], place[2]

    def source(t, i):
        if i < H0:
            return halo.at[t, 0], i * ROWS + (EDGE - H0 * ROWS)
        if i >= H0 + 32:
            return halo.at[t, 1], (i - H0 - 32) * ROWS
        x = i - H0
        return (lo.at[t], x * ROWS) if x < 16 else (hi.at[t], (x - 16) * ROWS)

    for i in range(N0):
        for t in range(2):
            ref, base = source(t, i)
            for k, out in enumerate((bE, bO, lv["fR"], lv["fB"], lv["vB"])):
                out[i, 4 * t : 4 * t + 4, :] = ref[base + 4 * k : base + 4 * k + 4, :]

    row, lane = iota((8, 256), 0), iota((8, 256), 1)
    top, bot = row == 7, row == 0
    end, begin = lane == 255, lane == 0

    def faces(i, carry):
        p = parity(i, (8, 256), 1)
        e, o = bE[i], bO[i]
        fxe, fxo = 0.5 * (e + bE[i + 1]), 0.5 * (o + bO[i + 1])
        lv["xR"][i] = jnp.where(p, fxe, fxo)
        lv["xB"][i] = jnp.where(p, fxo, fxe)
        fye = 0.5 * (e + jnp.where(end, 0.0, up(e, 1)))
        fyo = 0.5 * (o + jnp.where(end, 0.0, up(o, 1)))
        gye = 0.5 * (e + jnp.where(begin, 0.0, down(e, 1)))
        gyo = 0.5 * (o + jnp.where(begin, 0.0, down(o, 1)))
        yr, yb = jnp.where(p, fye, fyo), jnp.where(p, fyo, fye)
        lv["yR"][i] = jnp.where(end, 0.0, yr)
        lv["yB"][i] = jnp.where(end, 0.0, yb)
        s = 0.5 * (e + o)
        above = 0.5 * (o + jnp.where(top, 0.0, up(e, 0)))
        below = 0.5 * (e + jnp.where(bot, 0.0, down(o, 0)))
        lv["s"][i] = s
        lv["c"][i] = jnp.where(top, 0.0, above)
        ze, zo = fye + gye + (s + below), fyo + gyo + (s + above)
        lv["cR"][i] = jnp.where(p, ze, zo)
        lv["cB"][i] = jnp.where(p, zo, ze)
        return carry

    lax.fori_loop(0, N0 - 1, faces, 0, unroll=7)

    def inverses(i, carry):
        x = box * 32 - H0 + i
        inside = jnp.logical_and(x >= 0, x < boxes * 32)
        cr = lv["cR"][i] + (lv["xR"][i] + lv["xB"][i - 1])
        cb = lv["cB"][i] + (lv["xB"][i] + lv["xR"][i - 1])
        lv["cR"][i] = cr
        lv["cB"][i] = cb
        lv["iR"][i] = jnp.where(inside, 1.0 / cr, 0.0)
        lv["iB"][i] = jnp.where(inside, 1.0 / cb, 0.0)
        return carry

    lax.fori_loop(1, N0 - 1, inverses, 0, unroll=6)

    for k in range(2):
        sweep_packed(lv, True, 1 + 2 * k, N0 - 1 - 2 * k)
        sweep_packed(lv, False, 2 + 2 * k, N0 - 2 - 2 * k)

    def restrict(j, carry):
        a, b, _ = residual_packed(lv, H0 + 2 * j)
        c, d, _ = residual_packed(lv, H0 + 1 + 2 * j)
        i = H0 + 2 * j
        pair_r[j] = (a + b) + (c + d)
        pair_b[j] = (bE[i] + bO[i]) + (bE[i + 1] + bO[i + 1])
        return carry

    lax.fori_loop(0, 16, restrict, 0, unroll=4)

    halve = one_hot((256, 128), lambda i, j: (i >> 1) == j)
    f1 = 0.125 * matmul(pair_r[...].reshape(128, 256), halve)
    b1 = 0.125 * matmul(pair_b[...].reshape(128, 256), halve)
    own[0:16] = f1.reshape(16, 8, 128)
    own[16:32] = b1.reshape(16, 8, 128)

    for k in range(8):
        tmp[8 * k : 8 * k + 8, :] = own[16 + 2 * k] + own[17 + 2 * k]
    summed = tmp[pl.ds(0, 32, stride=2), :] + tmp[pl.ds(1, 32, stride=2), :]
    halve = one_hot((128, 128), lambda i, j: (i >> 1) == j)
    b2 = 0.125 * matmul(summed, halve)
    own[32:40] = jnp.zeros((8, 8, 128), F32)
    for k in range(8):
        own[32 + k, 0:4, :] = b2[4 * k : 4 * k + 4]
    bottom[...] = bottom_row([own[32 + 2 * k] + own[33 + 2 * k] for k in range(4)], slab)

    first = jnp.where(slab == 0, 1, 0)
    send[0:H1] = own[pl.ds(first * (16 - H1), H1)]
    send[H1 : 2 * H1 + 1] = own[pl.ds(16 + first * (15 - H1), H1 + 1)]
    send[2 * H1 + 1 :] = own[32:40]


def bottom_row(pairs, slab):
    total = None
    for k, plane in enumerate(pairs):
        spread = one_hot((128, 128), lambda i, j, k=k: jnp.logical_and((i >> 1) + 32 * k == j, i < 64))
        part = matmul(plane, spread)
        total = part if total is None else total + part
    low, high = total[0:1] + total[1:2], total[2:3] + total[3:4]
    row = 0.125 * jnp.where(slab == 0, low, high)
    return jnp.broadcast_to(row, (8, 128))


def level_faces(b, ax, ay, az, inv, n, factor, depth, width, inside):
    row, lane = iota((8, 128), 0), iota((8, 128), 1)
    top, bot = row == depth - 1, row == 0
    end, begin = lane == width - 1, lane == 0
    cell = jnp.logical_and(row < depth, lane < width)
    for i in range(n - 1):
        ax[i] = factor * (b[i] + b[i + 1])
    for i in range(1, n - 1):
        v = b[i]
        fy = factor * (v + jnp.where(end, 0.0, up(v, 1)))
        gy = factor * (v + jnp.where(begin, 0.0, down(v, 1)))
        fz = factor * (v + jnp.where(top, 0.0, up(v, 0)))
        gz = factor * (v + jnp.where(bot, 0.0, down(v, 0)))
        ay[i] = jnp.where(end, 0.0, fy)
        az[i] = jnp.where(top, 0.0, fz)
        center = (fz + gz) + (ax[i] + ax[i - 1]) + (fy + gy)
        inv[i] = jnp.where(jnp.logical_and(cell, inside(i)), 1.0 / center, 0.0)


def nsum_plain(v, ax, ay, az, i):
    here = v[i]
    t = ax[i] * v[i + 1] + ax[i - 1] * v[i - 1]
    t = t + (ay[i] * up(here, 1) + down(ay[i] * here, 1))
    return t + (az[i] * up(here, 0) + down(az[i] * here, 0))


def sweep_plain(v, f, ax, ay, az, inv, odd, shift, first, last):
    row, lane = iota((8, 128), 0), iota((8, 128), 1)
    even = ((row + lane) & 1) == 0
    masks = (even, jnp.logical_not(even))
    for i in range(first, last):
        cells = masks[(i + shift + odd) % 2]
        v[i] = jnp.where(cells, (f[i] + nsum_plain(v, ax, ay, az, i)) * inv[i], v[i])


def first_plain(v, f, inv, shift, first, last):
    row, lane = iota((8, 128), 0), iota((8, 128), 1)
    even = ((row + lane) & 1) == 0
    masks = (even, jnp.logical_not(even))
    for i in range(first, last):
        v[i] = jnp.where(masks[(i + shift) % 2], f[i] * inv[i], 0.0)


def residual_plain(v, f, ax, ay, az, center, i):
    return f[i] - (center * v[i] - nsum_plain(v, ax, ay, az, i))


def center_plain(b, ax, i, factor, depth, width):
    row, lane = iota((8, 128), 0), iota((8, 128), 1)
    v = b[i]
    fy = jnp.where(lane == width - 1, 0.0, up(v, 1)) + jnp.where(lane == 0, 0.0, down(v, 1))
    fz = jnp.where(row == depth - 1, 0.0, up(v, 0)) + jnp.where(row == 0, 0.0, down(v, 0))
    return factor * (4.0 * v + fy + fz) + (ax[i] + ax[i - 1])


def middle_kernel(place, own, halo, v1, f1, ax1, ay1, az1, inv1, ax2, ay2, az2, inv2, send, v2, f2, b2, b1, tmp):
    box, boxes = place[1], place[2]
    w = H1 + 1
    b1[0:w] = halo[0, H1 : H1 + w]
    b1[w : w + 16] = own[16:32]
    b1[w + 16 :] = halo[1, H1 : H1 + w]
    f1[0:1] = jnp.zeros((1, 8, 128), F32)
    f1[1 : 1 + H1] = halo[0, 0:H1]
    f1[w : w + 16] = own[0:16]
    f1[w + 16 : w + 16 + H1] = halo[1, 0:H1]
    f1[N1 - 1 :] = jnp.zeros((1, 8, 128), F32)
    b2[0:8] = halo[0, H1 + w :]
    b2[8:16] = own[32:40]
    b2[16:24] = halo[1, H1 + w :]
    v1[...] = jnp.zeros(v1.shape, F32)
    v2[...] = jnp.zeros(v2.shape, F32)
    f2[...] = jnp.zeros(f2.shape, F32)

    def within(size, width):
        def inside(i):
            x = box * size - width + i
            return jnp.logical_and(x >= 0, x < boxes * size)

        return inside

    k1, k2 = 0.5 * 0.25, 0.5 * 0.25**2
    level_faces(b1, ax1, ay1, az1, inv1, N1, k1, 8, 128, within(16, w))
    level_faces(b2, ax2, ay2, az2, inv2, N2, k2, 4, 64, within(8, 8))

    one = (f1, ax1, ay1, az1, inv1)
    first_plain(v1, f1, inv1, 1, 1, N1 - 1)
    sweep_plain(v1, *one, 1, 1, 2, N1 - 2)
    sweep_plain(v1, *one, 0, 1, 3, N1 - 3)
    sweep_plain(v1, *one, 1, 1, 4, N1 - 4)
    for j in range(16):
        parts = [
            residual_plain(v1, *one[:4], center_plain(b1, ax1, i, k1, 8, 128), i)
            for i in (5 + 2 * j, 6 + 2 * j)
        ]
        tmp[8 * j : 8 * j + 8, :] = parts[0] + parts[1]
    summed = tmp[pl.ds(0, 64, stride=2), :] + tmp[pl.ds(1, 64, stride=2), :]
    coarse = 0.125 * matmul(summed, one_hot((128, 128), lambda i, j: (i >> 1) == j))
    for j in range(16):
        f2[4 + j, 0:4, :] = coarse[4 * j : 4 * j + 4]

    two = (f2, ax2, ay2, az2, inv2)
    first_plain(v2, f2, inv2, 0, 4, 20)
    sweep_plain(v2, *two, 1, 0, 5, 19)
    sweep_plain(v2, *two, 0, 0, 6, 18)
    sweep_plain(v2, *two, 1, 0, 7, 17)
    send[0:8] = v2[8:16]
    send[8:16] = f2[8:16]


def source_kernel(place, v2, f2, b2, ax2, ay2, az2, bottom, rows):
    two, k2 = (f2, ax2, ay2, az2), 0.5 * 0.25**2
    pairs = []
    for k in range(4):
        parts = [
            residual_plain(v2, *two, center_plain(b2, ax2, i, k2, 4, 64), i)
            for i in (8 + 2 * k, 9 + 2 * k)
        ]
        pairs.append(parts[0] + parts[1])
    source = bottom_row(pairs, place[0])
    rows[...] = jnp.where((iota((8, 128), 0) & 1) == 0, source, bottom[...])


def spread_kernel(rows, beside, message):
    del beside
    value = rows[...]
    for k in range(message.shape[0] // 8):
        message[8 * k : 8 * k + 8, :] = value


def coarse_solve(n, source, coefficient, dref, qref, eref):
    row, lane = iota((n, 128), 0), iota((n, 128), 1)
    factor = 0.5 * 0.25**3
    last = jnp.logical_and(row == n - 1, lane >= 96)
    first = jnp.logical_and(row == 0, lane < 32)
    inner_hi, inner_lo = lane < 96, lane >= 32
    end, begin = (lane & 31) == 31, (lane & 31) == 0

    def xp(v):
        a = pltpu.roll(v, 96, 1)
        return jnp.where(inner_hi, a, up(a, 0))

    def xm(v):
        a = pltpu.roll(v, 32, 1)
        return jnp.where(inner_lo, a, down(a, 0))

    ax, ay, center = [], [], []
    az = factor * (coefficient[0] + coefficient[1])
    for b in coefficient:
        fx = factor * (b + jnp.where(last, 0.0, xp(b)))
        gx = factor * (b + jnp.where(first, 0.0, xm(b)))
        fy = factor * (b + jnp.where(end, 0.0, up(b, 1)))
        gy = factor * (b + jnp.where(begin, 0.0, down(b, 1)))
        ax.append(jnp.where(last, 0.0, fx))
        ay.append(jnp.where(end, 0.0, fy))
        center.append((factor * b + az) + (fx + gx) + (fy + gy))

    def total(u, w):
        s = u[0] * w[0] + u[1] * w[1]
        return jnp.sum(jnp.sum(s, axis=0, keepdims=True), axis=1, keepdims=True)

    for t in range(2):
        dref[t] = source[t]
        qref[t] = source[t]
        eref[t, 8 : 8 + n] = jnp.zeros((n, 128), F32)
        eref[t, 0:8] = jnp.zeros((8, 128), F32)
        eref[t, 8 + n :] = jnp.zeros((8, 128), F32)

    def iterate(k, now):
        d = (dref[0], dref[1])
        w = []
        for t in range(2):
            v = d[t]
            s = ax[t] * xp(v) + xm(ax[t] * v)
            s = s + (ay[t] * up(v, 1) + down(ay[t] * v, 1))
            w.append(center[t] * v - (s + az * d[1 - t]))
        alpha = now / total(d, w)
        q = []
        for t in range(2):
            eref[t, 8 : 8 + n] = eref[t, 8 : 8 + n] + alpha * d[t]
            q.append(qref[t] - alpha * w[t])
            qref[t] = q[t]
        later = total(q, q)
        beta = later / now
        for t in range(2):
            dref[t] = q[t] + beta * d[t]
        return later

    lax.fori_loop(0, ITERS, iterate, total(source, source))


def last_kernel(boxes, place, *refs):
    names = ("all", "own2", "v1", "f1", "ax1", "ay1", "az1", "inv1", "ax2", "ay2", "az2", "inv2")
    given = dict(zip(names, refs))
    refs = refs[len(names) :]
    level0 = dict(zip(PACKED, refs))
    refs = refs[len(PACKED) :]
    out_v, out_r, vR, vB, v1, v2, f2, dref, qref, eref, wide, e0 = refs
    slab, box = place[0], place[1]
    gathered = given["all"]

    source = [gathered[t, pl.ds(0, boxes, stride=2), :] for t in range(2)]
    coefficient = [gathered[t, pl.ds(1, boxes, stride=2), :] for t in range(2)]
    coarse_solve(boxes, source, coefficient, dref, qref, eref)

    base = 2 * boxes
    for side, at in ((0, 0), (1, 16)):
        for k in range(8):
            v2[at + k] = gathered[side, base + 8 * k : base + 8 * k + 8, :]
            f2[at + k] = gathered[side, base + 64 + 8 * k : base + 64 + 8 * k + 8, :]
    v2[8:16] = given["own2"][0:8]
    f2[8:16] = given["own2"][8:16]
    near = [eref[t, pl.ds(7 + box, 8), :] for t in range(2)]
    spread = one_hot((128, 512), lambda i, j: jnp.logical_and(((j >> 7) * 32) + ((j & 127) >> 1) == i, (j & 127) < 64))
    fine = [matmul(e, spread) for e in near]
    row = iota((8, 128), 0)
    for i in range(N2):
        cell, k = (i // 2) // 4, (i // 2) % 4
        low, high = (f[cell : cell + 1, 128 * k : 128 * k + 128] for f in fine)
        v2[i] = v2[i] + jnp.where(row < 2, low, jnp.where(row < 4, high, 0.0))
    two = (f2, given["ax2"], given["ay2"], given["az2"], given["inv2"])
    for k in range(2):
        sweep_plain(v2, *two, 0, 0, 1 + 2 * k, N2 - 1 - 2 * k)
        sweep_plain(v2, *two, 1, 0, 2 + 2 * k, N2 - 2 - 2 * k)

    packed = jnp.concatenate([v2[4 + j, 0:4, :] for j in range(16)], axis=0)
    fine = matmul(packed, one_hot((128, 128), lambda i, j: (j >> 1) == i))
    wide[pl.ds(0, 64, stride=2), :] = fine
    wide[pl.ds(1, 64, stride=2), :] = fine
    for i in range(6, N1 - 6):
        j = (i + 3) // 2 - 4
        v1[i] = given["v1"][i] + wide[8 * j : 8 * j + 8, :]
    one = (given["f1"], given["ax1"], given["ay1"], given["az1"], given["inv1"])
    for k in range(2):
        sweep_plain(v1, *one, 0, 1, 7 + 2 * k, N1 - 7 - 2 * k)
        sweep_plain(v1, *one, 1, 1, 8 + 2 * k, N1 - 8 - 2 * k)

    double = one_hot((128, 256), lambda i, j: (j >> 1) == i)
    e0[...] = matmul(v1[10:32].reshape(176, 128), double).reshape(22, 8, 256)
    lv = dict(level0, vR=vR, vB=vB)

    def correct(j, carry):
        e = e0[j]
        vB[3 + 2 * j] = level0["vB"][3 + 2 * j] + e
        vB[4 + 2 * j] = level0["vB"][4 + 2 * j] + e
        return carry

    lax.fori_loop(0, 22, correct, 0, unroll=2)
    for k in range(2):
        sweep_packed(lv, True, 5 + 2 * k, N0 - 5 - 2 * k)
        sweep_packed(lv, False, 6 + 2 * k, N0 - 6 - 2 * k)

    for x in range(32):
        i = H0 + x
        red, black, p = residual_packed(lv, i)
        for out, a, b in ((out_v, vR[i], vB[i]), (out_r, red, black)):
            even, odd = jnp.where(p, a, b), jnp.where(p, b, a)
            even = jnp.where(slab == 0, even[0:4], even[4:8])
            odd = jnp.where(slab == 0, odd[0:4], odd[4:8])
            for half in range(2):
                lanes = slice(128 * half, 128 * half + 128)
                out[slab_rows(x, half, 0), :] = even[:, lanes]
                out[slab_rows(x, half, 1), :] = odd[:, lanes]


def call(kernel, outs, scratch, *args, scalars=0, limit=12):
    vmem = pl.BlockSpec(memory_space=pltpu.VMEM)
    smem = pl.BlockSpec(memory_space=pltpu.SMEM)
    return pl.pallas_call(
        kernel,
        out_shape=[jax.ShapeDtypeStruct(s, F32) for s in outs],
        in_specs=[smem] * scalars + [vmem] * (len(args) - scalars),
        out_specs=[vmem] * len(outs),
        scratch_shapes=[pltpu.VMEM(s, F32) for s in scratch],
        compiler_params=pltpu.CompilerParams(vmem_limit_bytes=limit * 1024 * 1024),
    )(*args)


def pack(*args):
    return pl.pallas_call(
        pack_kernel,
        out_shape=[jax.ShapeDtypeStruct((16 * ROWS, 256), F32)] * 2,
        in_specs=[pl.BlockSpec(memory_space=pltpu.HBM)] * 3,
        out_specs=[pl.BlockSpec(memory_space=pltpu.VMEM)] * 2,
        scratch_shapes=[pltpu.VMEM((512, 128), F32)] * 3 + [pltpu.SemaphoreType.DMA((3,))],
        compiler_params=pltpu.CompilerParams(vmem_limit_bytes=4 * 1024 * 1024),
    )(*args)


def by_tiles(a):
    return a.reshape(8, 4, 8, 2, 128).transpose(0, 1, 3, 2, 4).reshape(512, 128)


def from_tiles(a):
    return a.reshape(8, 4, 2, 8, 128).transpose(0, 1, 3, 2, 4).reshape(8, 32, 256)


def body(pressure_guess, right_side, coefficient):
    boxes = lax.axis_size("box")
    slab, box = lax.axis_index("slab"), lax.axis_index("box")
    place = jnp.stack([slab, box, jnp.int32(boxes), jnp.int32(0)]).astype(jnp.int32)
    rightward = [(i, i + 1) for i in range(boxes - 1)]
    leftward = [(i + 1, i) for i in range(boxes - 1)]
    both = [(2 * i, 2 * i + 2) for i in range(boxes - 1)] + [(2 * i + 3, 2 * i + 1) for i in range(boxes - 1)]

    flat = [by_tiles(a) for a in (pressure_guess, right_side, coefficient)]
    low, high = pack(*flat)
    from_left = lax.ppermute(high[16 * ROWS - EDGE :], "box", rightward)
    from_right = lax.ppermute(low[:EDGE], "box", leftward)
    low, high = lax.all_gather(low, "slab"), lax.all_gather(high, "slab")
    halo = lax.all_gather(jnp.stack([from_left, from_right]), "slab")

    plane = (N0, 8, 256)
    fine = call(
        fine_kernel,
        [plane] * len(PACKED) + [(40, 8, 128), (SEND1, 8, 128), (8, 128)],
        [plane] * 3 + [(16, 8, 256)] * 2 + [(64, 128)],
        place,
        low,
        high,
        halo,
        scalars=1,
    )
    level0 = fine[: len(PACKED)]
    own, send, bottom = fine[len(PACKED) :]
    halo = lax.all_gather(lax.ppermute(send, ("box", "slab"), both), "slab")

    one, two = (N1, 8, 128), (N2, 8, 128)
    *levels, send, v2, f2, b2 = call(
        middle_kernel,
        [one] * 6 + [two] * 4 + [(16, 8, 128)] + [two] * 3,
        [one, (128, 128)],
        place,
        own,
        halo,
        scalars=1,
    )
    beside = lax.ppermute(send, ("box", "slab"), both)
    (rows,) = call(source_kernel, [(8, 128)], [], place, v2, f2, b2, *levels[6:9], bottom, scalars=1)
    (message,) = call(spread_kernel, [(2 * boxes, 128)], [], rows, beside)
    spread = lax.all_to_all(message.reshape(boxes, 2, 128), "box", 0, 0)
    both_parts = jnp.concatenate([spread.reshape(2 * boxes, 128), beside.reshape(128, 128)], axis=0)
    gathered = lax.all_gather(both_parts, "slab")

    flat_out = [(512, 128)] * 2
    pressure, residual = call(
        functools.partial(last_kernel, boxes),
        flat_out,
        [plane, plane, one, two, two, (2, boxes, 128), (2, boxes, 128), (2, boxes + 16, 128), (128, 128), (22, 8, 256)],
        place,
        gathered,
        send,
        *levels,
        *level0,
        scalars=1,
    )
    return from_tiles(pressure), from_tiles(residual)


def solution(mesh):
    split = P("slab", "box", None)
    return jax.shard_map(body, mesh=mesh, in_specs=(split,) * 3, out_specs=(split,) * 2, check_vma=False)
```

```python
import functools

import jax
import jax.numpy as jnp
from jax import lax
from jax.experimental import pallas as pl
from jax.experimental.pallas import tpu as pltpu
from jax.sharding import PartitionSpec as P

ITERS = 8
F32 = jnp.float32
BF16 = jnp.bfloat16

H0 = 9
H1 = 12
N0 = 32 + 2 * H0
N1 = 16 + 2 * (H1 + 1)
N2 = 24
ROWS = 20
EDGE = 184
SEND1 = H1 + (H1 + 1) + 8


def matmul(x, m):
    high = x.astype(BF16)
    rest = x - high.astype(F32)
    mid = rest.astype(BF16)
    low = (rest - mid.astype(F32)).astype(BF16)
    dot = functools.partial(jnp.dot, preferred_element_type=F32)
    return dot(high, m) + (dot(mid, m) + dot(low, m))


def one_hot(shape, rule):
    i = lax.broadcasted_iota(jnp.int32, shape, 0)
    j = lax.broadcasted_iota(jnp.int32, shape, 1)
    return rule(i, j).astype(F32).astype(BF16)


def iota(shape, axis):
    return lax.broadcasted_iota(jnp.int32, shape, axis)


def up(v, axis):
    return pltpu.roll(v, v.shape[axis] - 1, axis)


def down(v, axis):
    return pltpu.roll(v, 1, axis)


def slab_rows(x, half, odd):
    return pl.ds((x // 8) * 16 + half * 8 + x % 8 + 64 * odd, 4, stride=128)


def pack_kernel(place, g_hbm, r_hbm, c_hbm, low, high, first, second, g, r, c, sem):
    copies = [pltpu.make_async_copy(a, b, sem.at[k]) for k, (a, b) in enumerate(((g_hbm, g), (r_hbm, r), (c_hbm, c)))]
    for copy in copies:
        copy.start()
    for copy in copies:
        copy.wait()
    even_y = (iota((4, 128), 1) & 1) == 0
    odd_y = jnp.logical_not(even_y)
    for x in range(32):
        out, base = (low, x * ROWS) if x < 16 else (high, (x - 16) * ROWS)
        p0 = even_y if x % 2 == 0 else odd_y
        for half in range(2):
            lanes = slice(128 * half, 128 * half + 128)
            even, odd = slab_rows(x, half, 0), slab_rows(x, half, 1)
            out[base : base + 4, lanes] = c[even, :]
            out[base + 4 : base + 8, lanes] = c[odd, :]
            fe, fo = r[even, :], r[odd, :]
            out[base + 8 : base + 12, lanes] = jnp.where(p0, fe, fo)
            out[base + 12 : base + 16, lanes] = jnp.where(p0, fo, fe)
            out[base + 16 : base + 20, lanes] = jnp.where(p0, g[odd, :], g[even, :])

    right_first = (place[1] & 1) == 1

    @pl.when(right_first)
    def _():
        first[...] = high[16 * ROWS - EDGE :, :]
        second[...] = low[:EDGE, :]

    @pl.when(jnp.logical_not(right_first))
    def _():
        first[...] = low[:EDGE, :]
        second[...] = high[16 * ROWS - EDGE :, :]


def parity(i, shape, shift):
    return ((iota(shape, 1) + i + shift) & 1) == 0


def nsum_packed(lv, v, xa, xb, ya, yb, i, p):
    here = v[i]
    t = xa[i] * v[i + 1] + xb[i - 1] * v[i - 1]
    t = t + (ya[i] * up(here, 1) + down(yb[i] * here, 1))
    cross = lv["c"][i]
    z = jnp.where(p, down(cross * here, 0), cross * up(here, 0))
    return t + (lv["s"][i] * here + z)


def sweep_packed(lv, red, first, last):
    def body(i, carry):
        p = parity(i, (8, 256), 1)
        if red:
            n = nsum_packed(lv, lv["vB"], lv["xR"], lv["xB"], lv["yR"], lv["yB"], i, p)
            lv["vR"][i] = (lv["fR"][i] + n) * lv["iR"][i]
        else:
            p = jnp.logical_not(p)
            n = nsum_packed(lv, lv["vR"], lv["xB"], lv["xR"], lv["yB"], lv["yR"], i, p)
            lv["vB"][i] = (lv["fB"][i] + n) * lv["iB"][i]
        return carry

    lax.fori_loop(first, last, body, 0, unroll=6)


def residual_packed(lv, i):
    p = parity(i, (8, 256), 1)
    n = nsum_packed(lv, lv["vB"], lv["xR"], lv["xB"], lv["yR"], lv["yB"], i, p)
    r_red = lv["fR"][i] - (lv["cR"][i] * lv["vR"][i] - n)
    q = jnp.logical_not(p)
    n = nsum_packed(lv, lv["vR"], lv["xB"], lv["xR"], lv["yB"], lv["yR"], i, q)
    r_black = lv["fB"][i] - (lv["cB"][i] * lv["vB"][i] - n)
    return r_red, r_black, p


PACKED = ("vB", "fR", "fB", "xR", "xB", "yR", "yB", "s", "c", "iR", "iB", "cR", "cB")


def fine_kernel(place, lo, hi, halo, *refs):
    outs = dict(zip(PACKED, refs))
    own, send, bottom = refs[len(PACKED) : len(PACKED) + 3]
    vR, bE, bO, pair_r, pair_b, tmp = refs[len(PACKED) + 3 :]
    lv = dict(outs, vR=vR)
    slab, box, boxes = place[0], place[1], place[2]
    odd = box & 1

    def source(t, i):
        if i < H0:
            return halo.at[t, odd], i * ROWS + (EDGE - H0 * ROWS)
        if i >= H0 + 32:
            return halo.at[t, 1 - odd], (i - H0 - 32) * ROWS
        x = i - H0
        return (lo.at[t], x * ROWS) if x < 16 else (hi.at[t], (x - 16) * ROWS)

    for i in range(N0):
        for t in range(2):
            ref, base = source(t, i)
            for k, out in enumerate((bE, bO, lv["fR"], lv["fB"], lv["vB"])):
                out[i, 4 * t : 4 * t + 4, :] = ref[base + 4 * k : base + 4 * k + 4, :]

    row, lane = iota((8, 256), 0), iota((8, 256), 1)
    top, bot = row == 7, row == 0
    end, begin = lane == 255, lane == 0

    def faces(i, carry):
        p = parity(i, (8, 256), 1)
        e, o = bE[i], bO[i]
        fxe, fxo = 0.5 * (e + bE[i + 1]), 0.5 * (o + bO[i + 1])
        lv["xR"][i] = jnp.where(p, fxe, fxo)
        lv["xB"][i] = jnp.where(p, fxo, fxe)
        fye = 0.5 * (e + jnp.where(end, 0.0, up(e, 1)))
        fyo = 0.5 * (o + jnp.where(end, 0.0, up(o, 1)))
        gye = 0.5 * (e + jnp.where(begin, 0.0, down(e, 1)))
        gyo = 0.5 * (o + jnp.where(begin, 0.0, down(o, 1)))
        yr, yb = jnp.where(p, fye, fyo), jnp.where(p, fyo, fye)
        lv["yR"][i] = jnp.where(end, 0.0, yr)
        lv["yB"][i] = jnp.where(end, 0.0, yb)
        s = 0.5 * (e + o)
        above = 0.5 * (o + jnp.where(top, 0.0, up(e, 0)))
        below = 0.5 * (e + jnp.where(bot, 0.0, down(o, 0)))
        lv["s"][i] = s
        lv["c"][i] = jnp.where(top, 0.0, above)
        ze, zo = fye + gye + (s + below), fyo + gyo + (s + above)
        lv["cR"][i] = jnp.where(p, ze, zo)
        lv["cB"][i] = jnp.where(p, zo, ze)
        return carry

    lax.fori_loop(0, N0 - 1, faces, 0, unroll=7)

    def inverses(i, carry):
        x = box * 32 - H0 + i
        inside = jnp.logical_and(x >= 0, x < boxes * 32)
        cr = lv["cR"][i] + (lv["xR"][i] + lv["xB"][i - 1])
        cb = lv["cB"][i] + (lv["xB"][i] + lv["xR"][i - 1])
        lv["cR"][i] = cr
        lv["cB"][i] = cb
        lv["iR"][i] = jnp.where(inside, 1.0 / cr, 0.0)
        lv["iB"][i] = jnp.where(inside, 1.0 / cb, 0.0)
        return carry

    lax.fori_loop(1, N0 - 1, inverses, 0, unroll=6)

    for k in range(2):
        sweep_packed(lv, True, 1 + 2 * k, N0 - 1 - 2 * k)
        sweep_packed(lv, False, 2 + 2 * k, N0 - 2 - 2 * k)

    def restrict(j, carry):
        a, b, _ = residual_packed(lv, H0 + 2 * j)
        c, d, _ = residual_packed(lv, H0 + 1 + 2 * j)
        i = H0 + 2 * j
        pair_r[j] = (a + b) + (c + d)
        pair_b[j] = (bE[i] + bO[i]) + (bE[i + 1] + bO[i + 1])
        return carry

    lax.fori_loop(0, 16, restrict, 0, unroll=4)

    halve = one_hot((256, 128), lambda i, j: (i >> 1) == j)
    f1 = 0.125 * matmul(pair_r[...].reshape(128, 256), halve)
    b1 = 0.125 * matmul(pair_b[...].reshape(128, 256), halve)
    own[0:16] = f1.reshape(16, 8, 128)
    own[16:32] = b1.reshape(16, 8, 128)

    for k in range(8):
        tmp[8 * k : 8 * k + 8, :] = own[16 + 2 * k] + own[17 + 2 * k]
    summed = tmp[pl.ds(0, 32, stride=2), :] + tmp[pl.ds(1, 32, stride=2), :]
    halve = one_hot((128, 128), lambda i, j: (i >> 1) == j)
    b2 = 0.125 * matmul(summed, halve)
    own[32:40] = jnp.zeros((8, 8, 128), F32)
    for k in range(8):
        own[32 + k, 0:4, :] = b2[4 * k : 4 * k + 4]
    bottom[...] = bottom_row([own[32 + 2 * k] + own[33 + 2 * k] for k in range(4)], slab)

    first = jnp.where(slab == 0, 1, 0)
    send[0:H1] = own[pl.ds(first * (16 - H1), H1)]
    send[H1 : 2 * H1 + 1] = own[pl.ds(16 + first * (15 - H1), H1 + 1)]
    send[2 * H1 + 1 :] = own[32:40]


def bottom_row(pairs, slab):
    total = None
    for k, plane in enumerate(pairs):
        spread = one_hot((128, 128), lambda i, j, k=k: jnp.logical_and((i >> 1) + 32 * k == j, i < 64))
        part = matmul(plane, spread)
        total = part if total is None else total + part
    low, high = total[0:1] + total[1:2], total[2:3] + total[3:4]
    row = 0.125 * jnp.where(slab == 0, low, high)
    return jnp.broadcast_to(row, (8, 128))


def level_faces(b, ax, ay, az, inv, n, factor, depth, width, inside):
    row, lane = iota((8, 128), 0), iota((8, 128), 1)
    top, bot = row == depth - 1, row == 0
    end, begin = lane == width - 1, lane == 0
    cell = jnp.logical_and(row < depth, lane < width)
    for i in range(n - 1):
        ax[i] = factor * (b[i] + b[i + 1])
    for i in range(1, n - 1):
        v = b[i]
        fy = factor * (v + jnp.where(end, 0.0, up(v, 1)))
        gy = factor * (v + jnp.where(begin, 0.0, down(v, 1)))
        fz = factor * (v + jnp.where(top, 0.0, up(v, 0)))
        gz = factor * (v + jnp.where(bot, 0.0, down(v, 0)))
        ay[i] = jnp.where(end, 0.0, fy)
        az[i] = jnp.where(top, 0.0, fz)
        center = (fz + gz) + (ax[i] + ax[i - 1]) + (fy + gy)
        inv[i] = jnp.where(jnp.logical_and(cell, inside(i)), 1.0 / center, 0.0)


def nsum_plain(v, ax, ay, az, i):
    here = v[i]
    t = ax[i] * v[i + 1] + ax[i - 1] * v[i - 1]
    t = t + (ay[i] * up(here, 1) + down(ay[i] * here, 1))
    return t + (az[i] * up(here, 0) + down(az[i] * here, 0))


def sweep_plain(v, f, ax, ay, az, inv, odd, shift, first, last):
    row, lane = iota((8, 128), 0), iota((8, 128), 1)
    even = ((row + lane) & 1) == 0
    masks = (even, jnp.logical_not(even))
    for i in range(first, last):
        cells = masks[(i + shift + odd) % 2]
        v[i] = jnp.where(cells, (f[i] + nsum_plain(v, ax, ay, az, i)) * inv[i], v[i])


def first_plain(v, f, inv, shift, first, last):
    row, lane = iota((8, 128), 0), iota((8, 128), 1)
    even = ((row + lane) & 1) == 0
    masks = (even, jnp.logical_not(even))
    for i in range(first, last):
        v[i] = jnp.where(masks[(i + shift) % 2], f[i] * inv[i], 0.0)


def residual_plain(v, f, ax, ay, az, center, i):
    return f[i] - (center * v[i] - nsum_plain(v, ax, ay, az, i))


def center_plain(b, ax, i, factor, depth, width):
    row, lane = iota((8, 128), 0), iota((8, 128), 1)
    v = b[i]
    fy = jnp.where(lane == width - 1, 0.0, up(v, 1)) + jnp.where(lane == 0, 0.0, down(v, 1))
    fz = jnp.where(row == depth - 1, 0.0, up(v, 0)) + jnp.where(row == 0, 0.0, down(v, 0))
    return factor * (4.0 * v + fy + fz) + (ax[i] + ax[i - 1])


def middle_kernel(place, own, halo, bottom, v1, f1, ax1, ay1, az1, inv1, ax2, ay2, az2, inv2, send, message, v2, f2, b2, b1, tmp):
    slab, box, boxes = place[0], place[1], place[2]
    w = H1 + 1
    b1[0:w] = halo[0, H1 : H1 + w]
    b1[w : w + 16] = own[16:32]
    b1[w + 16 :] = halo[1, H1 : H1 + w]
    f1[0:1] = jnp.zeros((1, 8, 128), F32)
    f1[1 : 1 + H1] = halo[0, 0:H1]
    f1[w : w + 16] = own[0:16]
    f1[w + 16 : w + 16 + H1] = halo[1, 0:H1]
    f1[N1 - 1 :] = jnp.zeros((1, 8, 128), F32)
    b2[0:8] = halo[0, H1 + w :]
    b2[8:16] = own[32:40]
    b2[16:24] = halo[1, H1 + w :]
    v1[...] = jnp.zeros(v1.shape, F32)
    v2[...] = jnp.zeros(v2.shape, F32)
    f2[...] = jnp.zeros(f2.shape, F32)

    def within(size, width):
        def inside(i):
            x = box * size - width + i
            return jnp.logical_and(x >= 0, x < boxes * size)

        return inside

    k1, k2 = 0.5 * 0.25, 0.5 * 0.25**2
    level_faces(b1, ax1, ay1, az1, inv1, N1, k1, 8, 128, within(16, w))
    level_faces(b2, ax2, ay2, az2, inv2, N2, k2, 4, 64, within(8, 8))

    one = (f1, ax1, ay1, az1, inv1)
    first_plain(v1, f1, inv1, 1, 1, N1 - 1)
    sweep_plain(v1, *one, 1, 1, 2, N1 - 2)
    sweep_plain(v1, *one, 0, 1, 3, N1 - 3)
    sweep_plain(v1, *one, 1, 1, 4, N1 - 4)
    for j in range(16):
        parts = [
            residual_plain(v1, *one[:4], center_plain(b1, ax1, i, k1, 8, 128), i)
            for i in (5 + 2 * j, 6 + 2 * j)
        ]
        tmp[8 * j : 8 * j + 8, :] = parts[0] + parts[1]
    summed = tmp[pl.ds(0, 64, stride=2), :] + tmp[pl.ds(1, 64, stride=2), :]
    coarse = 0.125 * matmul(summed, one_hot((128, 128), lambda i, j: (i >> 1) == j))
    for j in range(16):
        f2[4 + j, 0:4, :] = coarse[4 * j : 4 * j + 4]

    two = (f2, ax2, ay2, az2, inv2)
    first_plain(v2, f2, inv2, 0, 4, 20)
    sweep_plain(v2, *two, 1, 0, 5, 19)
    sweep_plain(v2, *two, 0, 0, 6, 18)
    sweep_plain(v2, *two, 1, 0, 7, 17)
    send[0:8] = v2[8:16]
    send[8:16] = f2[8:16]

    pairs = []
    for k in range(4):
        parts = [
            residual_plain(v2, *two[:4], center_plain(b2, ax2, i, k2, 4, 64), i)
            for i in (8 + 2 * k, 9 + 2 * k)
        ]
        pairs.append(parts[0] + parts[1])
    source = bottom_row(pairs, slab)
    rows = jnp.where((iota((8, 128), 0) & 1) == 0, source, bottom[...])
    for k in range(message.shape[0] // 8):
        message[8 * k : 8 * k + 8, :] = rows


def coarse_solve(n, source, coefficient, dref, qref, eref):
    row, lane = iota((n, 128), 0), iota((n, 128), 1)
    factor = 0.5 * 0.25**3
    last = jnp.logical_and(row == n - 1, lane >= 96)
    first = jnp.logical_and(row == 0, lane < 32)
    inner_hi, inner_lo = lane < 96, lane >= 32
    end, begin = (lane & 31) == 31, (lane & 31) == 0

    def xp(v):
        a = pltpu.roll(v, 96, 1)
        return jnp.where(inner_hi, a, up(a, 0))

    def xm(v):
        a = pltpu.roll(v, 32, 1)
        return jnp.where(inner_lo, a, down(a, 0))

    ax, ay, center = [], [], []
    az = factor * (coefficient[0] + coefficient[1])
    for b in coefficient:
        fx = factor * (b + jnp.where(last, 0.0, xp(b)))
        gx = factor * (b + jnp.where(first, 0.0, xm(b)))
        fy = factor * (b + jnp.where(end, 0.0, up(b, 1)))
        gy = factor * (b + jnp.where(begin, 0.0, down(b, 1)))
        ax.append(jnp.where(last, 0.0, fx))
        ay.append(jnp.where(end, 0.0, fy))
        center.append((factor * b + az) + (fx + gx) + (fy + gy))

    def total(u, w):
        s = u[0] * w[0] + u[1] * w[1]
        return jnp.sum(jnp.sum(s, axis=0, keepdims=True), axis=1, keepdims=True)

    for t in range(2):
        dref[t] = source[t]
        qref[t] = source[t]
        eref[t, 8 : 8 + n] = jnp.zeros((n, 128), F32)
        eref[t, 0:8] = jnp.zeros((8, 128), F32)
        eref[t, 8 + n :] = jnp.zeros((8, 128), F32)

    def iterate(k, now):
        d = (dref[0], dref[1])
        w = []
        for t in range(2):
            v = d[t]
            s = ax[t] * xp(v) + xm(ax[t] * v)
            s = s + (ay[t] * up(v, 1) + down(ay[t] * v, 1))
            w.append(center[t] * v - (s + az * d[1 - t]))
        alpha = now / total(d, w)
        q = []
        for t in range(2):
            eref[t, 8 : 8 + n] = eref[t, 8 : 8 + n] + alpha * d[t]
            q.append(qref[t] - alpha * w[t])
            qref[t] = q[t]
        later = total(q, q)
        beta = later / now
        for t in range(2):
            dref[t] = q[t] + beta * d[t]
        return later

    lax.fori_loop(0, ITERS, iterate, total(source, source))


def last_kernel(boxes, place, *refs):
    names = ("all", "own2", "v1", "f1", "ax1", "ay1", "az1", "inv1", "ax2", "ay2", "az2", "inv2")
    given = dict(zip(names, refs))
    refs = refs[len(names) :]
    level0 = dict(zip(PACKED, refs))
    refs = refs[len(PACKED) :]
    out_v, out_r, vR, vB, v1, v2, f2, dref, qref, eref, wide, e0 = refs
    slab, box = place[0], place[1]
    gathered = given["all"]

    source = [gathered[t, pl.ds(0, boxes, stride=2), :] for t in range(2)]
    coefficient = [gathered[t, pl.ds(1, boxes, stride=2), :] for t in range(2)]
    coarse_solve(boxes, source, coefficient, dref, qref, eref)

    base = 2 * boxes
    for side, at in ((0, 0), (1, 16)):
        for k in range(8):
            v2[at + k] = gathered[side, base + 8 * k : base + 8 * k + 8, :]
            f2[at + k] = gathered[side, base + 64 + 8 * k : base + 64 + 8 * k + 8, :]
    v2[8:16] = given["own2"][0:8]
    f2[8:16] = given["own2"][8:16]
    near = [eref[t, pl.ds(7 + box, 8), :] for t in range(2)]
    spread = one_hot((128, 512), lambda i, j: jnp.logical_and(((j >> 7) * 32) + ((j & 127) >> 1) == i, (j & 127) < 64))
    fine = [matmul(e, spread) for e in near]
    row = iota((8, 128), 0)
    for i in range(N2):
        cell, k = (i // 2) // 4, (i // 2) % 4
        low, high = (f[cell : cell + 1, 128 * k : 128 * k + 128] for f in fine)
        v2[i] = v2[i] + jnp.where(row < 2, low, jnp.where(row < 4, high, 0.0))
    two = (f2, given["ax2"], given["ay2"], given["az2"], given["inv2"])
    for k in range(2):
        sweep_plain(v2, *two, 0, 0, 1 + 2 * k, N2 - 1 - 2 * k)
        sweep_plain(v2, *two, 1, 0, 2 + 2 * k, N2 - 2 - 2 * k)

    packed = jnp.concatenate([v2[4 + j, 0:4, :] for j in range(16)], axis=0)
    fine = matmul(packed, one_hot((128, 128), lambda i, j: (j >> 1) == i))
    wide[pl.ds(0, 64, stride=2), :] = fine
    wide[pl.ds(1, 64, stride=2), :] = fine
    for i in range(6, N1 - 6):
        j = (i + 3) // 2 - 4
        v1[i] = given["v1"][i] + wide[8 * j : 8 * j + 8, :]
    one = (given["f1"], given["ax1"], given["ay1"], given["az1"], given["inv1"])
    for k in range(2):
        sweep_plain(v1, *one, 0, 1, 7 + 2 * k, N1 - 7 - 2 * k)
        sweep_plain(v1, *one, 1, 1, 8 + 2 * k, N1 - 8 - 2 * k)

    double = one_hot((128, 256), lambda i, j: (j >> 1) == i)
    e0[...] = matmul(v1[10:32].reshape(176, 128), double).reshape(22, 8, 256)
    lv = dict(level0, vR=vR, vB=vB)

    def correct(j, carry):
        e = e0[j]
        vB[3 + 2 * j] = level0["vB"][3 + 2 * j] + e
        vB[4 + 2 * j] = level0["vB"][4 + 2 * j] + e
        return carry

    lax.fori_loop(0, 22, correct, 0, unroll=2)
    for k in range(2):
        sweep_packed(lv, True, 5 + 2 * k, N0 - 5 - 2 * k)
        sweep_packed(lv, False, 6 + 2 * k, N0 - 6 - 2 * k)

    for x in range(32):
        i = H0 + x
        red, black, p = residual_packed(lv, i)
        for out, a, b in ((out_v, vR[i], vB[i]), (out_r, red, black)):
            even, odd = jnp.where(p, a, b), jnp.where(p, b, a)
            even = jnp.where(slab == 0, even[0:4], even[4:8])
            odd = jnp.where(slab == 0, odd[0:4], odd[4:8])
            for half in range(2):
                lanes = slice(128 * half, 128 * half + 128)
                out[slab_rows(x, half, 0), :] = even[:, lanes]
                out[slab_rows(x, half, 1), :] = odd[:, lanes]


def call(kernel, outs, scratch, *args, scalars=0, limit=12):
    vmem = pl.BlockSpec(memory_space=pltpu.VMEM)
    smem = pl.BlockSpec(memory_space=pltpu.SMEM)
    return pl.pallas_call(
        kernel,
        out_shape=[jax.ShapeDtypeStruct(s, F32) for s in outs],
        in_specs=[smem] * scalars + [vmem] * (len(args) - scalars),
        out_specs=[vmem] * len(outs),
        scratch_shapes=[pltpu.VMEM(s, F32) for s in scratch],
        compiler_params=pltpu.CompilerParams(vmem_limit_bytes=limit * 1024 * 1024),
    )(*args)


def pack(*args):
    return pl.pallas_call(
        pack_kernel,
        out_shape=[jax.ShapeDtypeStruct((rows, 256), F32) for rows in (16 * ROWS, 16 * ROWS, EDGE, EDGE)],
        in_specs=[pl.BlockSpec(memory_space=pltpu.SMEM)] + [pl.BlockSpec(memory_space=pl.ANY)] * 3,
        out_specs=[pl.BlockSpec(memory_space=pltpu.VMEM)] * 4,
        scratch_shapes=[pltpu.VMEM((512, 128), F32)] * 3 + [pltpu.SemaphoreType.DMA((3,))],
        compiler_params=pltpu.CompilerParams(vmem_limit_bytes=4 * 1024 * 1024),
    )(*args)


def by_tiles(a):
    return a.reshape(8, 4, 8, 2, 128).transpose(0, 1, 3, 2, 4).reshape(512, 128)


def from_tiles(a):
    return a.reshape(8, 4, 2, 8, 128).transpose(0, 1, 3, 2, 4).reshape(8, 32, 256)


def body(pressure_guess, right_side, coefficient):
    boxes = lax.axis_size("box")
    slab, box = lax.axis_index("slab"), lax.axis_index("box")
    place = jnp.stack([slab, box, jnp.int32(boxes), jnp.int32(0)]).astype(jnp.int32)
    both = [(2 * i, 2 * i + 2) for i in range(boxes - 1)] + [(2 * i + 3, 2 * i + 1) for i in range(boxes - 1)]

    flat = [by_tiles(a) for a in (pressure_guess, right_side, coefficient)]
    low, high, first, second = pack(place, *flat)
    odd_pairs = [(i, i + 1) for i in range(1, boxes - 1, 2)]
    even_pairs = [(i, i + 1) for i in range(0, boxes - 1, 2)]
    first = lax.ppermute(first, "box", odd_pairs + [(j, i) for i, j in odd_pairs])
    second = lax.ppermute(second, "box", even_pairs + [(j, i) for i, j in even_pairs])
    low, high = lax.all_gather(low, "slab"), lax.all_gather(high, "slab")
    halo = lax.all_gather(jnp.stack([first, second]), "slab")

    plane = (N0, 8, 256)
    fine = call(
        fine_kernel,
        [plane] * len(PACKED) + [(40, 8, 128), (SEND1, 8, 128), (8, 128)],
        [plane] * 3 + [(16, 8, 256)] * 2 + [(64, 128)],
        place,
        low,
        high,
        halo,
        scalars=1,
    )
    level0 = fine[: len(PACKED)]
    own, send, bottom = fine[len(PACKED) :]
    halo = lax.all_gather(lax.ppermute(send, ("box", "slab"), both), "slab")

    one, two = (N1, 8, 128), (N2, 8, 128)
    *levels, send, message = call(
        middle_kernel,
        [one] * 6 + [two] * 4 + [(16, 8, 128), (2 * boxes, 128)],
        [two] * 3 + [one, (128, 128)],
        place,
        own,
        halo,
        bottom,
        scalars=1,
    )
    beside = lax.ppermute(send, ("box", "slab"), both)
    spread = lax.all_to_all(message.reshape(boxes, 2, 128), "box", 0, 0)
    both_parts = jnp.concatenate([spread.reshape(2 * boxes, 128), beside.reshape(128, 128)], axis=0)
    gathered = lax.all_gather(both_parts, "slab")

    flat_out = [(512, 128)] * 2
    pressure, residual = call(
        functools.partial(last_kernel, boxes),
        flat_out,
        [plane, plane, one, two, two, (2, boxes, 128), (2, boxes, 128), (2, boxes + 16, 128), (128, 128), (22, 8, 256)],
        place,
        gathered,
        send,
        *levels,
        *level0,
        scalars=1,
    )
    return from_tiles(pressure), from_tiles(residual)


def solution(mesh):
    split = P("slab", "box", None)
    return jax.shard_map(body, mesh=mesh, in_specs=(split,) * 3, out_specs=(split,) * 2, check_vma=False)
```

```python
import functools

import jax
import jax.numpy as jnp
from jax import lax
from jax.experimental import pallas as pl
from jax.experimental.pallas import tpu as pltpu
from jax.sharding import PartitionSpec as P

ITERS = 8
F32 = jnp.float32
BF16 = jnp.bfloat16

H0 = 9
H1 = 12
N0 = 32 + 2 * H0
N1 = 16 + 2 * (H1 + 1)
N2 = 24
ROWS = 20
EDGE = 184
SEND1 = H1 + (H1 + 1) + 8


def matmul(x, m):
    high = x.astype(BF16)
    rest = x - high.astype(F32)
    mid = rest.astype(BF16)
    low = (rest - mid.astype(F32)).astype(BF16)
    dot = functools.partial(jnp.dot, preferred_element_type=F32)
    return dot(high, m) + (dot(mid, m) + dot(low, m))


def one_hot(shape, rule):
    i = lax.broadcasted_iota(jnp.int32, shape, 0)
    j = lax.broadcasted_iota(jnp.int32, shape, 1)
    return rule(i, j).astype(F32).astype(BF16)


def iota(shape, axis):
    return lax.broadcasted_iota(jnp.int32, shape, axis)


def up(v, axis):
    return pltpu.roll(v, v.shape[axis] - 1, axis)


def down(v, axis):
    return pltpu.roll(v, 1, axis)


def slab_rows(x, half, odd):
    return pl.ds((x // 8) * 16 + half * 8 + x % 8 + 64 * odd, 4, stride=128)


def pack_kernel(place, g_hbm, r_hbm, c_hbm, low, high, first, second, g, r, c, sem):
    copies = [pltpu.make_async_copy(a, b, sem.at[k]) for k, (a, b) in enumerate(((g_hbm, g), (r_hbm, r), (c_hbm, c)))]
    for copy in copies:
        copy.start()
    for copy in copies:
        copy.wait()
    even_y = (iota((4, 128), 1) & 1) == 0
    odd_y = jnp.logical_not(even_y)
    for x in range(32):
        out, base = (low, x * ROWS) if x < 16 else (high, (x - 16) * ROWS)
        p0 = even_y if x % 2 == 0 else odd_y
        for half in range(2):
            lanes = slice(128 * half, 128 * half + 128)
            even, odd = slab_rows(x, half, 0), slab_rows(x, half, 1)
            out[base : base + 4, lanes] = c[even, :]
            out[base + 4 : base + 8, lanes] = c[odd, :]
            fe, fo = r[even, :], r[odd, :]
            out[base + 8 : base + 12, lanes] = jnp.where(p0, fe, fo)
            out[base + 12 : base + 16, lanes] = jnp.where(p0, fo, fe)
            out[base + 16 : base + 20, lanes] = jnp.where(p0, g[odd, :], g[even, :])

    right_first = (place[1] & 1) == 1

    @pl.when(right_first)
    def _():
        first[...] = high[16 * ROWS - EDGE :, :]
        second[...] = low[:EDGE, :]

    @pl.when(jnp.logical_not(right_first))
    def _():
        first[...] = low[:EDGE, :]
        second[...] = high[16 * ROWS - EDGE :, :]


def parity(i, shape, shift):
    return ((iota(shape, 1) + i + shift) & 1) == 0


def nsum_packed(lv, v, xa, xb, ya, yb, i, p):
    here = v[i]
    t = xa[i] * v[i + 1] + xb[i - 1] * v[i - 1]
    t = t + (ya[i] * up(here, 1) + down(yb[i] * here, 1))
    cross = lv["c"][i]
    z = jnp.where(p, down(cross * here, 0), cross * up(here, 0))
    return t + (lv["s"][i] * here + z)


def sweep_packed(lv, red, first, last):
    def body(i, carry):
        p = parity(i, (8, 256), 1)
        if red:
            n = nsum_packed(lv, lv["vB"], lv["xR"], lv["xB"], lv["yR"], lv["yB"], i, p)
            lv["vR"][i] = (lv["fR"][i] + n) * lv["iR"][i]
        else:
            p = jnp.logical_not(p)
            n = nsum_packed(lv, lv["vR"], lv["xB"], lv["xR"], lv["yB"], lv["yR"], i, p)
            lv["vB"][i] = (lv["fB"][i] + n) * lv["iB"][i]
        return carry

    lax.fori_loop(first, last, body, 0, unroll=6)


def residual_packed(lv, i):
    p = parity(i, (8, 256), 1)
    n = nsum_packed(lv, lv["vB"], lv["xR"], lv["xB"], lv["yR"], lv["yB"], i, p)
    r_red = lv["fR"][i] - (lv["cR"][i] * lv["vR"][i] - n)
    q = jnp.logical_not(p)
    n = nsum_packed(lv, lv["vR"], lv["xB"], lv["xR"], lv["yB"], lv["yR"], i, q)
    r_black = lv["fB"][i] - (lv["cB"][i] * lv["vB"][i] - n)
    return r_red, r_black, p


PACKED = ("vB", "fR", "fB", "xR", "xB", "yR", "yB", "s", "c", "iR", "iB", "cR", "cB")


def fine_kernel(place, lo, hi, halo, *refs):
    outs = dict(zip(PACKED, refs))
    own, send, bottom = refs[len(PACKED) : len(PACKED) + 3]
    vR, bE, bO, pair_r, pair_b, tmp = refs[len(PACKED) + 3 :]
    lv = dict(outs, vR=vR)
    slab, box, boxes = place[0], place[1], place[2]
    odd = box & 1

    def source(t, i):
        if i < H0:
            return halo.at[t, odd], i * ROWS + (EDGE - H0 * ROWS)
        if i >= H0 + 32:
            return halo.at[t, 1 - odd], (i - H0 - 32) * ROWS
        x = i - H0
        return (lo.at[t], x * ROWS) if x < 16 else (hi.at[t], (x - 16) * ROWS)

    for i in range(N0):
        for t in range(2):
            ref, base = source(t, i)
            for k, out in enumerate((bE, bO, lv["fR"], lv["fB"], lv["vB"])):
                out[i, 4 * t : 4 * t + 4, :] = ref[base + 4 * k : base + 4 * k + 4, :]

    row, lane = iota((8, 256), 0), iota((8, 256), 1)
    top, bot = row == 7, row == 0
    end, begin = lane == 255, lane == 0

    def faces(i, carry):
        p = parity(i, (8, 256), 1)
        e, o = bE[i], bO[i]
        fxe, fxo = 0.5 * (e + bE[i + 1]), 0.5 * (o + bO[i + 1])
        lv["xR"][i] = jnp.where(p, fxe, fxo)
        lv["xB"][i] = jnp.where(p, fxo, fxe)
        fye = 0.5 * (e + jnp.where(end, 0.0, up(e, 1)))
        fyo = 0.5 * (o + jnp.where(end, 0.0, up(o, 1)))
        gye = 0.5 * (e + jnp.where(begin, 0.0, down(e, 1)))
        gyo = 0.5 * (o + jnp.where(begin, 0.0, down(o, 1)))
        yr, yb = jnp.where(p, fye, fyo), jnp.where(p, fyo, fye)
        lv["yR"][i] = jnp.where(end, 0.0, yr)
        lv["yB"][i] = jnp.where(end, 0.0, yb)
        s = 0.5 * (e + o)
        above = 0.5 * (o + jnp.where(top, 0.0, up(e, 0)))
        below = 0.5 * (e + jnp.where(bot, 0.0, down(o, 0)))
        lv["s"][i] = s
        lv["c"][i] = jnp.where(top, 0.0, above)
        ze, zo = fye + gye + (s + below), fyo + gyo + (s + above)
        lv["cR"][i] = jnp.where(p, ze, zo)
        lv["cB"][i] = jnp.where(p, zo, ze)
        return carry

    lax.fori_loop(0, N0 - 1, faces, 0, unroll=7)

    def inverses(i, carry):
        x = box * 32 - H0 + i
        inside = jnp.logical_and(x >= 0, x < boxes * 32)
        cr = lv["cR"][i] + (lv["xR"][i] + lv["xB"][i - 1])
        cb = lv["cB"][i] + (lv["xB"][i] + lv["xR"][i - 1])
        lv["cR"][i] = cr
        lv["cB"][i] = cb
        lv["iR"][i] = jnp.where(inside, 1.0 / cr, 0.0)
        lv["iB"][i] = jnp.where(inside, 1.0 / cb, 0.0)
        return carry

    lax.fori_loop(1, N0 - 1, inverses, 0, unroll=6)

    for k in range(2):
        sweep_packed(lv, True, 1 + 2 * k, N0 - 1 - 2 * k)
        sweep_packed(lv, False, 2 + 2 * k, N0 - 2 - 2 * k)

    def restrict(j, carry):
        a, b, _ = residual_packed(lv, H0 + 2 * j)
        c, d, _ = residual_packed(lv, H0 + 1 + 2 * j)
        i = H0 + 2 * j
        pair_r[j] = (a + b) + (c + d)
        pair_b[j] = (bE[i] + bO[i]) + (bE[i + 1] + bO[i + 1])
        return carry

    lax.fori_loop(0, 16, restrict, 0, unroll=4)

    halve = one_hot((256, 128), lambda i, j: (i >> 1) == j)
    f1 = 0.125 * matmul(pair_r[...].reshape(128, 256), halve)
    b1 = 0.125 * matmul(pair_b[...].reshape(128, 256), halve)
    own[0:16] = f1.reshape(16, 8, 128)
    own[16:32] = b1.reshape(16, 8, 128)

    for k in range(8):
        tmp[8 * k : 8 * k + 8, :] = own[16 + 2 * k] + own[17 + 2 * k]
    summed = tmp[pl.ds(0, 32, stride=2), :] + tmp[pl.ds(1, 32, stride=2), :]
    halve = one_hot((128, 128), lambda i, j: (i >> 1) == j)
    b2 = 0.125 * matmul(summed, halve)
    own[32:40] = jnp.zeros((8, 8, 128), F32)
    for k in range(8):
        own[32 + k, 0:4, :] = b2[4 * k : 4 * k + 4]
    bottom[...] = bottom_row([own[32 + 2 * k] + own[33 + 2 * k] for k in range(4)], slab)

    first = jnp.where(slab == 0, 1, 0)
    send[0:H1] = own[pl.ds(first * (16 - H1), H1)]
    send[H1 : 2 * H1 + 1] = own[pl.ds(16 + first * (15 - H1), H1 + 1)]
    send[2 * H1 + 1 :] = own[32:40]


def bottom_row(pairs, slab):
    total = None
    for k, plane in enumerate(pairs):
        spread = one_hot((128, 128), lambda i, j, k=k: jnp.logical_and((i >> 1) + 32 * k == j, i < 64))
        part = matmul(plane, spread)
        total = part if total is None else total + part
    low, high = total[0:1] + total[1:2], total[2:3] + total[3:4]
    row = 0.125 * jnp.where(slab == 0, low, high)
    return jnp.broadcast_to(row, (8, 128))


def level_faces(b, ax, ay, az, inv, n, factor, depth, width, inside):
    row, lane = iota((8, 128), 0), iota((8, 128), 1)
    top, bot = row == depth - 1, row == 0
    end, begin = lane == width - 1, lane == 0
    cell = jnp.logical_and(row < depth, lane < width)
    for i in range(n - 1):
        ax[i] = factor * (b[i] + b[i + 1])
    for i in range(1, n - 1):
        v = b[i]
        fy = factor * (v + jnp.where(end, 0.0, up(v, 1)))
        gy = factor * (v + jnp.where(begin, 0.0, down(v, 1)))
        fz = factor * (v + jnp.where(top, 0.0, up(v, 0)))
        gz = factor * (v + jnp.where(bot, 0.0, down(v, 0)))
        ay[i] = jnp.where(end, 0.0, fy)
        az[i] = jnp.where(top, 0.0, fz)
        center = (fz + gz) + (ax[i] + ax[i - 1]) + (fy + gy)
        inv[i] = jnp.where(jnp.logical_and(cell, inside(i)), 1.0 / center, 0.0)


def nsum_plain(v, ax, ay, az, i):
    here = v[i]
    t = ax[i] * v[i + 1] + ax[i - 1] * v[i - 1]
    t = t + (ay[i] * up(here, 1) + down(ay[i] * here, 1))
    return t + (az[i] * up(here, 0) + down(az[i] * here, 0))


def sweep_plain(v, f, ax, ay, az, inv, odd, shift, first, last):
    row, lane = iota((8, 128), 0), iota((8, 128), 1)
    even = ((row + lane) & 1) == 0
    masks = (even, jnp.logical_not(even))
    for i in range(first, last):
        cells = masks[(i + shift + odd) % 2]
        v[i] = jnp.where(cells, (f[i] + nsum_plain(v, ax, ay, az, i)) * inv[i], v[i])


def first_plain(v, f, inv, shift, first, last):
    row, lane = iota((8, 128), 0), iota((8, 128), 1)
    even = ((row + lane) & 1) == 0
    masks = (even, jnp.logical_not(even))
    for i in range(first, last):
        v[i] = jnp.where(masks[(i + shift) % 2], f[i] * inv[i], 0.0)


def residual_plain(v, f, ax, ay, az, center, i):
    return f[i] - (center * v[i] - nsum_plain(v, ax, ay, az, i))


def center_plain(b, ax, i, factor, depth, width):
    row, lane = iota((8, 128), 0), iota((8, 128), 1)
    v = b[i]
    fy = jnp.where(lane == width - 1, 0.0, up(v, 1)) + jnp.where(lane == 0, 0.0, down(v, 1))
    fz = jnp.where(row == depth - 1, 0.0, up(v, 0)) + jnp.where(row == 0, 0.0, down(v, 0))
    return factor * (4.0 * v + fy + fz) + (ax[i] + ax[i - 1])


def middle_kernel(place, own, halo, bottom, v1, f1, ax1, ay1, az1, inv1, ax2, ay2, az2, inv2, send, message, v2, f2, b2, b1, tmp):
    slab, box, boxes = place[0], place[1], place[2]
    w = H1 + 1
    b1[0:w] = halo[0, H1 : H1 + w]
    b1[w : w + 16] = own[16:32]
    b1[w + 16 :] = halo[1, H1 : H1 + w]
    f1[0:1] = jnp.zeros((1, 8, 128), F32)
    f1[1 : 1 + H1] = halo[0, 0:H1]
    f1[w : w + 16] = own[0:16]
    f1[w + 16 : w + 16 + H1] = halo[1, 0:H1]
    f1[N1 - 1 :] = jnp.zeros((1, 8, 128), F32)
    b2[0:8] = halo[0, H1 + w :]
    b2[8:16] = own[32:40]
    b2[16:24] = halo[1, H1 + w :]
    v1[...] = jnp.zeros(v1.shape, F32)
    v2[...] = jnp.zeros(v2.shape, F32)
    f2[...] = jnp.zeros(f2.shape, F32)

    def within(size, width):
        def inside(i):
            x = box * size - width + i
            return jnp.logical_and(x >= 0, x < boxes * size)

        return inside

    k1, k2 = 0.5 * 0.25, 0.5 * 0.25**2
    level_faces(b1, ax1, ay1, az1, inv1, N1, k1, 8, 128, within(16, w))
    level_faces(b2, ax2, ay2, az2, inv2, N2, k2, 4, 64, within(8, 8))

    one = (f1, ax1, ay1, az1, inv1)
    first_plain(v1, f1, inv1, 1, 1, N1 - 1)
    sweep_plain(v1, *one, 1, 1, 2, N1 - 2)
    sweep_plain(v1, *one, 0, 1, 3, N1 - 3)
    sweep_plain(v1, *one, 1, 1, 4, N1 - 4)
    for j in range(16):
        parts = [
            residual_plain(v1, *one[:4], center_plain(b1, ax1, i, k1, 8, 128), i)
            for i in (5 + 2 * j, 6 + 2 * j)
        ]
        tmp[8 * j : 8 * j + 8, :] = parts[0] + parts[1]
    summed = tmp[pl.ds(0, 64, stride=2), :] + tmp[pl.ds(1, 64, stride=2), :]
    coarse = 0.125 * matmul(summed, one_hot((128, 128), lambda i, j: (i >> 1) == j))
    for j in range(16):
        f2[4 + j, 0:4, :] = coarse[4 * j : 4 * j + 4]

    two = (f2, ax2, ay2, az2, inv2)
    first_plain(v2, f2, inv2, 0, 4, 20)
    sweep_plain(v2, *two, 1, 0, 5, 19)
    sweep_plain(v2, *two, 0, 0, 6, 18)
    sweep_plain(v2, *two, 1, 0, 7, 17)
    send[0:8] = v2[8:16]
    send[8:16] = f2[8:16]

    pairs = []
    for k in range(4):
        parts = [
            residual_plain(v2, *two[:4], center_plain(b2, ax2, i, k2, 4, 64), i)
            for i in (8 + 2 * k, 9 + 2 * k)
        ]
        pairs.append(parts[0] + parts[1])
    source = bottom_row(pairs, slab)
    rows = jnp.where((iota((8, 128), 0) & 1) == 0, source, bottom[...])
    for k in range(message.shape[0] // 8):
        message[8 * k : 8 * k + 8, :] = rows


def coarse_solve(n, source, coefficient, dref, qref, eref):
    row, lane = iota((n, 128), 0), iota((n, 128), 1)
    factor = 0.5 * 0.25**3
    last = jnp.logical_and(row == n - 1, lane >= 96)
    first = jnp.logical_and(row == 0, lane < 32)
    inner_hi, inner_lo = lane < 96, lane >= 32
    end, begin = (lane & 31) == 31, (lane & 31) == 0

    def xp(v):
        a = pltpu.roll(v, 96, 1)
        return jnp.where(inner_hi, a, up(a, 0))

    def xm(v):
        a = pltpu.roll(v, 32, 1)
        return jnp.where(inner_lo, a, down(a, 0))

    ax, ay, center = [], [], []
    az = factor * (coefficient[0] + coefficient[1])
    for b in coefficient:
        fx = factor * (b + jnp.where(last, 0.0, xp(b)))
        gx = factor * (b + jnp.where(first, 0.0, xm(b)))
        fy = factor * (b + jnp.where(end, 0.0, up(b, 1)))
        gy = factor * (b + jnp.where(begin, 0.0, down(b, 1)))
        ax.append(jnp.where(last, 0.0, fx))
        ay.append(jnp.where(end, 0.0, fy))
        center.append((factor * b + az) + (fx + gx) + (fy + gy))

    def total(u, w):
        s = u[0] * w[0] + u[1] * w[1]
        return jnp.sum(jnp.sum(s, axis=0, keepdims=True), axis=1, keepdims=True)

    for t in range(2):
        dref[t] = source[t]
        qref[t] = source[t]
        eref[t, 8 : 8 + n] = jnp.zeros((n, 128), F32)
        eref[t, 0:8] = jnp.zeros((8, 128), F32)
        eref[t, 8 + n :] = jnp.zeros((8, 128), F32)

    def iterate(k, now):
        d = (dref[0], dref[1])
        w = []
        for t in range(2):
            v = d[t]
            s = ax[t] * xp(v) + xm(ax[t] * v)
            s = s + (ay[t] * up(v, 1) + down(ay[t] * v, 1))
            w.append(center[t] * v - (s + az * d[1 - t]))
        alpha = now / total(d, w)
        q = []
        for t in range(2):
            eref[t, 8 : 8 + n] = eref[t, 8 : 8 + n] + alpha * d[t]
            q.append(qref[t] - alpha * w[t])
            qref[t] = q[t]
        later = total(q, q)
        beta = later / now
        for t in range(2):
            dref[t] = q[t] + beta * d[t]
        return later

    lax.fori_loop(0, ITERS, iterate, total(source, source))


def coarse_kernel(boxes, place, gathered, e2, dref, qref, eref):
    box = place[1]
    source = [gathered[t, pl.ds(0, boxes, stride=2), :] for t in range(2)]
    coefficient = [gathered[t, pl.ds(1, boxes, stride=2), :] for t in range(2)]
    coarse_solve(boxes, source, coefficient, dref, qref, eref)
    near = [eref[t, pl.ds(7 + box, 8), :] for t in range(2)]
    spread = one_hot((128, 512), lambda i, j: jnp.logical_and(((j >> 7) * 32) + ((j & 127) >> 1) == i, (j & 127) < 64))
    fine = [matmul(e, spread) for e in near]
    row = iota((8, 128), 0)
    for i in range(N2):
        cell, k = (i // 2) // 4, (i // 2) % 4
        low, high = (f[cell : cell + 1, 128 * k : 128 * k + 128] for f in fine)
        e2[i] = jnp.where(row < 2, low, jnp.where(row < 4, high, 0.0))


def after_kernel(send, gathered, out):
    del gathered
    out[...] = send[...]


def last_kernel(place, *refs):
    names = ("e2", "beside", "own2", "v1", "f1", "ax1", "ay1", "az1", "inv1", "ax2", "ay2", "az2", "inv2")
    given = dict(zip(names, refs))
    refs = refs[len(names) :]
    level0 = dict(zip(PACKED, refs))
    refs = refs[len(PACKED) :]
    out_v, out_r, vR, vB, v1, v2, f2, wide, e0 = refs
    slab = place[0]
    e2, beside, own2 = given["e2"], given["beside"], given["own2"]

    for ref, part in ((v2, 0), (f2, 8)):
        ref[0:8] = beside[0, part : part + 8]
        ref[8:16] = own2[part : part + 8]
        ref[16:24] = beside[1, part : part + 8]
    for i in range(N2):
        v2[i] = v2[i] + e2[i]
    two = (f2, given["ax2"], given["ay2"], given["az2"], given["inv2"])
    for k in range(2):
        sweep_plain(v2, *two, 0, 0, 1 + 2 * k, N2 - 1 - 2 * k)
        sweep_plain(v2, *two, 1, 0, 2 + 2 * k, N2 - 2 - 2 * k)

    packed = jnp.concatenate([v2[4 + j, 0:4, :] for j in range(16)], axis=0)
    fine = matmul(packed, one_hot((128, 128), lambda i, j: (j >> 1) == i))
    wide[pl.ds(0, 64, stride=2), :] = fine
    wide[pl.ds(1, 64, stride=2), :] = fine
    for i in range(6, N1 - 6):
        j = (i + 3) // 2 - 4
        v1[i] = given["v1"][i] + wide[8 * j : 8 * j + 8, :]
    one = (given["f1"], given["ax1"], given["ay1"], given["az1"], given["inv1"])
    for k in range(2):
        sweep_plain(v1, *one, 0, 1, 7 + 2 * k, N1 - 7 - 2 * k)
        sweep_plain(v1, *one, 1, 1, 8 + 2 * k, N1 - 8 - 2 * k)

    double = one_hot((128, 256), lambda i, j: (j >> 1) == i)
    e0[...] = matmul(v1[10:32].reshape(176, 128), double).reshape(22, 8, 256)
    lv = dict(level0, vR=vR, vB=vB)

    def correct(j, carry):
        e = e0[j]
        vB[3 + 2 * j] = level0["vB"][3 + 2 * j] + e
        vB[4 + 2 * j] = level0["vB"][4 + 2 * j] + e
        return carry

    lax.fori_loop(0, 22, correct, 0, unroll=2)
    for k in range(2):
        sweep_packed(lv, True, 5 + 2 * k, N0 - 5 - 2 * k)
        sweep_packed(lv, False, 6 + 2 * k, N0 - 6 - 2 * k)

    for x in range(32):
        i = H0 + x
        red, black, p = residual_packed(lv, i)
        for out, a, b in ((out_v, vR[i], vB[i]), (out_r, red, black)):
            even, odd = jnp.where(p, a, b), jnp.where(p, b, a)
            even = jnp.where(slab == 0, even[0:4], even[4:8])
            odd = jnp.where(slab == 0, odd[0:4], odd[4:8])
            for half in range(2):
                lanes = slice(128 * half, 128 * half + 128)
                out[slab_rows(x, half, 0), :] = even[:, lanes]
                out[slab_rows(x, half, 1), :] = odd[:, lanes]


def call(kernel, outs, scratch, *args, scalars=0, limit=12):
    vmem = pl.BlockSpec(memory_space=pltpu.VMEM)
    smem = pl.BlockSpec(memory_space=pltpu.SMEM)
    return pl.pallas_call(
        kernel,
        out_shape=[jax.ShapeDtypeStruct(s, F32) for s in outs],
        in_specs=[smem] * scalars + [vmem] * (len(args) - scalars),
        out_specs=[vmem] * len(outs),
        scratch_shapes=[pltpu.VMEM(s, F32) for s in scratch],
        compiler_params=pltpu.CompilerParams(vmem_limit_bytes=limit * 1024 * 1024),
    )(*args)


def pack(*args):
    return pl.pallas_call(
        pack_kernel,
        out_shape=[jax.ShapeDtypeStruct((rows, 256), F32) for rows in (16 * ROWS, 16 * ROWS, EDGE, EDGE)],
        in_specs=[pl.BlockSpec(memory_space=pltpu.SMEM)] + [pl.BlockSpec(memory_space=pl.ANY)] * 3,
        out_specs=[pl.BlockSpec(memory_space=pltpu.VMEM)] * 4,
        scratch_shapes=[pltpu.VMEM((512, 128), F32)] * 3 + [pltpu.SemaphoreType.DMA((3,))],
        compiler_params=pltpu.CompilerParams(vmem_limit_bytes=4 * 1024 * 1024),
    )(*args)


def by_tiles(a):
    return a.reshape(8, 4, 8, 2, 128).transpose(0, 1, 3, 2, 4).reshape(512, 128)


def from_tiles(a):
    return a.reshape(8, 4, 2, 8, 128).transpose(0, 1, 3, 2, 4).reshape(8, 32, 256)


def body(pressure_guess, right_side, coefficient):
    boxes = lax.axis_size("box")
    slab, box = lax.axis_index("slab"), lax.axis_index("box")
    place = jnp.stack([slab, box, jnp.int32(boxes), jnp.int32(0)]).astype(jnp.int32)
    both = [(2 * i, 2 * i + 2) for i in range(boxes - 1)] + [(2 * i + 3, 2 * i + 1) for i in range(boxes - 1)]

    flat = [by_tiles(a) for a in (pressure_guess, right_side, coefficient)]
    low, high, first, second = pack(place, *flat)
    odd_pairs = [(i, i + 1) for i in range(1, boxes - 1, 2)]
    even_pairs = [(i, i + 1) for i in range(0, boxes - 1, 2)]
    first = lax.ppermute(first, "box", odd_pairs + [(j, i) for i, j in odd_pairs])
    second = lax.ppermute(second, "box", even_pairs + [(j, i) for i, j in even_pairs])
    low, high = lax.all_gather(low, "slab"), lax.all_gather(high, "slab")
    halo = lax.all_gather(jnp.stack([first, second]), "slab")

    plane = (N0, 8, 256)
    fine = call(
        fine_kernel,
        [plane] * len(PACKED) + [(40, 8, 128), (SEND1, 8, 128), (8, 128)],
        [plane] * 3 + [(16, 8, 256)] * 2 + [(64, 128)],
        place,
        low,
        high,
        halo,
        scalars=1,
    )
    level0 = fine[: len(PACKED)]
    own, send, bottom = fine[len(PACKED) :]
    halo = lax.all_gather(lax.ppermute(send, ("box", "slab"), both), "slab")

    one, two = (N1, 8, 128), (N2, 8, 128)
    *levels, send, message = call(
        middle_kernel,
        [one] * 6 + [two] * 4 + [(16, 8, 128), (2 * boxes, 128)],
        [two] * 3 + [one, (128, 128)],
        place,
        own,
        halo,
        bottom,
        scalars=1,
    )
    spread = lax.all_to_all(message.reshape(boxes, 2, 128), "box", 0, 0).reshape(2 * boxes, 128)
    (late,) = call(after_kernel, [(16, 8, 128)], [], send, spread)
    beside = lax.ppermute(late, ("box", "slab"), both)
    gathered = lax.all_gather(spread, "slab")
    (e2,) = call(
        functools.partial(coarse_kernel, boxes),
        [two],
        [(2, boxes, 128), (2, boxes, 128), (2, boxes + 16, 128)],
        place,
        gathered,
        scalars=1,
    )
    beside = lax.all_gather(beside, "slab")
    pressure, residual = call(
        last_kernel,
        [(512, 128)] * 2,
        [plane, plane, one, two, two, (128, 128), (22, 8, 256)],
        place,
        e2,
        beside,
        send,
        *levels,
        *level0,
        scalars=1,
    )
    return from_tiles(pressure), from_tiles(residual)


def solution(mesh):
    split = P("slab", "box", None)
    return jax.shard_map(body, mesh=mesh, in_specs=(split,) * 3, out_specs=(split,) * 2, check_vma=False)
```

```python
import functools

import jax
import jax.numpy as jnp
from jax import lax
from jax.experimental import pallas as pl
from jax.experimental.pallas import tpu as pltpu
from jax.sharding import PartitionSpec as P

ITERS = 8
F32 = jnp.float32
BF16 = jnp.bfloat16

H0 = 5
H1 = 12
N0 = 32 + 2 * H0
N1 = 16 + 2 * (H1 + 1)
N2 = 24
ROWS = 24
EDGE = H0 * ROWS
SWEEP, FACES, RESTRICT, MERGE, FINISH = 10, 5, 4, 8, 99
SEND1 = H1 + (H1 + 1) + 8


def matmul(x, m):
    high = x.astype(BF16)
    rest = x - high.astype(F32)
    mid = rest.astype(BF16)
    low = (rest - mid.astype(F32)).astype(BF16)
    dot = functools.partial(jnp.dot, preferred_element_type=F32)
    return dot(high, m) + (dot(mid, m) + dot(low, m))


def one_hot(shape, rule):
    i = lax.broadcasted_iota(jnp.int32, shape, 0)
    j = lax.broadcasted_iota(jnp.int32, shape, 1)
    return rule(i, j).astype(F32).astype(BF16)


def iota(shape, axis):
    return lax.broadcasted_iota(jnp.int32, shape, axis)


def up(v, axis):
    return pltpu.roll(v, v.shape[axis] - 1, axis)


def down(v, axis):
    return pltpu.roll(v, 1, axis)


def planes(first, last, unroll, step, carry=0):
    def pair(k, carry):
        i = first + 2 * k
        return step(i + 1, (first + 1) % 2, step(i, first % 2, carry))

    count = (last - first) // 2
    if unroll < count:
        return lax.fori_loop(0, count, pair, carry, unroll=unroll)
    for k in range(count):
        carry = pair(k, carry)
    return carry


def my_place():
    return lax.axis_index("slab"), lax.axis_index("box")


def slab_rows(x, half, odd):
    return pl.ds((x // 8) * 16 + half * 8 + x % 8 + 64 * odd, 4, stride=128)


def pack_plane(g, r, c, x, rows, even_y, out, base):
    p0 = even_y if x % 2 == 0 else jnp.logical_not(even_y)
    for half in range(2):
        lanes = slice(128 * half, 128 * half + 128)
        even, odd = rows(half, 0), rows(half, 1)
        out[base : base + 4, lanes] = c[even, :]
        out[base + 4 : base + 8, lanes] = c[odd, :]
        fe, fo = r[even, :], r[odd, :]
        out[base + 8 : base + 12, lanes] = jnp.where(p0, fe, fo)
        out[base + 12 : base + 16, lanes] = jnp.where(p0, fo, fe)
        out[base + 16 : base + 20, lanes] = jnp.where(p0, g[odd, :], g[even, :])
        out[base + 20 : base + 24, lanes] = jnp.zeros((4, 128), F32)


def pack_kernel(g, r, c, low, high):
    even_y = (iota((4, 128), 1) & 1) == 0
    for x in range(32):
        out, base = (low, x * ROWS) if x < 16 else (high, (x - 16) * ROWS)
        pack_plane(g, r, c, x, functools.partial(slab_rows, x), even_y, out, base)


def edge_kernel(g_hbm, r_hbm, c_hbm, first, second, *scratch):
    left, right, sem = scratch[0:3], scratch[3:6], scratch[6]
    copies = []
    for k, source in enumerate((g_hbm, r_hbm, c_hbm)):
        for side, (target, at) in enumerate(((left[k], 0), (right[k], 48))):
            copies.append(
                pltpu.make_async_copy(source.at[:, at : at + 16, :], target.reshape(8, 16, 128), sem.at[2 * k + side])
            )
    for copy in copies:
        copy.start()
    for copy in copies:
        copy.wait()
    even_y = (iota((4, 128), 1) & 1) == 0

    def pack(parts, start, out):
        for k in range(H0):
            x = start + k
            rows = lambda half, odd, x=x: pl.ds(half * 8 + x % 8 + 16 * odd, 4, stride=32)
            pack_plane(*parts, x, rows, even_y, out, k * ROWS)

    right_first = (my_place()[1] & 1) == 1

    @pl.when(right_first)
    def _():
        pack(right, 32 - H0, first)
        pack(left, 0, second)

    @pl.when(jnp.logical_not(right_first))
    def _():
        pack(left, 0, first)
        pack(right, 32 - H0, second)


def parity(odd):
    return ((iota((8, 256), 1) + odd + 1) & 1) == 0


def nsum_packed(lv, v, xa, xb, ya, yb, i, p):
    here = v[i]
    t = xa[i] * v[i + 1] + xb[i - 1] * v[i - 1]
    t = t + (ya[i] * up(here, 1) + down(yb[i] * here, 1))
    cross = lv["c"][i]
    z = jnp.where(p, down(cross * here, 0), cross * up(here, 0))
    return t + (lv["s"][i] * here + z)


def sweep_packed(lv, red, first, last):
    def step(i, odd, carry):
        p = parity(odd)
        if red:
            n = nsum_packed(lv, lv["vB"], lv["xR"], lv["xB"], lv["yR"], lv["yB"], i, p)
            lv["vR"][i] = (lv["fR"][i] + n) * lv["iR"][i]
        else:
            p = jnp.logical_not(p)
            n = nsum_packed(lv, lv["vR"], lv["xB"], lv["xR"], lv["yB"], lv["yR"], i, p)
            lv["vB"][i] = (lv["fB"][i] + n) * lv["iB"][i]
        return carry

    planes(first, last, SWEEP, step)


def residual_packed(lv, i, odd):
    p = parity(odd)
    n = nsum_packed(lv, lv["vB"], lv["xR"], lv["xB"], lv["yR"], lv["yB"], i, p)
    r_red = lv["fR"][i] - (lv["cR"][i] * lv["vR"][i] - n)
    q = jnp.logical_not(p)
    n = nsum_packed(lv, lv["vR"], lv["xB"], lv["xR"], lv["yB"], lv["yR"], i, q)
    r_black = lv["fB"][i] - (lv["cB"][i] * lv["vB"][i] - n)
    return r_red, r_black, p


PACKED = ("vB", "fR", "fB", "xR", "xB", "yR", "yB", "s", "c", "iR", "iB", "cR", "cB")


def fine_kernel(boxes, lo, hi, halo, *refs):
    outs = dict(zip(PACKED, refs))
    own, send, bottom = refs[len(PACKED) : len(PACKED) + 3]
    vR, bE, bO, pair_r, pair_b, tmp = refs[len(PACKED) + 3 :]
    lv = dict(outs, vR=vR)
    slab, box = my_place()
    odd = box & 1
    row, lane = iota((8, 256), 0), iota((8, 256), 1)
    low_half = row < 4

    def merge(part0, part1, count, first):
        def step(k, carry):
            base = pl.multiple_of(k * ROWS, 8) if not isinstance(k, int) else k * ROWS
            i = first + k
            for at, (low, high) in enumerate(((bE, bO), (lv["fR"], lv["fB"]), (lv["vB"], None))):
                a, b = part0[pl.ds(base + 8 * at, 8), :], part1[pl.ds(base + 8 * at, 8), :]
                low[i] = jnp.where(low_half, a, pltpu.roll(b, 4, 0))
                if high is not None:
                    high[i] = jnp.where(low_half, pltpu.roll(a, 4, 0), b)
            return carry

        lax.fori_loop(0, count, step, 0, unroll=min(count, MERGE))

    merge(halo.at[0, odd], halo.at[1, odd], H0, 0)
    merge(lo.at[0], lo.at[1], 16, H0)
    merge(hi.at[0], hi.at[1], 16, H0 + 16)
    merge(halo.at[0, 1 - odd], halo.at[1, 1 - odd], H0, H0 + 32)

    top, bot = row == 7, row == 0
    end, begin = lane == 255, lane == 0

    def x_faces(i, p):
        fxe, fxo = 0.5 * (bE[i] + bE[i + 1]), 0.5 * (bO[i] + bO[i + 1])
        lv["xR"][i] = jnp.where(p, fxe, fxo)
        lv["xB"][i] = jnp.where(p, fxo, fxe)
        return fxe, fxo

    def faces(i, odd, before):
        p = parity(odd)
        e, o = bE[i], bO[i]
        fxe, fxo = x_faces(i, p)
        fye = 0.5 * (e + jnp.where(end, 0.0, up(e, 1)))
        fyo = 0.5 * (o + jnp.where(end, 0.0, up(o, 1)))
        gye = 0.5 * (e + jnp.where(begin, 0.0, down(e, 1)))
        gyo = 0.5 * (o + jnp.where(begin, 0.0, down(o, 1)))
        yr, yb = jnp.where(p, fye, fyo), jnp.where(p, fyo, fye)
        lv["yR"][i] = jnp.where(end, 0.0, yr)
        lv["yB"][i] = jnp.where(end, 0.0, yb)
        s = 0.5 * (e + o)
        above = 0.5 * (o + jnp.where(top, 0.0, up(e, 0)))
        below = 0.5 * (e + jnp.where(bot, 0.0, down(o, 0)))
        lv["s"][i] = s
        lv["c"][i] = jnp.where(top, 0.0, above)
        ce = fye + gye + (s + below) + (fxe + before[0])
        co = fyo + gyo + (s + above) + (fxo + before[1])
        cr, cb = jnp.where(p, ce, co), jnp.where(p, co, ce)
        lv["cR"][i] = cr
        lv["cB"][i] = cb
        x = box * 32 - H0 + i
        inside = jnp.logical_and(x >= 0, x < boxes * 32)
        lv["iR"][i] = jnp.where(inside, 1.0 / cr, 0.0)
        lv["iB"][i] = jnp.where(inside, 1.0 / cb, 0.0)
        return fxe, fxo

    planes(1, N0 - 1, FACES, faces, x_faces(0, parity(0)))

    for k in range(2):
        sweep_packed(lv, True, 1 + 2 * k, N0 - 1 - 2 * k)
        sweep_packed(lv, False, 2 + 2 * k, N0 - 2 - 2 * k)

    def restrict(j, carry):
        i = H0 + 2 * j
        a, b, _ = residual_packed(lv, i, H0 % 2)
        c, d, _ = residual_packed(lv, i + 1, (H0 + 1) % 2)
        pair_r[j] = (a + b) + (c + d)
        pair_b[j] = (bE[i] + bO[i]) + (bE[i + 1] + bO[i + 1])
        return carry

    lax.fori_loop(0, 16, restrict, 0, unroll=RESTRICT)

    halve = one_hot((256, 128), lambda i, j: (i >> 1) == j)
    f1 = 0.125 * matmul(pair_r[...].reshape(128, 256), halve)
    b1 = 0.125 * matmul(pair_b[...].reshape(128, 256), halve)
    own[0:16] = f1.reshape(16, 8, 128)
    own[16:32] = b1.reshape(16, 8, 128)

    for k in range(8):
        tmp[8 * k : 8 * k + 8, :] = own[16 + 2 * k] + own[17 + 2 * k]
    summed = tmp[pl.ds(0, 32, stride=2), :] + tmp[pl.ds(1, 32, stride=2), :]
    halve = one_hot((128, 128), lambda i, j: (i >> 1) == j)
    b2 = 0.125 * matmul(summed, halve)
    own[32:40] = jnp.zeros((8, 8, 128), F32)
    for k in range(8):
        own[32 + k, 0:4, :] = b2[4 * k : 4 * k + 4]
    bottom[...] = bottom_row([own[32 + 2 * k] + own[33 + 2 * k] for k in range(4)], slab)

    first = jnp.where(slab == 0, 1, 0)
    send[0:H1] = own[pl.ds(first * (16 - H1), H1)]
    send[H1 : 2 * H1 + 1] = own[pl.ds(16 + first * (15 - H1), H1 + 1)]
    send[2 * H1 + 1 :] = own[32:40]


def bottom_row(pairs, slab):
    total = None
    for k, plane in enumerate(pairs):
        spread = one_hot((128, 128), lambda i, j, k=k: jnp.logical_and((i >> 1) + 32 * k == j, i < 64))
        part = matmul(plane, spread)
        total = part if total is None else total + part
    low, high = total[0:1] + total[1:2], total[2:3] + total[3:4]
    row = 0.125 * jnp.where(slab == 0, low, high)
    return jnp.broadcast_to(row, (8, 128))


def level_faces(b, ax, ay, az, inv, n, factor, depth, width, inside):
    row, lane = iota((8, 128), 0), iota((8, 128), 1)
    top, bot = row == depth - 1, row == 0
    end, begin = lane == width - 1, lane == 0
    cell = jnp.logical_and(row < depth, lane < width)
    ax[0] = factor * (b[0] + b[1])

    def step(i, odd, before):
        v = b[i]
        fx = factor * (v + b[i + 1])
        ax[i] = fx
        fy = factor * (v + jnp.where(end, 0.0, up(v, 1)))
        gy = factor * (v + jnp.where(begin, 0.0, down(v, 1)))
        fz = factor * (v + jnp.where(top, 0.0, up(v, 0)))
        gz = factor * (v + jnp.where(bot, 0.0, down(v, 0)))
        ay[i] = jnp.where(end, 0.0, fy)
        az[i] = jnp.where(top, 0.0, fz)
        center = (fz + gz) + (fx + before) + (fy + gy)
        inv[i] = jnp.where(jnp.logical_and(cell, inside(i)), 1.0 / center, 0.0)
        return fx

    planes(1, n - 1, 99, step, ax[0])


def nsum_plain(v, ax, ay, az, i):
    here = v[i]
    t = ax[i] * v[i + 1] + ax[i - 1] * v[i - 1]
    t = t + (ay[i] * up(here, 1) + down(ay[i] * here, 1))
    return t + (az[i] * up(here, 0) + down(az[i] * here, 0))


def colour(odd):
    return ((iota((8, 128), 0) + iota((8, 128), 1) + odd) & 1) == 0


def sweep_plain(v, f, ax, ay, az, inv, odd, shift, first, last):
    def step(i, plane_odd, carry):
        cells = colour((plane_odd + shift + odd) % 2)
        v[i] = jnp.where(cells, (f[i] + nsum_plain(v, ax, ay, az, i)) * inv[i], v[i])
        return carry

    planes(first, last, 99, step)


def first_plain(v, f, inv, shift, first, last):
    def step(i, plane_odd, carry):
        v[i] = jnp.where(colour((plane_odd + shift) % 2), f[i] * inv[i], 0.0)
        return carry

    planes(first, last, 99, step)


def residual_plain(v, f, ax, ay, az, center, i):
    return f[i] - (center * v[i] - nsum_plain(v, ax, ay, az, i))


def center_plain(b, ax, i, factor, depth, width):
    row, lane = iota((8, 128), 0), iota((8, 128), 1)
    v = b[i]
    fy = jnp.where(lane == width - 1, 0.0, up(v, 1)) + jnp.where(lane == 0, 0.0, down(v, 1))
    fz = jnp.where(row == depth - 1, 0.0, up(v, 0)) + jnp.where(row == 0, 0.0, down(v, 0))
    return factor * (4.0 * v + fy + fz) + (ax[i] + ax[i - 1])


def middle_kernel(boxes, own, halo, bottom, v1, f1, ax1, ay1, az1, inv1, ax2, ay2, az2, inv2, send, message, v2, f2, b2, b1, tmp):
    slab, box = my_place()
    w = H1 + 1
    b1[0:w] = halo[0, H1 : H1 + w]
    b1[w : w + 16] = own[16:32]
    b1[w + 16 :] = halo[1, H1 : H1 + w]
    f1[0:1] = jnp.zeros((1, 8, 128), F32)
    f1[1 : 1 + H1] = halo[0, 0:H1]
    f1[w : w + 16] = own[0:16]
    f1[w + 16 : w + 16 + H1] = halo[1, 0:H1]
    f1[N1 - 1 :] = jnp.zeros((1, 8, 128), F32)
    b2[0:8] = halo[0, H1 + w :]
    b2[8:16] = own[32:40]
    b2[16:24] = halo[1, H1 + w :]
    v1[...] = jnp.zeros(v1.shape, F32)
    v2[...] = jnp.zeros(v2.shape, F32)
    f2[...] = jnp.zeros(f2.shape, F32)

    def within(size, width):
        def inside(i):
            x = box * size - width + i
            return jnp.logical_and(x >= 0, x < boxes * size)

        return inside

    k1, k2 = 0.5 * 0.25, 0.5 * 0.25**2
    level_faces(b1, ax1, ay1, az1, inv1, N1, k1, 8, 128, within(16, w))
    level_faces(b2, ax2, ay2, az2, inv2, N2, k2, 4, 64, within(8, 8))

    one = (f1, ax1, ay1, az1, inv1)
    first_plain(v1, f1, inv1, 1, 1, N1 - 1)
    sweep_plain(v1, *one, 1, 1, 2, N1 - 2)
    sweep_plain(v1, *one, 0, 1, 3, N1 - 3)
    sweep_plain(v1, *one, 1, 1, 4, N1 - 4)

    def restrict(j, carry):
        i = 5 + 2 * j
        parts = [residual_plain(v1, *one[:4], center_plain(b1, ax1, k, k1, 8, 128), k) for k in (i, i + 1)]
        tmp[8 * j : 8 * j + 8, :] = parts[0] + parts[1]
        return carry

    for j in range(16):
        restrict(j, 0)
    summed = tmp[pl.ds(0, 64, stride=2), :] + tmp[pl.ds(1, 64, stride=2), :]
    coarse = 0.125 * matmul(summed, one_hot((128, 128), lambda i, j: (i >> 1) == j))
    for j in range(16):
        f2[4 + j, 0:4, :] = coarse[4 * j : 4 * j + 4]

    two = (f2, ax2, ay2, az2, inv2)
    first_plain(v2, f2, inv2, 0, 4, 20)
    sweep_plain(v2, *two, 1, 0, 5, 19)
    sweep_plain(v2, *two, 0, 0, 6, 18)
    sweep_plain(v2, *two, 1, 0, 7, 17)
    send[0:8] = v2[8:16]
    send[8:16] = f2[8:16]

    pairs = []
    for k in range(4):
        parts = [
            residual_plain(v2, *two[:4], center_plain(b2, ax2, i, k2, 4, 64), i)
            for i in (8 + 2 * k, 9 + 2 * k)
        ]
        pairs.append(parts[0] + parts[1])
    source = bottom_row(pairs, slab)
    rows = jnp.where((iota((8, 128), 0) & 1) == 0, source, bottom[...])
    for k in range(message.shape[0] // 8):
        message[8 * k : 8 * k + 8, :] = rows


def coarse_solve(n, source, coefficient, dref, qref, eref):
    row, lane = iota((n, 128), 0), iota((n, 128), 1)
    factor = 0.5 * 0.25**3
    last = jnp.logical_and(row == n - 1, lane >= 96)
    first = jnp.logical_and(row == 0, lane < 32)
    inner_hi, inner_lo = lane < 96, lane >= 32
    end, begin = (lane & 31) == 31, (lane & 31) == 0

    def xp(v):
        a = pltpu.roll(v, 96, 1)
        return jnp.where(inner_hi, a, up(a, 0))

    def xm(v):
        a = pltpu.roll(v, 32, 1)
        return jnp.where(inner_lo, a, down(a, 0))

    ax, ay, center = [], [], []
    az = factor * (coefficient[0] + coefficient[1])
    for b in coefficient:
        fx = factor * (b + jnp.where(last, 0.0, xp(b)))
        gx = factor * (b + jnp.where(first, 0.0, xm(b)))
        fy = factor * (b + jnp.where(end, 0.0, up(b, 1)))
        gy = factor * (b + jnp.where(begin, 0.0, down(b, 1)))
        ax.append(jnp.where(last, 0.0, fx))
        ay.append(jnp.where(end, 0.0, fy))
        center.append((factor * b + az) + (fx + gx) + (fy + gy))

    def total(u, w):
        s = u[0] * w[0] + u[1] * w[1]
        return jnp.sum(jnp.sum(s, axis=0, keepdims=True), axis=1, keepdims=True)

    for t in range(2):
        dref[t] = source[t]
        qref[t] = source[t]
        eref[t, 8 : 8 + n] = jnp.zeros((n, 128), F32)
        eref[t, 0:8] = jnp.zeros((8, 128), F32)
        eref[t, 8 + n :] = jnp.zeros((8, 128), F32)

    def iterate(k, now):
        d = (dref[0], dref[1])
        w = []
        for t in range(2):
            v = d[t]
            s = ax[t] * xp(v) + xm(ax[t] * v)
            s = s + (ay[t] * up(v, 1) + down(ay[t] * v, 1))
            w.append(center[t] * v - (s + az * d[1 - t]))
        alpha = now / total(d, w)
        q = []
        for t in range(2):
            eref[t, 8 : 8 + n] = eref[t, 8 : 8 + n] + alpha * d[t]
            q.append(qref[t] - alpha * w[t])
            qref[t] = q[t]
        later = total(q, q)
        beta = later / now
        for t in range(2):
            dref[t] = q[t] + beta * d[t]
        return later

    lax.fori_loop(0, ITERS, iterate, total(source, source))


def coarse_kernel(boxes, gathered, e2, dref, qref, eref):
    box = my_place()[1]
    source = [gathered[t, pl.ds(0, boxes, stride=2), :] for t in range(2)]
    coefficient = [gathered[t, pl.ds(1, boxes, stride=2), :] for t in range(2)]
    coarse_solve(boxes, source, coefficient, dref, qref, eref)
    near = [eref[t, pl.ds(7 + box, 8), :] for t in range(2)]
    spread = one_hot((128, 512), lambda i, j: jnp.logical_and(((j >> 7) * 32) + ((j & 127) >> 1) == i, (j & 127) < 64))
    fine = [matmul(e, spread) for e in near]
    row = iota((8, 128), 0)
    for i in range(N2):
        cell, k = (i // 2) // 4, (i // 2) % 4
        low, high = (f[cell : cell + 1, 128 * k : 128 * k + 128] for f in fine)
        e2[i] = jnp.where(row < 2, low, jnp.where(row < 4, high, 0.0))


def after_kernel(send, black, gathered, out):
    del gathered
    out[0:16] = send[...]
    start = jnp.where(my_place()[0] == 0, 32, H0)
    for k in range(H0):
        for half in range(2):
            out[16 + 2 * k + half] = black[start + k, :, 128 * half : 128 * half + 128]


def last_kernel(*refs):
    names = ("e2", "beside", "own2", "v1", "f1", "ax1", "ay1", "az1", "inv1", "ax2", "ay2", "az2", "inv2")
    given = dict(zip(names, refs))
    refs = refs[len(names) :]
    level0 = dict(zip(PACKED, refs))
    refs = refs[len(PACKED) :]
    out_v, out_r, vR, vB, v1, v2, f2, wide, e0 = refs
    slab = my_place()[0]
    e2, beside, own2 = given["e2"], given["beside"], given["own2"]

    for ref, part in ((v2, 0), (f2, 8)):
        ref[0:8] = beside[0, part : part + 8]
        ref[8:16] = own2[part : part + 8]
        ref[16:24] = beside[1, part : part + 8]
    for i in range(N2):
        v2[i] = v2[i] + e2[i]
    two = (f2, given["ax2"], given["ay2"], given["az2"], given["inv2"])
    for k in range(2):
        sweep_plain(v2, *two, 0, 0, 1 + 2 * k, N2 - 1 - 2 * k)
        sweep_plain(v2, *two, 1, 0, 2 + 2 * k, N2 - 2 - 2 * k)

    packed = jnp.concatenate([v2[4 + j, 0:4, :] for j in range(16)], axis=0)
    fine = matmul(packed, one_hot((128, 128), lambda i, j: (j >> 1) == i))
    wide[pl.ds(0, 64, stride=2), :] = fine
    wide[pl.ds(1, 64, stride=2), :] = fine
    for i in range(6, N1 - 6):
        j = (i + 3) // 2 - 4
        v1[i] = given["v1"][i] + wide[8 * j : 8 * j + 8, :]
    one = (given["f1"], given["ax1"], given["ay1"], given["az1"], given["inv1"])
    for k in range(2):
        sweep_plain(v1, *one, 0, 1, 7 + 2 * k, N1 - 7 - 2 * k)
        sweep_plain(v1, *one, 1, 1, 8 + 2 * k, N1 - 8 - 2 * k)

    double = one_hot((128, 256), lambda i, j: (j >> 1) == i)
    e0[...] = matmul(v1[10:32].reshape(176, 128), double).reshape(22, 8, 256)
    lv = dict(level0, vR=vR, vB=vB)

    black = level0["vB"]

    def correct(j, carry):
        e = e0[j]
        vB[2 * j - 1] = black[2 * j - 1] + e
        vB[2 * j] = black[2 * j] + e
        return carry

    lax.fori_loop(3, 19, correct, 0, unroll=4)
    for side, at in ((0, 0), (1, H0 + 32)):
        for k in range(H0):
            for half in range(2):
                lanes = slice(128 * half, 128 * half + 128)
                vB[at + k, :, lanes] = beside[side, 16 + 2 * k + half] + e0[(at + k + 1) // 2, :, lanes]
    for k in range(2):
        sweep_packed(lv, True, 1 + 2 * k, N0 - 1 - 2 * k)
        sweep_packed(lv, False, 2 + 2 * k, N0 - 2 - 2 * k)


    def finish(i, odd, carry):
        x = i - H0
        red, black, p = residual_packed(lv, i, odd)
        for out, a, b in ((out_v, vR[i], vB[i]), (out_r, red, black)):
            for at, whole in ((0, jnp.where(p, a, b)), (1, jnp.where(p, b, a))):
                part = jnp.where(slab == 0, whole[0:4], whole[4:8])
                for half in range(2):
                    out[slab_rows(x, half, at), :] = part[:, 128 * half : 128 * half + 128]
        return carry

    planes(H0, H0 + 32, FINISH, finish)


def call(kernel, outs, scratch, *args, limit=12):
    vmem = pl.BlockSpec(memory_space=pltpu.VMEM)
    return pl.pallas_call(
        kernel,
        out_shape=[jax.ShapeDtypeStruct(s, F32) for s in outs],
        in_specs=[vmem] * len(args),
        out_specs=[vmem] * len(outs),
        scratch_shapes=[pltpu.VMEM(s, F32) for s in scratch],
        compiler_params=pltpu.CompilerParams(vmem_limit_bytes=limit * 1024 * 1024),
    )(*args)


def edges(*args):
    return pl.pallas_call(
        edge_kernel,
        out_shape=[jax.ShapeDtypeStruct((EDGE, 256), F32)] * 2,
        in_specs=[pl.BlockSpec(memory_space=pl.ANY)] * 3,
        out_specs=[pl.BlockSpec(memory_space=pltpu.VMEM)] * 2,
        scratch_shapes=[pltpu.VMEM((128, 128), F32)] * 6 + [pltpu.SemaphoreType.DMA((6,))],
        compiler_params=pltpu.CompilerParams(vmem_limit_bytes=60 * 1024 * 1024),
    )(*[a.reshape(8, 64, 128) for a in args])


def by_tiles(a):
    return a.reshape(8, 4, 8, 2, 128).transpose(0, 1, 3, 2, 4).reshape(512, 128)


def from_tiles(a):
    return a.reshape(8, 4, 2, 8, 128).transpose(0, 1, 3, 2, 4).reshape(8, 32, 256)


def body(pressure_guess, right_side, coefficient):
    boxes = lax.axis_size("box")
    both = [(2 * i, 2 * i + 2) for i in range(boxes - 1)] + [(2 * i + 3, 2 * i + 1) for i in range(boxes - 1)]

    flat = [by_tiles(a) for a in (pressure_guess, right_side, coefficient)]
    first, second = edges(*flat)
    low, high = call(pack_kernel, [(16 * ROWS, 256)] * 2, [], *flat)
    odd_pairs = [(i, i + 1) for i in range(1, boxes - 1, 2)]
    even_pairs = [(i, i + 1) for i in range(0, boxes - 1, 2)]
    first = lax.ppermute(first, "box", odd_pairs + [(j, i) for i, j in odd_pairs])
    second = lax.ppermute(second, "box", even_pairs + [(j, i) for i, j in even_pairs])
    low, high = lax.all_gather(low, "slab"), lax.all_gather(high, "slab")
    halo = lax.all_gather(jnp.stack([first, second]), "slab")

    plane = (N0, 8, 256)
    fine = call(
        functools.partial(fine_kernel, boxes),
        [plane] * len(PACKED) + [(40, 8, 128), (SEND1, 8, 128), (8, 128)],
        [plane] * 3 + [(16, 8, 256)] * 2 + [(64, 128)],
        low,
        high,
        halo,
    )
    level0 = fine[: len(PACKED)]
    own, send, bottom = fine[len(PACKED) :]
    halo = lax.all_gather(lax.ppermute(send, ("box", "slab"), both), "slab")

    one, two = (N1, 8, 128), (N2, 8, 128)
    *levels, send, message = call(
        functools.partial(middle_kernel, boxes),
        [one] * 6 + [two] * 4 + [(16, 8, 128), (2 * boxes, 128)],
        [two] * 3 + [one, (128, 128)],
        own,
        halo,
        bottom,
    )
    spread = lax.all_to_all(message.reshape(boxes, 2, 128), "box", 0, 0).reshape(2 * boxes, 128)
    (late,) = call(after_kernel, [(16 + 2 * H0, 8, 128)], [], send, level0[0], spread)
    beside = lax.ppermute(late, ("box", "slab"), both)
    gathered = lax.all_gather(spread, "slab")
    (e2,) = call(
        functools.partial(coarse_kernel, boxes),
        [two],
        [(2, boxes, 128), (2, boxes, 128), (2, boxes + 16, 128)],
        gathered,
    )
    beside = lax.all_gather(beside, "slab")
    pressure, residual = call(
        last_kernel,
        [(512, 128)] * 2,
        [plane, plane, one, two, two, (128, 128), (22, 8, 256)],
        e2,
        beside,
        send,
        *levels,
        *level0,
    )
    return from_tiles(pressure), from_tiles(residual)


def solution(mesh):
    split = P("slab", "box", None)
    return jax.shard_map(body, mesh=mesh, in_specs=(split,) * 3, out_specs=(split,) * 2, check_vma=False)
```

```python
import functools

import jax
import jax.numpy as jnp
from jax import lax
from jax.experimental import pallas as pl
from jax.experimental.pallas import tpu as pltpu
from jax.sharding import PartitionSpec as P

ITERS = 8
F32 = jnp.float32
BF16 = jnp.bfloat16

H0 = 5
H1 = 12
N0 = 32 + 2 * H0
N1 = 16 + 2 * (H1 + 1)
N2 = 24
ROWS = 24
EDGE = H0 * ROWS
SWEEP, FACES, RESTRICT, MERGE, FINISH = 99, 99, 16, 16, 99
SEND1 = H1 + (H1 + 1) + 8


def matmul(x, m):
    high = x.astype(BF16)
    rest = x - high.astype(F32)
    mid = rest.astype(BF16)
    low = (rest - mid.astype(F32)).astype(BF16)
    dot = functools.partial(jnp.dot, preferred_element_type=F32)
    return dot(high, m) + (dot(mid, m) + dot(low, m))


def one_hot(shape, rule):
    i = lax.broadcasted_iota(jnp.int32, shape, 0)
    j = lax.broadcasted_iota(jnp.int32, shape, 1)
    return rule(i, j).astype(F32).astype(BF16)


def iota(shape, axis):
    return lax.broadcasted_iota(jnp.int32, shape, axis)


def up(v, axis):
    return pltpu.roll(v, v.shape[axis] - 1, axis)


def down(v, axis):
    return pltpu.roll(v, 1, axis)


def planes(first, last, unroll, step, carry=0):
    def pair(k, carry):
        i = first + 2 * k
        return step(i + 1, (first + 1) % 2, step(i, first % 2, carry))

    count = (last - first) // 2
    if unroll < count:
        return lax.fori_loop(0, count, pair, carry, unroll=unroll)
    for k in range(count):
        carry = pair(k, carry)
    return carry


def my_place():
    return lax.axis_index("slab"), lax.axis_index("box")


def slab_rows(x, half, odd):
    return pl.ds((x // 8) * 16 + half * 8 + x % 8 + 64 * odd, 4, stride=128)


def pack_plane(g, r, c, x, rows, even_y, out, base):
    p0 = even_y if x % 2 == 0 else jnp.logical_not(even_y)
    for half in range(2):
        lanes = slice(128 * half, 128 * half + 128)
        even, odd = rows(half, 0), rows(half, 1)
        out[base : base + 4, lanes] = c[even, :]
        out[base + 4 : base + 8, lanes] = c[odd, :]
        fe, fo = r[even, :], r[odd, :]
        out[base + 8 : base + 12, lanes] = jnp.where(p0, fe, fo)
        out[base + 12 : base + 16, lanes] = jnp.where(p0, fo, fe)
        out[base + 16 : base + 20, lanes] = jnp.where(p0, g[odd, :], g[even, :])
        out[base + 20 : base + 24, lanes] = jnp.zeros((4, 128), F32)


def pack_kernel(g, r, c, low, high):
    even_y = (iota((4, 128), 1) & 1) == 0
    for x in range(32):
        out, base = (low, x * ROWS) if x < 16 else (high, (x - 16) * ROWS)
        pack_plane(g, r, c, x, functools.partial(slab_rows, x), even_y, out, base)


def edge_kernel(g_hbm, r_hbm, c_hbm, first, second, *scratch):
    left, right, sem = scratch[0:3], scratch[3:6], scratch[6]
    copies = []
    for k, source in enumerate((g_hbm, r_hbm, c_hbm)):
        for side, (target, at) in enumerate(((left[k], 0), (right[k], 48))):
            copies.append(
                pltpu.make_async_copy(source.at[:, at : at + 16, :], target.reshape(8, 16, 128), sem.at[2 * k + side])
            )
    for copy in copies:
        copy.start()
    for copy in copies:
        copy.wait()
    even_y = (iota((4, 128), 1) & 1) == 0

    def pack(parts, start, out):
        for k in range(H0):
            x = start + k
            rows = lambda half, odd, x=x: pl.ds(half * 8 + x % 8 + 16 * odd, 4, stride=32)
            pack_plane(*parts, x, rows, even_y, out, k * ROWS)

    right_first = (my_place()[1] & 1) == 1

    @pl.when(right_first)
    def _():
        pack(right, 32 - H0, first)
        pack(left, 0, second)

    @pl.when(jnp.logical_not(right_first))
    def _():
        pack(left, 0, first)
        pack(right, 32 - H0, second)


def parity(odd):
    return ((iota((8, 256), 1) + odd + 1) & 1) == 0


def nsum_packed(lv, v, xa, xb, ya, yb, i, p):
    here = v[i]
    t = xa[i] * v[i + 1] + xb[i - 1] * v[i - 1]
    t = t + (ya[i] * up(here, 1) + down(yb[i] * here, 1))
    cross = lv["c"][i]
    z = jnp.where(p, down(cross * here, 0), cross * up(here, 0))
    return t + (lv["s"][i] * here + z)


def sweep_packed(lv, red, first, last):
    def step(i, odd, carry):
        p = parity(odd)
        if red:
            n = nsum_packed(lv, lv["vB"], lv["xR"], lv["xB"], lv["yR"], lv["yB"], i, p)
            lv["vR"][i] = (lv["fR"][i] + n) * lv["iR"][i]
        else:
            p = jnp.logical_not(p)
            n = nsum_packed(lv, lv["vR"], lv["xB"], lv["xR"], lv["yB"], lv["yR"], i, p)
            lv["vB"][i] = (lv["fB"][i] + n) * lv["iB"][i]
        return carry

    planes(first, last, SWEEP, step)


def residual_packed(lv, i, odd):
    p = parity(odd)
    n = nsum_packed(lv, lv["vB"], lv["xR"], lv["xB"], lv["yR"], lv["yB"], i, p)
    r_red = lv["fR"][i] - (lv["cR"][i] * lv["vR"][i] - n)
    q = jnp.logical_not(p)
    n = nsum_packed(lv, lv["vR"], lv["xB"], lv["xR"], lv["yB"], lv["yR"], i, q)
    r_black = lv["fB"][i] - (lv["cB"][i] * lv["vB"][i] - n)
    return r_red, r_black, p


PACKED = ("vB", "fR", "fB", "xR", "xB", "yR", "yB", "s", "c", "iR", "iB", "cR", "cB")


def fine_kernel(boxes, lo, hi, halo, *refs):
    outs = dict(zip(PACKED, refs))
    own, send, bottom = refs[len(PACKED) : len(PACKED) + 3]
    vR, bE, bO, pair_r, pair_b, tmp = refs[len(PACKED) + 3 :]
    lv = dict(outs, vR=vR)
    slab, box = my_place()
    odd = box & 1
    row, lane = iota((8, 256), 0), iota((8, 256), 1)
    low_half = row < 4

    def merge(part0, part1, count, first):
        def step(k, carry):
            base = pl.multiple_of(k * ROWS, 8) if not isinstance(k, int) else k * ROWS
            i = first + k
            for at, (low, high) in enumerate(((bE, bO), (lv["fR"], lv["fB"]), (lv["vB"], None))):
                a, b = part0[pl.ds(base + 8 * at, 8), :], part1[pl.ds(base + 8 * at, 8), :]
                low[i] = jnp.where(low_half, a, pltpu.roll(b, 4, 0))
                if high is not None:
                    high[i] = jnp.where(low_half, pltpu.roll(a, 4, 0), b)
            return carry

        lax.fori_loop(0, count, step, 0, unroll=min(count, MERGE))

    merge(halo.at[0, odd], halo.at[1, odd], H0, 0)
    merge(lo.at[0], lo.at[1], 16, H0)
    merge(hi.at[0], hi.at[1], 16, H0 + 16)
    merge(halo.at[0, 1 - odd], halo.at[1, 1 - odd], H0, H0 + 32)

    top, bot = row == 7, row == 0
    end, begin = lane == 255, lane == 0

    def x_faces(i, p):
        fxe, fxo = 0.5 * (bE[i] + bE[i + 1]), 0.5 * (bO[i] + bO[i + 1])
        lv["xR"][i] = jnp.where(p, fxe, fxo)
        lv["xB"][i] = jnp.where(p, fxo, fxe)
        return fxe, fxo

    def faces(i, odd, before):
        p = parity(odd)
        e, o = bE[i], bO[i]
        fxe, fxo = x_faces(i, p)
        fye = 0.5 * (e + jnp.where(end, 0.0, up(e, 1)))
        fyo = 0.5 * (o + jnp.where(end, 0.0, up(o, 1)))
        gye = 0.5 * (e + jnp.where(begin, 0.0, down(e, 1)))
        gyo = 0.5 * (o + jnp.where(begin, 0.0, down(o, 1)))
        yr, yb = jnp.where(p, fye, fyo), jnp.where(p, fyo, fye)
        lv["yR"][i] = jnp.where(end, 0.0, yr)
        lv["yB"][i] = jnp.where(end, 0.0, yb)
        s = 0.5 * (e + o)
        above = 0.5 * (o + jnp.where(top, 0.0, up(e, 0)))
        below = 0.5 * (e + jnp.where(bot, 0.0, down(o, 0)))
        lv["s"][i] = s
        lv["c"][i] = jnp.where(top, 0.0, above)
        ce = fye + gye + (s + below) + (fxe + before[0])
        co = fyo + gyo + (s + above) + (fxo + before[1])
        cr, cb = jnp.where(p, ce, co), jnp.where(p, co, ce)
        lv["cR"][i] = cr
        lv["cB"][i] = cb
        x = box * 32 - H0 + i
        inside = jnp.logical_and(x >= 0, x < boxes * 32)
        lv["iR"][i] = jnp.where(inside, 1.0 / cr, 0.0)
        lv["iB"][i] = jnp.where(inside, 1.0 / cb, 0.0)
        return fxe, fxo

    planes(1, N0 - 1, FACES, faces, x_faces(0, parity(0)))

    for k in range(2):
        sweep_packed(lv, True, 1 + 2 * k, N0 - 1 - 2 * k)
        sweep_packed(lv, False, 2 + 2 * k, N0 - 2 - 2 * k)

    def restrict(j, carry):
        i = H0 + 2 * j
        a, b, _ = residual_packed(lv, i, H0 % 2)
        c, d, _ = residual_packed(lv, i + 1, (H0 + 1) % 2)
        pair_r[j] = (a + b) + (c + d)
        pair_b[j] = (bE[i] + bO[i]) + (bE[i + 1] + bO[i + 1])
        return carry

    lax.fori_loop(0, 16, restrict, 0, unroll=RESTRICT)

    halve = one_hot((256, 128), lambda i, j: (i >> 1) == j)
    f1 = 0.125 * matmul(pair_r[...].reshape(128, 256), halve)
    b1 = 0.125 * matmul(pair_b[...].reshape(128, 256), halve)
    own[0:16] = f1.reshape(16, 8, 128)
    own[16:32] = b1.reshape(16, 8, 128)

    for k in range(8):
        tmp[8 * k : 8 * k + 8, :] = own[16 + 2 * k] + own[17 + 2 * k]
    summed = tmp[pl.ds(0, 32, stride=2), :] + tmp[pl.ds(1, 32, stride=2), :]
    halve = one_hot((128, 128), lambda i, j: (i >> 1) == j)
    b2 = 0.125 * matmul(summed, halve)
    own[32:40] = jnp.zeros((8, 8, 128), F32)
    for k in range(8):
        own[32 + k, 0:4, :] = b2[4 * k : 4 * k + 4]
    bottom[...] = bottom_row([own[32 + 2 * k] + own[33 + 2 * k] for k in range(4)], slab)

    first = jnp.where(slab == 0, 1, 0)
    send[0:H1] = own[pl.ds(first * (16 - H1), H1)]
    send[H1 : 2 * H1 + 1] = own[pl.ds(16 + first * (15 - H1), H1 + 1)]
    send[2 * H1 + 1 :] = own[32:40]


def bottom_row(pairs, slab):
    total = None
    for k, plane in enumerate(pairs):
        spread = one_hot((128, 128), lambda i, j, k=k: jnp.logical_and((i >> 1) + 32 * k == j, i < 64))
        part = matmul(plane, spread)
        total = part if total is None else total + part
    low, high = total[0:1] + total[1:2], total[2:3] + total[3:4]
    row = 0.125 * jnp.where(slab == 0, low, high)
    return jnp.broadcast_to(row, (8, 128))


def level_faces(b, ax, ay, az, inv, n, factor, depth, width, inside):
    row, lane = iota((8, 128), 0), iota((8, 128), 1)
    top, bot = row == depth - 1, row == 0
    end, begin = lane == width - 1, lane == 0
    cell = jnp.logical_and(row < depth, lane < width)
    ax[0] = factor * (b[0] + b[1])

    def step(i, odd, before):
        v = b[i]
        fx = factor * (v + b[i + 1])
        ax[i] = fx
        fy = factor * (v + jnp.where(end, 0.0, up(v, 1)))
        gy = factor * (v + jnp.where(begin, 0.0, down(v, 1)))
        fz = factor * (v + jnp.where(top, 0.0, up(v, 0)))
        gz = factor * (v + jnp.where(bot, 0.0, down(v, 0)))
        ay[i] = jnp.where(end, 0.0, fy)
        az[i] = jnp.where(top, 0.0, fz)
        center = (fz + gz) + (fx + before) + (fy + gy)
        inv[i] = jnp.where(jnp.logical_and(cell, inside(i)), 1.0 / center, 0.0)
        return fx

    planes(1, n - 1, 99, step, ax[0])


def nsum_plain(v, ax, ay, az, i):
    here = v[i]
    t = ax[i] * v[i + 1] + ax[i - 1] * v[i - 1]
    t = t + (ay[i] * up(here, 1) + down(ay[i] * here, 1))
    return t + (az[i] * up(here, 0) + down(az[i] * here, 0))


def colour(odd):
    return ((iota((8, 128), 0) + iota((8, 128), 1) + odd) & 1) == 0


def sweep_plain(v, f, ax, ay, az, inv, odd, shift, first, last):
    def step(i, plane_odd, carry):
        cells = colour((plane_odd + shift + odd) % 2)
        v[i] = jnp.where(cells, (f[i] + nsum_plain(v, ax, ay, az, i)) * inv[i], v[i])
        return carry

    planes(first, last, 99, step)


def first_plain(v, f, inv, shift, first, last):
    def step(i, plane_odd, carry):
        v[i] = jnp.where(colour((plane_odd + shift) % 2), f[i] * inv[i], 0.0)
        return carry

    planes(first, last, 99, step)


def residual_plain(v, f, ax, ay, az, center, i):
    return f[i] - (center * v[i] - nsum_plain(v, ax, ay, az, i))


def center_plain(b, ax, i, factor, depth, width):
    row, lane = iota((8, 128), 0), iota((8, 128), 1)
    v = b[i]
    fy = jnp.where(lane == width - 1, 0.0, up(v, 1)) + jnp.where(lane == 0, 0.0, down(v, 1))
    fz = jnp.where(row == depth - 1, 0.0, up(v, 0)) + jnp.where(row == 0, 0.0, down(v, 0))
    return factor * (4.0 * v + fy + fz) + (ax[i] + ax[i - 1])


def middle_kernel(boxes, own, halo, bottom, v1, f1, ax1, ay1, az1, inv1, ax2, ay2, az2, inv2, send, message, v2, f2, b2, b1, tmp):
    slab, box = my_place()
    w = H1 + 1
    b1[0:w] = halo[0, H1 : H1 + w]
    b1[w : w + 16] = own[16:32]
    b1[w + 16 :] = halo[1, H1 : H1 + w]
    f1[0:1] = jnp.zeros((1, 8, 128), F32)
    f1[1 : 1 + H1] = halo[0, 0:H1]
    f1[w : w + 16] = own[0:16]
    f1[w + 16 : w + 16 + H1] = halo[1, 0:H1]
    f1[N1 - 1 :] = jnp.zeros((1, 8, 128), F32)
    b2[0:8] = halo[0, H1 + w :]
    b2[8:16] = own[32:40]
    b2[16:24] = halo[1, H1 + w :]
    v1[...] = jnp.zeros(v1.shape, F32)
    v2[...] = jnp.zeros(v2.shape, F32)
    f2[...] = jnp.zeros(f2.shape, F32)

    def within(size, width):
        def inside(i):
            x = box * size - width + i
            return jnp.logical_and(x >= 0, x < boxes * size)

        return inside

    k1, k2 = 0.5 * 0.25, 0.5 * 0.25**2
    level_faces(b1, ax1, ay1, az1, inv1, N1, k1, 8, 128, within(16, w))
    level_faces(b2, ax2, ay2, az2, inv2, N2, k2, 4, 64, within(8, 8))

    one = (f1, ax1, ay1, az1, inv1)
    first_plain(v1, f1, inv1, 1, 1, N1 - 1)
    sweep_plain(v1, *one, 1, 1, 2, N1 - 2)
    sweep_plain(v1, *one, 0, 1, 3, N1 - 3)
    sweep_plain(v1, *one, 1, 1, 4, N1 - 4)

    def restrict(j, carry):
        i = 5 + 2 * j
        parts = [residual_plain(v1, *one[:4], center_plain(b1, ax1, k, k1, 8, 128), k) for k in (i, i + 1)]
        tmp[8 * j : 8 * j + 8, :] = parts[0] + parts[1]
        return carry

    for j in range(16):
        restrict(j, 0)
    summed = tmp[pl.ds(0, 64, stride=2), :] + tmp[pl.ds(1, 64, stride=2), :]
    coarse = 0.125 * matmul(summed, one_hot((128, 128), lambda i, j: (i >> 1) == j))
    for j in range(16):
        f2[4 + j, 0:4, :] = coarse[4 * j : 4 * j + 4]

    two = (f2, ax2, ay2, az2, inv2)
    first_plain(v2, f2, inv2, 0, 4, 20)
    sweep_plain(v2, *two, 1, 0, 5, 19)
    sweep_plain(v2, *two, 0, 0, 6, 18)
    sweep_plain(v2, *two, 1, 0, 7, 17)
    send[0:8] = v2[8:16]
    send[8:16] = f2[8:16]

    pairs = []
    for k in range(4):
        parts = [
            residual_plain(v2, *two[:4], center_plain(b2, ax2, i, k2, 4, 64), i)
            for i in (8 + 2 * k, 9 + 2 * k)
        ]
        pairs.append(parts[0] + parts[1])
    source = bottom_row(pairs, slab)
    rows = jnp.where((iota((8, 128), 0) & 1) == 0, source, bottom[...])
    for k in range(message.shape[0] // 8):
        message[8 * k : 8 * k + 8, :] = rows


def coarse_solve(n, source, coefficient, dref, qref, eref):
    row, lane = iota((n, 128), 0), iota((n, 128), 1)
    factor = 0.5 * 0.25**3
    last = jnp.logical_and(row == n - 1, lane >= 96)
    first = jnp.logical_and(row == 0, lane < 32)
    inner_hi, inner_lo = lane < 96, lane >= 32
    end, begin = (lane & 31) == 31, (lane & 31) == 0

    def xp(v):
        a = pltpu.roll(v, 96, 1)
        return jnp.where(inner_hi, a, up(a, 0))

    def xm(v):
        a = pltpu.roll(v, 32, 1)
        return jnp.where(inner_lo, a, down(a, 0))

    ax, ay, center = [], [], []
    az = factor * (coefficient[0] + coefficient[1])
    for b in coefficient:
        fx = factor * (b + jnp.where(last, 0.0, xp(b)))
        gx = factor * (b + jnp.where(first, 0.0, xm(b)))
        fy = factor * (b + jnp.where(end, 0.0, up(b, 1)))
        gy = factor * (b + jnp.where(begin, 0.0, down(b, 1)))
        ax.append(jnp.where(last, 0.0, fx))
        ay.append(jnp.where(end, 0.0, fy))
        center.append((factor * b + az) + (fx + gx) + (fy + gy))

    def total(u, w):
        s = u[0] * w[0] + u[1] * w[1]
        return jnp.sum(jnp.sum(s, axis=0, keepdims=True), axis=1, keepdims=True)

    for t in range(2):
        dref[t] = source[t]
        qref[t] = source[t]
        eref[t, 8 : 8 + n] = jnp.zeros((n, 128), F32)
        eref[t, 0:8] = jnp.zeros((8, 128), F32)
        eref[t, 8 + n :] = jnp.zeros((8, 128), F32)

    def iterate(k, now):
        d = (dref[0], dref[1])
        w = []
        for t in range(2):
            v = d[t]
            s = ax[t] * xp(v) + xm(ax[t] * v)
            s = s + (ay[t] * up(v, 1) + down(ay[t] * v, 1))
            w.append(center[t] * v - (s + az * d[1 - t]))
        alpha = now / total(d, w)
        q = []
        for t in range(2):
            eref[t, 8 : 8 + n] = eref[t, 8 : 8 + n] + alpha * d[t]
            q.append(qref[t] - alpha * w[t])
            qref[t] = q[t]
        later = total(q, q)
        beta = later / now
        for t in range(2):
            dref[t] = q[t] + beta * d[t]
        return later

    lax.fori_loop(0, ITERS, iterate, total(source, source))


def coarse_kernel(boxes, gathered, e2, dref, qref, eref):
    box = my_place()[1]
    source = [gathered[t, pl.ds(0, boxes, stride=2), :] for t in range(2)]
    coefficient = [gathered[t, pl.ds(1, boxes, stride=2), :] for t in range(2)]
    coarse_solve(boxes, source, coefficient, dref, qref, eref)
    near = [eref[t, pl.ds(7 + box, 8), :] for t in range(2)]
    spread = one_hot((128, 512), lambda i, j: jnp.logical_and(((j >> 7) * 32) + ((j & 127) >> 1) == i, (j & 127) < 64))
    fine = [matmul(e, spread) for e in near]
    row = iota((8, 128), 0)
    for i in range(N2):
        cell, k = (i // 2) // 4, (i // 2) % 4
        low, high = (f[cell : cell + 1, 128 * k : 128 * k + 128] for f in fine)
        e2[i] = jnp.where(row < 2, low, jnp.where(row < 4, high, 0.0))


def after_kernel(send, black, gathered, out):
    del gathered
    out[0:16] = send[...]
    start = jnp.where(my_place()[0] == 0, 32, H0)
    for k in range(H0):
        for half in range(2):
            out[16 + 2 * k + half] = black[start + k, :, 128 * half : 128 * half + 128]


def last_kernel(*refs):
    names = ("e2", "beside", "own2", "v1", "f1", "ax1", "ay1", "az1", "inv1", "ax2", "ay2", "az2", "inv2")
    given = dict(zip(names, refs))
    refs = refs[len(names) :]
    level0 = dict(zip(PACKED, refs))
    refs = refs[len(PACKED) :]
    out_v, out_r, vR, vB, v1, v2, f2, wide, e0 = refs
    slab = my_place()[0]
    e2, beside, own2 = given["e2"], given["beside"], given["own2"]

    for ref, part in ((v2, 0), (f2, 8)):
        ref[0:8] = beside[0, part : part + 8]
        ref[8:16] = own2[part : part + 8]
        ref[16:24] = beside[1, part : part + 8]
    for i in range(N2):
        v2[i] = v2[i] + e2[i]
    two = (f2, given["ax2"], given["ay2"], given["az2"], given["inv2"])
    for k in range(2):
        sweep_plain(v2, *two, 0, 0, 1 + 2 * k, N2 - 1 - 2 * k)
        sweep_plain(v2, *two, 1, 0, 2 + 2 * k, N2 - 2 - 2 * k)

    packed = jnp.concatenate([v2[4 + j, 0:4, :] for j in range(16)], axis=0)
    fine = matmul(packed, one_hot((128, 128), lambda i, j: (j >> 1) == i))
    wide[pl.ds(0, 64, stride=2), :] = fine
    wide[pl.ds(1, 64, stride=2), :] = fine
    for i in range(6, N1 - 6):
        j = (i + 3) // 2 - 4
        v1[i] = given["v1"][i] + wide[8 * j : 8 * j + 8, :]
    one = (given["f1"], given["ax1"], given["ay1"], given["az1"], given["inv1"])
    for k in range(2):
        sweep_plain(v1, *one, 0, 1, 7 + 2 * k, N1 - 7 - 2 * k)
        sweep_plain(v1, *one, 1, 1, 8 + 2 * k, N1 - 8 - 2 * k)

    double = one_hot((128, 256), lambda i, j: (j >> 1) == i)
    e0[...] = matmul(v1[10:32].reshape(176, 128), double).reshape(22, 8, 256)
    lv = dict(level0, vR=vR, vB=vB)

    black = level0["vB"]

    def correct(j, carry):
        e = e0[j]
        vB[2 * j - 1] = black[2 * j - 1] + e
        vB[2 * j] = black[2 * j] + e
        return carry

    lax.fori_loop(3, 19, correct, 0, unroll=4)
    for side, at in ((0, 0), (1, H0 + 32)):
        for k in range(H0):
            for half in range(2):
                lanes = slice(128 * half, 128 * half + 128)
                vB[at + k, :, lanes] = beside[side, 16 + 2 * k + half] + e0[(at + k + 1) // 2, :, lanes]
    for k in range(2):
        sweep_packed(lv, True, 1 + 2 * k, N0 - 1 - 2 * k)
        sweep_packed(lv, False, 2 + 2 * k, N0 - 2 - 2 * k)


    def finish(i, odd, carry):
        x = i - H0
        red, black, p = residual_packed(lv, i, odd)
        for out, a, b in ((out_v, vR[i], vB[i]), (out_r, red, black)):
            for at, whole in ((0, jnp.where(p, a, b)), (1, jnp.where(p, b, a))):
                part = jnp.where(slab == 0, whole[0:4], whole[4:8])
                for half in range(2):
                    out[slab_rows(x, half, at), :] = part[:, 128 * half : 128 * half + 128]
        return carry

    planes(H0, H0 + 32, FINISH, finish)


def call(kernel, outs, scratch, *args, limit=12):
    vmem = pl.BlockSpec(memory_space=pltpu.VMEM)
    return pl.pallas_call(
        kernel,
        out_shape=[jax.ShapeDtypeStruct(s, F32) for s in outs],
        in_specs=[vmem] * len(args),
        out_specs=[vmem] * len(outs),
        scratch_shapes=[pltpu.VMEM(s, F32) for s in scratch],
        compiler_params=pltpu.CompilerParams(vmem_limit_bytes=limit * 1024 * 1024),
    )(*args)


def edges(*args):
    return pl.pallas_call(
        edge_kernel,
        out_shape=[jax.ShapeDtypeStruct((EDGE, 256), F32)] * 2,
        in_specs=[pl.BlockSpec(memory_space=pl.ANY)] * 3,
        out_specs=[pl.BlockSpec(memory_space=pltpu.VMEM)] * 2,
        scratch_shapes=[pltpu.VMEM((128, 128), F32)] * 6 + [pltpu.SemaphoreType.DMA((6,))],
        compiler_params=pltpu.CompilerParams(vmem_limit_bytes=60 * 1024 * 1024),
    )(*[a.reshape(8, 64, 128) for a in args])


def by_tiles(a):
    return a.reshape(8, 4, 8, 2, 128).transpose(0, 1, 3, 2, 4).reshape(512, 128)


def from_tiles(a):
    return a.reshape(8, 4, 2, 8, 128).transpose(0, 1, 3, 2, 4).reshape(8, 32, 256)


def body(pressure_guess, right_side, coefficient):
    boxes = lax.axis_size("box")
    both = [(2 * i, 2 * i + 2) for i in range(boxes - 1)] + [(2 * i + 3, 2 * i + 1) for i in range(boxes - 1)]

    flat = [by_tiles(a) for a in (pressure_guess, right_side, coefficient)]
    first, second = edges(*flat)
    low, high = call(pack_kernel, [(16 * ROWS, 256)] * 2, [], *flat)
    odd_pairs = [(i, i + 1) for i in range(1, boxes - 1, 2)]
    even_pairs = [(i, i + 1) for i in range(0, boxes - 1, 2)]
    first = lax.ppermute(first, "box", odd_pairs + [(j, i) for i, j in odd_pairs])
    second = lax.ppermute(second, "box", even_pairs + [(j, i) for i, j in even_pairs])
    low, high = lax.all_gather(low, "slab"), lax.all_gather(high, "slab")
    halo = lax.all_gather(jnp.stack([first, second]), "slab")

    plane = (N0, 8, 256)
    fine = call(
        functools.partial(fine_kernel, boxes),
        [plane] * len(PACKED) + [(40, 8, 128), (SEND1, 8, 128), (8, 128)],
        [plane] * 3 + [(16, 8, 256)] * 2 + [(64, 128)],
        low,
        high,
        halo,
    )
    level0 = fine[: len(PACKED)]
    own, send, bottom = fine[len(PACKED) :]
    halo = lax.all_gather(lax.ppermute(send, ("box", "slab"), both), "slab")

    one, two = (N1, 8, 128), (N2, 8, 128)
    *levels, send, message = call(
        functools.partial(middle_kernel, boxes),
        [one] * 6 + [two] * 4 + [(16, 8, 128), (2 * boxes, 128)],
        [two] * 3 + [one, (128, 128)],
        own,
        halo,
        bottom,
    )
    spread = lax.all_to_all(message.reshape(boxes, 2, 128), "box", 0, 0).reshape(2 * boxes, 128)
    (late,) = call(after_kernel, [(16 + 2 * H0, 8, 128)], [], send, level0[0], spread)
    beside = lax.ppermute(late, ("box", "slab"), both)
    gathered = lax.all_gather(spread, "slab")
    (e2,) = call(
        functools.partial(coarse_kernel, boxes),
        [two],
        [(2, boxes, 128), (2, boxes, 128), (2, boxes + 16, 128)],
        gathered,
    )
    beside = lax.all_gather(beside, "slab")
    pressure, residual = call(
        last_kernel,
        [(512, 128)] * 2,
        [plane, plane, one, two, two, (128, 128), (22, 8, 256)],
        e2,
        beside,
        send,
        *levels,
        *level0,
    )
    return from_tiles(pressure), from_tiles(residual)


def solution(mesh):
    split = P("slab", "box", None)
    return jax.shard_map(body, mesh=mesh, in_specs=(split,) * 3, out_specs=(split,) * 2, check_vma=False)
```

```python
import functools

import jax
import jax.numpy as jnp
from jax import lax
from jax.experimental import pallas as pl
from jax.experimental.pallas import tpu as pltpu
from jax.sharding import PartitionSpec as P

ITERS = 8
F32 = jnp.float32
BF16 = jnp.bfloat16

H0 = 5
H1 = 12
N0 = 32 + 2 * H0
N1 = 16 + 2 * (H1 + 1)
N2 = 24
ROWS = 24
EDGE = H0 * ROWS
SWEEP, FACES, RESTRICT, MERGE, FINISH = 99, 99, 16, 16, 99
SEND1 = H1 + (H1 + 1) + 4
SEND2 = 16 + 2 * H0


def matmul(x, m):
    high = x.astype(BF16)
    rest = x - high.astype(F32)
    mid = rest.astype(BF16)
    low = (rest - mid.astype(F32)).astype(BF16)
    dot = functools.partial(jnp.dot, preferred_element_type=F32)
    return dot(high, m) + (dot(mid, m) + dot(low, m))


def one_hot(shape, rule):
    i = lax.broadcasted_iota(jnp.int32, shape, 0)
    j = lax.broadcasted_iota(jnp.int32, shape, 1)
    return rule(i, j).astype(F32).astype(BF16)


def iota(shape, axis):
    return lax.broadcasted_iota(jnp.int32, shape, axis)


def up(v, axis):
    return pltpu.roll(v, v.shape[axis] - 1, axis)


def down(v, axis):
    return pltpu.roll(v, 1, axis)


def planes(first, last, unroll, step, carry=0):
    def pair(k, carry):
        i = first + 2 * k
        return step(i + 1, (first + 1) % 2, step(i, first % 2, carry))

    count = (last - first) // 2
    if unroll < count:
        return lax.fori_loop(0, count, pair, carry, unroll=unroll)
    for k in range(count):
        carry = pair(k, carry)
    return carry


def my_place():
    return lax.axis_index("slab"), lax.axis_index("box")


def slab_rows(x, half, odd):
    return pl.ds((x // 8) * 16 + half * 8 + x % 8 + 64 * odd, 4, stride=128)


def pack_plane(g, r, c, x, rows, even_y, out, base):
    p0 = even_y if x % 2 == 0 else jnp.logical_not(even_y)
    for half in range(2):
        lanes = slice(128 * half, 128 * half + 128)
        even, odd = rows(half, 0), rows(half, 1)
        out[base : base + 4, lanes] = c[even, :]
        out[base + 4 : base + 8, lanes] = c[odd, :]
        fe, fo = r[even, :], r[odd, :]
        out[base + 8 : base + 12, lanes] = jnp.where(p0, fe, fo)
        out[base + 12 : base + 16, lanes] = jnp.where(p0, fo, fe)
        out[base + 16 : base + 20, lanes] = jnp.where(p0, g[odd, :], g[even, :])
        out[base + 20 : base + 24, lanes] = jnp.zeros((4, 128), F32)


def pack_kernel(g, r, c, low, high):
    even_y = (iota((4, 128), 1) & 1) == 0
    for x in range(32):
        out, base = (low, x * ROWS) if x < 16 else (high, (x - 16) * ROWS)
        pack_plane(g, r, c, x, functools.partial(slab_rows, x), even_y, out, base)


def edge_kernel(g_hbm, r_hbm, c_hbm, first, second, *scratch):
    left, right, sem = scratch[0:3], scratch[3:6], scratch[6]
    copies = []
    for k, source in enumerate((g_hbm, r_hbm, c_hbm)):
        for side, (target, at) in enumerate(((left[k], 0), (right[k], 48))):
            copies.append(
                pltpu.make_async_copy(source.at[:, at : at + 16, :], target.reshape(8, 16, 128), sem.at[2 * k + side])
            )
    for copy in copies:
        copy.start()
    for copy in copies:
        copy.wait()
    even_y = (iota((4, 128), 1) & 1) == 0

    def pack(parts, start, out):
        for k in range(H0):
            x = start + k
            rows = lambda half, odd, x=x: pl.ds(half * 8 + x % 8 + 16 * odd, 4, stride=32)
            pack_plane(*parts, x, rows, even_y, out, k * ROWS)

    right_first = (my_place()[1] & 1) == 1

    @pl.when(right_first)
    def _():
        pack(right, 32 - H0, first)
        pack(left, 0, second)

    @pl.when(jnp.logical_not(right_first))
    def _():
        pack(left, 0, first)
        pack(right, 32 - H0, second)


def parity(odd):
    return ((iota((8, 256), 1) + odd + 1) & 1) == 0


def nsum_packed(lv, v, xa, xb, ya, yb, i, p):
    here = v[i]
    t = xa[i] * v[i + 1] + xb[i - 1] * v[i - 1]
    t = t + (ya[i] * up(here, 1) + down(yb[i] * here, 1))
    cross = lv["c"][i]
    z = jnp.where(p, down(cross * here, 0), cross * up(here, 0))
    return t + (lv["s"][i] * here + z)


def sweep_packed(lv, red, first, last):
    def step(i, odd, carry):
        p = parity(odd)
        if red:
            n = nsum_packed(lv, lv["vB"], lv["xR"], lv["xB"], lv["yR"], lv["yB"], i, p)
            lv["vR"][i] = (lv["fR"][i] + n) * lv["iR"][i]
        else:
            p = jnp.logical_not(p)
            n = nsum_packed(lv, lv["vR"], lv["xB"], lv["xR"], lv["yB"], lv["yR"], i, p)
            lv["vB"][i] = (lv["fB"][i] + n) * lv["iB"][i]
        return carry

    planes(first, last, SWEEP, step)


def residual_packed(lv, i, odd):
    p = parity(odd)
    n = nsum_packed(lv, lv["vB"], lv["xR"], lv["xB"], lv["yR"], lv["yB"], i, p)
    r_red = lv["fR"][i] - (lv["cR"][i] * lv["vR"][i] - n)
    q = jnp.logical_not(p)
    n = nsum_packed(lv, lv["vR"], lv["xB"], lv["xR"], lv["yB"], lv["yR"], i, q)
    r_black = lv["fB"][i] - (lv["cB"][i] * lv["vB"][i] - n)
    return r_red, r_black, p


PACKED = ("vB", "fR", "fB", "xR", "xB", "yR", "yB", "s", "c", "iR", "iB", "cR", "cB")


def fine_kernel(boxes, lo, hi, halo, *refs):
    outs = dict(zip(PACKED, refs))
    own, first, second, bottom = refs[len(PACKED) : len(PACKED) + 4]
    vR, bE, bO, pair_r, pair_b, tmp = refs[len(PACKED) + 4 :]
    lv = dict(outs, vR=vR)
    box = my_place()[1]
    odd = box & 1
    row, lane = iota((8, 256), 0), iota((8, 256), 1)
    low_half = row < 4

    def merge(part0, part1, count, first):
        def step(k, carry):
            base = pl.multiple_of(k * ROWS, 8) if not isinstance(k, int) else k * ROWS
            i = first + k
            for at, (low, high) in enumerate(((bE, bO), (lv["fR"], lv["fB"]), (lv["vB"], None))):
                a, b = part0[pl.ds(base + 8 * at, 8), :], part1[pl.ds(base + 8 * at, 8), :]
                low[i] = jnp.where(low_half, a, pltpu.roll(b, 4, 0))
                if high is not None:
                    high[i] = jnp.where(low_half, pltpu.roll(a, 4, 0), b)
            return carry

        lax.fori_loop(0, count, step, 0, unroll=min(count, MERGE))

    merge(halo.at[0, odd], halo.at[1, odd], H0, 0)
    merge(lo.at[0], lo.at[1], 16, H0)
    merge(hi.at[0], hi.at[1], 16, H0 + 16)
    merge(halo.at[0, 1 - odd], halo.at[1, 1 - odd], H0, H0 + 32)

    top, bot = row == 7, row == 0
    end, begin = lane == 255, lane == 0

    def x_faces(i, p):
        fxe, fxo = 0.5 * (bE[i] + bE[i + 1]), 0.5 * (bO[i] + bO[i + 1])
        lv["xR"][i] = jnp.where(p, fxe, fxo)
        lv["xB"][i] = jnp.where(p, fxo, fxe)
        return fxe, fxo

    def faces(i, odd, before):
        p = parity(odd)
        e, o = bE[i], bO[i]
        fxe, fxo = x_faces(i, p)
        fye = 0.5 * (e + jnp.where(end, 0.0, up(e, 1)))
        fyo = 0.5 * (o + jnp.where(end, 0.0, up(o, 1)))
        gye = 0.5 * (e + jnp.where(begin, 0.0, down(e, 1)))
        gyo = 0.5 * (o + jnp.where(begin, 0.0, down(o, 1)))
        yr, yb = jnp.where(p, fye, fyo), jnp.where(p, fyo, fye)
        lv["yR"][i] = jnp.where(end, 0.0, yr)
        lv["yB"][i] = jnp.where(end, 0.0, yb)
        s = 0.5 * (e + o)
        above = 0.5 * (o + jnp.where(top, 0.0, up(e, 0)))
        below = 0.5 * (e + jnp.where(bot, 0.0, down(o, 0)))
        lv["s"][i] = s
        lv["c"][i] = jnp.where(top, 0.0, above)
        ce = fye + gye + (s + below) + (fxe + before[0])
        co = fyo + gyo + (s + above) + (fxo + before[1])
        cr, cb = jnp.where(p, ce, co), jnp.where(p, co, ce)
        lv["cR"][i] = cr
        lv["cB"][i] = cb
        x = box * 32 - H0 + i
        inside = jnp.logical_and(x >= 0, x < boxes * 32)
        lv["iR"][i] = jnp.where(inside, 1.0 / cr, 0.0)
        lv["iB"][i] = jnp.where(inside, 1.0 / cb, 0.0)
        return fxe, fxo

    planes(1, N0 - 1, FACES, faces, x_faces(0, parity(0)))

    for k in range(2):
        sweep_packed(lv, True, 1 + 2 * k, N0 - 1 - 2 * k)
        sweep_packed(lv, False, 2 + 2 * k, N0 - 2 - 2 * k)

    def restrict(j, carry):
        i = H0 + 2 * j
        a, b, _ = residual_packed(lv, i, H0 % 2)
        c, d, _ = residual_packed(lv, i + 1, (H0 + 1) % 2)
        pair_r[j] = (a + b) + (c + d)
        pair_b[j] = (bE[i] + bO[i]) + (bE[i + 1] + bO[i + 1])
        return carry

    lax.fori_loop(0, 16, restrict, 0, unroll=RESTRICT)

    halve = one_hot((256, 128), lambda i, j: (i >> 1) == j)
    f1 = 0.125 * matmul(pair_r[...].reshape(128, 256), halve)
    b1 = 0.125 * matmul(pair_b[...].reshape(128, 256), halve)
    own[0:16] = f1.reshape(16, 8, 128)
    own[16:32] = b1.reshape(16, 8, 128)

    for k in range(8):
        tmp[8 * k : 8 * k + 8, :] = own[16 + 2 * k] + own[17 + 2 * k]
    summed = tmp[pl.ds(0, 32, stride=2), :] + tmp[pl.ds(1, 32, stride=2), :]
    halve = one_hot((128, 128), lambda i, j: (i >> 1) == j)
    own[32:36] = (0.125 * matmul(summed, halve)).reshape(4, 8, 128)
    bottom[...] = bottom_row([own[32 + k] + pltpu.roll(own[32 + k], 4, 0) for k in range(4)])

    for out, right in ((first, odd), (second, 1 - odd)):
        out[0:H1] = own[pl.ds(right * (16 - H1), H1)]
        out[H1 : 2 * H1 + 1] = own[pl.ds(16 + right * (15 - H1), H1 + 1)]
        out[2 * H1 + 1 :] = own[32:36]


def bottom_row(pairs):
    total = None
    for k, plane in enumerate(pairs):
        spread = one_hot((128, 128), lambda i, j, k=k: jnp.logical_and((i >> 1) + 32 * k == j, i < 64))
        part = matmul(plane, spread)
        total = part if total is None else total + part
    low, high = total[0:1] + total[1:2], total[2:3] + total[3:4]
    row = 0.125 * jnp.where(my_place()[0] == 0, low, high)
    return jnp.broadcast_to(row, (8, 128))


def level_faces(b, ax, ay, az, inv, n, factor, depth, width, inside):
    row, lane = iota((8, 128), 0), iota((8, 128), 1)
    top, bot = row == depth - 1, row == 0
    end, begin = lane == width - 1, lane == 0
    cell = jnp.logical_and(row < depth, lane < width)
    ax[0] = factor * (b[0] + b[1])

    def step(i, odd, before):
        v = b[i]
        fx = factor * (v + b[i + 1])
        ax[i] = fx
        fy = factor * (v + jnp.where(end, 0.0, up(v, 1)))
        gy = factor * (v + jnp.where(begin, 0.0, down(v, 1)))
        fz = factor * (v + jnp.where(top, 0.0, up(v, 0)))
        gz = factor * (v + jnp.where(bot, 0.0, down(v, 0)))
        ay[i] = jnp.where(end, 0.0, fy)
        az[i] = jnp.where(top, 0.0, fz)
        center = (fz + gz) + (fx + before) + (fy + gy)
        inv[i] = jnp.where(jnp.logical_and(cell, inside(i)), 1.0 / center, 0.0)
        return fx

    planes(1, n - 1, 99, step, ax[0])


def nsum_plain(v, ax, ay, az, i):
    here = v[i]
    t = ax[i] * v[i + 1] + ax[i - 1] * v[i - 1]
    t = t + (ay[i] * up(here, 1) + down(ay[i] * here, 1))
    return t + (az[i] * up(here, 0) + down(az[i] * here, 0))


def colour(odd):
    return ((iota((8, 128), 0) + iota((8, 128), 1) + odd) & 1) == 0


def sweep_plain(v, f, ax, ay, az, inv, odd, shift, first, last):
    def step(i, plane_odd, carry):
        cells = colour((plane_odd + shift + odd) % 2)
        v[i] = jnp.where(cells, (f[i] + nsum_plain(v, ax, ay, az, i)) * inv[i], v[i])
        return carry

    planes(first, last, 99, step)


def first_plain(v, f, inv, shift, first, last):
    def step(i, plane_odd, carry):
        v[i] = jnp.where(colour((plane_odd + shift) % 2), f[i] * inv[i], 0.0)
        return carry

    planes(first, last, 99, step)


def residual_plain(v, f, ax, ay, az, center, i):
    return f[i] - (center * v[i] - nsum_plain(v, ax, ay, az, i))


def center_plain(b, ax, i, factor, depth, width):
    row, lane = iota((8, 128), 0), iota((8, 128), 1)
    v = b[i]
    fy = jnp.where(lane == width - 1, 0.0, up(v, 1)) + jnp.where(lane == 0, 0.0, down(v, 1))
    fz = jnp.where(row == depth - 1, 0.0, up(v, 0)) + jnp.where(row == 0, 0.0, down(v, 0))
    return factor * (4.0 * v + fy + fz) + (ax[i] + ax[i - 1])


def middle_kernel(boxes, own, first, second, bottom, v1, f1, ax1, ay1, az1, inv1, ax2, ay2, az2, inv2, send, message, v2, f2, b2, b1, tmp):
    box = my_place()[1]
    w = H1 + 1
    swapped = (box & 1) == 1

    def received(k, count):
        one, two = first[k : k + count], second[k : k + count]
        return jnp.where(swapped, two, one), jnp.where(swapped, one, two)

    left, right = received(H1, w)
    b1[0:w] = left
    b1[w : w + 16] = own[16:32]
    b1[w + 16 :] = right
    left, right = received(0, H1)
    f1[0:1] = jnp.zeros((1, 8, 128), F32)
    f1[1 : 1 + H1] = left
    f1[w : w + 16] = own[0:16]
    f1[w + 16 : w + 16 + H1] = right
    f1[N1 - 1 :] = jnp.zeros((1, 8, 128), F32)
    left, right = received(H1 + w, 4)
    b2[...] = jnp.zeros(b2.shape, F32)
    for at, part in ((0, left), (8, own[32:36]), (16, right)):
        for k in range(8):
            b2[at + k, 0:4, :] = part[k // 2, 4 * (k % 2) : 4 * (k % 2) + 4]
    v1[...] = jnp.zeros(v1.shape, F32)
    v2[...] = jnp.zeros(v2.shape, F32)
    f2[...] = jnp.zeros(f2.shape, F32)

    def within(size, width):
        def inside(i):
            x = box * size - width + i
            return jnp.logical_and(x >= 0, x < boxes * size)

        return inside

    k1, k2 = 0.5 * 0.25, 0.5 * 0.25**2
    level_faces(b1, ax1, ay1, az1, inv1, N1, k1, 8, 128, within(16, w))
    level_faces(b2, ax2, ay2, az2, inv2, N2, k2, 4, 64, within(8, 8))

    one = (f1, ax1, ay1, az1, inv1)
    first_plain(v1, f1, inv1, 1, 1, N1 - 1)
    sweep_plain(v1, *one, 1, 1, 2, N1 - 2)
    sweep_plain(v1, *one, 0, 1, 3, N1 - 3)
    sweep_plain(v1, *one, 1, 1, 4, N1 - 4)

    def restrict(j, carry):
        i = 5 + 2 * j
        parts = [residual_plain(v1, *one[:4], center_plain(b1, ax1, k, k1, 8, 128), k) for k in (i, i + 1)]
        tmp[8 * j : 8 * j + 8, :] = parts[0] + parts[1]
        return carry

    for j in range(16):
        restrict(j, 0)
    summed = tmp[pl.ds(0, 64, stride=2), :] + tmp[pl.ds(1, 64, stride=2), :]
    coarse = 0.125 * matmul(summed, one_hot((128, 128), lambda i, j: (i >> 1) == j))
    for j in range(16):
        f2[4 + j, 0:4, :] = coarse[4 * j : 4 * j + 4]

    two = (f2, ax2, ay2, az2, inv2)
    first_plain(v2, f2, inv2, 0, 4, 20)
    sweep_plain(v2, *two, 1, 0, 5, 19)
    sweep_plain(v2, *two, 0, 0, 6, 18)
    sweep_plain(v2, *two, 1, 0, 7, 17)
    send[0:8] = v2[8:16]
    send[8:16] = f2[8:16]

    pairs = []
    for k in range(4):
        parts = [
            residual_plain(v2, *two[:4], center_plain(b2, ax2, i, k2, 4, 64), i)
            for i in (8 + 2 * k, 9 + 2 * k)
        ]
        pairs.append(parts[0] + parts[1])
    source = bottom_row(pairs)
    rows = jnp.where((iota((8, 128), 0) & 1) == 0, source, bottom[...])
    for k in range(message.shape[0] // 8):
        message[8 * k : 8 * k + 8, :] = rows


def coarse_solve(n, source, coefficient, dref, qref, eref):
    row, lane = iota((n, 128), 0), iota((n, 128), 1)
    factor = 0.5 * 0.25**3
    last = jnp.logical_and(row == n - 1, lane >= 96)
    first = jnp.logical_and(row == 0, lane < 32)
    inner_hi, inner_lo = lane < 96, lane >= 32
    end, begin = (lane & 31) == 31, (lane & 31) == 0

    def xp(v):
        a = pltpu.roll(v, 96, 1)
        return jnp.where(inner_hi, a, up(a, 0))

    def xm(v):
        a = pltpu.roll(v, 32, 1)
        return jnp.where(inner_lo, a, down(a, 0))

    ax, ay, center = [], [], []
    az = factor * (coefficient[0] + coefficient[1])
    for b in coefficient:
        fx = factor * (b + jnp.where(last, 0.0, xp(b)))
        gx = factor * (b + jnp.where(first, 0.0, xm(b)))
        fy = factor * (b + jnp.where(end, 0.0, up(b, 1)))
        gy = factor * (b + jnp.where(begin, 0.0, down(b, 1)))
        ax.append(jnp.where(last, 0.0, fx))
        ay.append(jnp.where(end, 0.0, fy))
        center.append((factor * b + az) + (fx + gx) + (fy + gy))

    def total(u, w):
        s = u[0] * w[0] + u[1] * w[1]
        return jnp.sum(jnp.sum(s, axis=0, keepdims=True), axis=1, keepdims=True)

    for t in range(2):
        dref[t] = source[t]
        qref[t] = source[t]
        eref[t, 8 : 8 + n] = jnp.zeros((n, 128), F32)
        eref[t, 0:8] = jnp.zeros((8, 128), F32)
        eref[t, 8 + n :] = jnp.zeros((8, 128), F32)

    def iterate(k, now):
        d = (dref[0], dref[1])
        w = []
        for t in range(2):
            v = d[t]
            s = ax[t] * xp(v) + xm(ax[t] * v)
            s = s + (ay[t] * up(v, 1) + down(ay[t] * v, 1))
            w.append(center[t] * v - (s + az * d[1 - t]))
        alpha = now / total(d, w)
        q = []
        for t in range(2):
            eref[t, 8 : 8 + n] = eref[t, 8 : 8 + n] + alpha * d[t]
            q.append(qref[t] - alpha * w[t])
            qref[t] = q[t]
        later = total(q, q)
        beta = later / now
        for t in range(2):
            dref[t] = q[t] + beta * d[t]
        return later

    lax.fori_loop(0, ITERS, iterate, total(source, source))


def coarse_kernel(boxes, gathered, e2, dref, qref, eref):
    box = my_place()[1]
    source = [gathered[t, pl.ds(0, boxes, stride=2), :] for t in range(2)]
    coefficient = [gathered[t, pl.ds(1, boxes, stride=2), :] for t in range(2)]
    coarse_solve(boxes, source, coefficient, dref, qref, eref)
    near = [eref[t, pl.ds(7 + box, 8), :] for t in range(2)]
    spread = one_hot((128, 512), lambda i, j: jnp.logical_and(((j >> 7) * 32) + ((j & 127) >> 1) == i, (j & 127) < 64))
    fine = [matmul(e, spread) for e in near]
    row = iota((8, 128), 0)
    for i in range(N2):
        cell, k = (i // 2) // 4, (i // 2) % 4
        low, high = (f[cell : cell + 1, 128 * k : 128 * k + 128] for f in fine)
        e2[i] = jnp.where(row < 2, low, jnp.where(row < 4, high, 0.0))


def after_kernel(send, black, gathered, first, second):
    del gathered
    odd = my_place()[1] & 1
    for out, right in ((first, odd), (second, 1 - odd)):
        out[0:16] = send[...]
        start = H0 + right * (32 - H0)
        for k in range(H0):
            for half in range(2):
                out[16 + 2 * k + half] = black[start + k, :, 128 * half : 128 * half + 128]


def last_kernel(*refs):
    names = ("e2", "first", "second", "own2", "v1", "f1", "ax1", "ay1", "az1", "inv1", "ax2", "ay2", "az2", "inv2")
    given = dict(zip(names, refs))
    refs = refs[len(names) :]
    level0 = dict(zip(PACKED, refs))
    refs = refs[len(PACKED) :]
    out_v, out_r, vR, vB, v1, v2, f2, wide, e0 = refs
    slab, box = my_place()
    e2, first, second, own2 = given["e2"], given["first"], given["second"], given["own2"]
    swapped = (box & 1) == 1

    def received(side, k, count):
        one, two = (first, second) if side == 0 else (second, first)
        return jnp.where(swapped, two[k : k + count], one[k : k + count])

    for ref, part in ((v2, 0), (f2, 8)):
        ref[0:8] = received(0, part, 8)
        ref[8:16] = own2[part : part + 8]
        ref[16:24] = received(1, part, 8)
    for i in range(N2):
        v2[i] = v2[i] + e2[i]
    two = (f2, given["ax2"], given["ay2"], given["az2"], given["inv2"])
    for k in range(2):
        sweep_plain(v2, *two, 0, 0, 1 + 2 * k, N2 - 1 - 2 * k)
        sweep_plain(v2, *two, 1, 0, 2 + 2 * k, N2 - 2 - 2 * k)

    packed = jnp.concatenate([v2[4 + j, 0:4, :] for j in range(16)], axis=0)
    fine = matmul(packed, one_hot((128, 128), lambda i, j: (j >> 1) == i))
    wide[pl.ds(0, 64, stride=2), :] = fine
    wide[pl.ds(1, 64, stride=2), :] = fine
    for i in range(6, N1 - 6):
        j = (i + 3) // 2 - 4
        v1[i] = given["v1"][i] + wide[8 * j : 8 * j + 8, :]
    one = (given["f1"], given["ax1"], given["ay1"], given["az1"], given["inv1"])
    for k in range(2):
        sweep_plain(v1, *one, 0, 1, 7 + 2 * k, N1 - 7 - 2 * k)
        sweep_plain(v1, *one, 1, 1, 8 + 2 * k, N1 - 8 - 2 * k)

    double = one_hot((128, 256), lambda i, j: (j >> 1) == i)
    e0[...] = matmul(v1[10:32].reshape(176, 128), double).reshape(22, 8, 256)
    lv = dict(level0, vR=vR, vB=vB)

    black = level0["vB"]

    def correct(j, carry):
        e = e0[j]
        vB[2 * j - 1] = black[2 * j - 1] + e
        vB[2 * j] = black[2 * j] + e
        return carry

    lax.fori_loop(3, 19, correct, 0, unroll=4)
    for side, at in ((0, 0), (1, H0 + 32)):
        for k in range(H0):
            for half in range(2):
                lanes = slice(128 * half, 128 * half + 128)
                vB[at + k, :, lanes] = received(side, 16 + 2 * k + half, 1)[0] + e0[(at + k + 1) // 2, :, lanes]
    for k in range(2):
        sweep_packed(lv, True, 1 + 2 * k, N0 - 1 - 2 * k)
        sweep_packed(lv, False, 2 + 2 * k, N0 - 2 - 2 * k)


    def finish(i, odd, carry):
        x = i - H0
        red, black, p = residual_packed(lv, i, odd)
        for out, a, b in ((out_v, vR[i], vB[i]), (out_r, red, black)):
            for at, whole in ((0, jnp.where(p, a, b)), (1, jnp.where(p, b, a))):
                part = jnp.where(slab == 0, whole[0:4], whole[4:8])
                for half in range(2):
                    out[slab_rows(x, half, at), :] = part[:, 128 * half : 128 * half + 128]
        return carry

    planes(H0, H0 + 32, FINISH, finish)


def call(kernel, outs, scratch, *args, limit=12):
    vmem = pl.BlockSpec(memory_space=pltpu.VMEM)
    return pl.pallas_call(
        kernel,
        out_shape=[jax.ShapeDtypeStruct(s, F32) for s in outs],
        in_specs=[vmem] * len(args),
        out_specs=[vmem] * len(outs),
        scratch_shapes=[pltpu.VMEM(s, F32) for s in scratch],
        compiler_params=pltpu.CompilerParams(vmem_limit_bytes=limit * 1024 * 1024),
    )(*args)


def edges(*args):
    return pl.pallas_call(
        edge_kernel,
        out_shape=[jax.ShapeDtypeStruct((EDGE, 256), F32)] * 2,
        in_specs=[pl.BlockSpec(memory_space=pl.ANY)] * 3,
        out_specs=[pl.BlockSpec(memory_space=pltpu.VMEM)] * 2,
        scratch_shapes=[pltpu.VMEM((128, 128), F32)] * 6 + [pltpu.SemaphoreType.DMA((6,))],
        compiler_params=pltpu.CompilerParams(vmem_limit_bytes=60 * 1024 * 1024),
    )(*[a.reshape(8, 64, 128) for a in args])


def by_tiles(a):
    return a.reshape(8, 4, 8, 2, 128).transpose(0, 1, 3, 2, 4).reshape(512, 128)


def from_tiles(a):
    return a.reshape(8, 4, 2, 8, 128).transpose(0, 1, 3, 2, 4).reshape(8, 32, 256)


def exchange(first, second):
    boxes = lax.axis_size("box")
    odd = [(i, i + 1) for i in range(1, boxes - 1, 2)]
    even = [(i, i + 1) for i in range(0, boxes - 1, 2)]
    return [lax.ppermute(x, "box", p + [(j, i) for i, j in p]) for x, p in ((first, odd), (second, even))]


def body(pressure_guess, right_side, coefficient):
    boxes = lax.axis_size("box")
    flat = [by_tiles(a) for a in (pressure_guess, right_side, coefficient)]
    first, second = edges(*flat)
    low, high = call(pack_kernel, [(16 * ROWS, 256)] * 2, [], *flat)
    first, second = exchange(first, second)
    low, high = lax.all_gather(low, "slab"), lax.all_gather(high, "slab")
    halo = lax.all_gather(jnp.stack([first, second]), "slab")

    plane = (N0, 8, 256)
    fine = call(
        functools.partial(fine_kernel, boxes),
        [plane] * len(PACKED) + [(36, 8, 128), (SEND1, 8, 128), (SEND1, 8, 128), (8, 128)],
        [plane] * 3 + [(16, 8, 256)] * 2 + [(64, 128)],
        low,
        high,
        halo,
    )
    level0 = fine[: len(PACKED)]
    own, first, second, bottom = fine[len(PACKED) :]
    first, second = exchange(first, second)

    one, two = (N1, 8, 128), (N2, 8, 128)
    *levels, send, message = call(
        functools.partial(middle_kernel, boxes),
        [one] * 6 + [two] * 4 + [(16, 8, 128), (2 * boxes, 128)],
        [two] * 3 + [one, (128, 128)],
        own,
        first,
        second,
        bottom,
    )
    spread = lax.all_to_all(message.reshape(boxes, 2, 128), "box", 0, 0).reshape(2 * boxes, 128)
    first, second = exchange(*call(after_kernel, [(SEND2, 8, 128)] * 2, [], send, level0[0], spread))
    gathered = lax.all_gather(spread, "slab")
    (e2,) = call(
        functools.partial(coarse_kernel, boxes),
        [two],
        [(2, boxes, 128), (2, boxes, 128), (2, boxes + 16, 128)],
        gathered,
    )
    pressure, residual = call(
        last_kernel,
        [(512, 128)] * 2,
        [plane, plane, one, two, two, (128, 128), (22, 8, 256)],
        e2,
        first,
        second,
        send,
        *levels,
        *level0,
    )
    return from_tiles(pressure), from_tiles(residual)


def solution(mesh):
    split = P("slab", "box", None)
    return jax.shard_map(body, mesh=mesh, in_specs=(split,) * 3, out_specs=(split,) * 2, check_vma=False)
```

```python
import functools

import jax
import jax.numpy as jnp
from jax import lax
from jax.experimental import pallas as pl
from jax.experimental.pallas import tpu as pltpu
from jax.sharding import PartitionSpec as P

ITERS = 8
F32 = jnp.float32
BF16 = jnp.bfloat16

H0 = 5
H1 = 12
N0 = 32 + 2 * H0
N1 = 16 + 2 * (H1 + 1)
N2 = 24
ROWS = 20
EDGE = 96
EDGE_F, EDGE_V = 8 * H0, 16 * H0 - 8
SWEEP, FACES, RESTRICT, FINISH = 99, 99, 16, 99
SEND1 = H1 + (H1 + 1) + 4
SEND2 = 4 + 2 * H0


def matmul(x, m):
    high = x.astype(BF16)
    rest = x - high.astype(F32)
    mid = rest.astype(BF16)
    low = (rest - mid.astype(F32)).astype(BF16)
    dot = functools.partial(jnp.dot, preferred_element_type=F32)
    return dot(high, m) + (dot(mid, m) + dot(low, m))


def one_hot(shape, rule):
    i = lax.broadcasted_iota(jnp.int32, shape, 0)
    j = lax.broadcasted_iota(jnp.int32, shape, 1)
    return rule(i, j).astype(F32).astype(BF16)


def iota(shape, axis):
    return lax.broadcasted_iota(jnp.int32, shape, axis)


def up(v, axis):
    return pltpu.roll(v, v.shape[axis] - 1, axis)


def down(v, axis):
    return pltpu.roll(v, 1, axis)


def planes(first, last, unroll, step, carry=0):
    def pair(k, carry):
        i = first + 2 * k
        return step(i + 1, (first + 1) % 2, step(i, first % 2, carry))

    count = (last - first) // 2
    if unroll < count:
        return lax.fori_loop(0, count, pair, carry, unroll=unroll)
    for k in range(count):
        carry = pair(k, carry)
    return carry


def my_place():
    return lax.axis_index("slab"), lax.axis_index("box")


def slab_rows(x, half, odd):
    return pl.ds((x // 8) * 16 + half * 8 + x % 8 + 64 * odd, 4, stride=128)


def pack_plane(g, r, c, x, rows, even_y, out, b_at, f_at, v_at):
    p0 = even_y if x % 2 == 0 else jnp.logical_not(even_y)
    for half in range(2):
        lanes = slice(128 * half, 128 * half + 128)
        even, odd = rows(half, 0), rows(half, 1)
        out[b_at : b_at + 4, lanes] = c[even, :]
        out[b_at + 4 : b_at + 8, lanes] = c[odd, :]
        if f_at is not None:
            fe, fo = r[even, :], r[odd, :]
            out[f_at : f_at + 4, lanes] = jnp.where(p0, fe, fo)
            out[f_at + 4 : f_at + 8, lanes] = jnp.where(p0, fo, fe)
        out[v_at : v_at + 4, lanes] = jnp.where(p0, g[odd, :], g[even, :])


def pack_edge(parts, right, rows, even_y, out):
    for k in range(H0):
        x = 32 - H0 + k if right else k
        f_at = k - 1 if right else k
        f_at = EDGE_F + 8 * f_at if 0 <= f_at < H0 - 1 else None
        pack_plane(*parts, x, functools.partial(rows, x), even_y, out, 8 * k, f_at, EDGE_V + 4 * k)
    out[EDGE_V + 4 * H0 :, :] = jnp.zeros((EDGE - EDGE_V - 4 * H0, 256), F32)


def pack_kernel(g, r, c, low, high, second):
    even_y = (iota((4, 128), 1) & 1) == 0
    swapped = (my_place()[1] & 1) == 1

    @pl.when(swapped)
    def _():
        pack_edge((g, r, c), False, slab_rows, even_y, second)

    @pl.when(jnp.logical_not(swapped))
    def _():
        pack_edge((g, r, c), True, slab_rows, even_y, second)

    for x in range(32):
        out, base = (low, x * ROWS) if x < 16 else (high, (x - 16) * ROWS)
        pack_plane(g, r, c, x, functools.partial(slab_rows, x), even_y, out, base, base + 8, base + 16)


def edge_kernel(g_hbm, r_hbm, c_hbm, first, *scratch):
    parts, sem = scratch[0:3], scratch[3]
    odd = my_place()[1] & 1
    at = pl.multiple_of(48 * odd, 16)
    copies = [
        pltpu.make_async_copy(source.at[:, pl.ds(at, 16), :], target.reshape(8, 16, 128), sem.at[k])
        for k, (source, target) in enumerate(zip((g_hbm, r_hbm, c_hbm), parts))
    ]
    for copy in copies:
        copy.start()
    for copy in copies:
        copy.wait()
    even_y = (iota((4, 128), 1) & 1) == 0

    def rows(x, half, second_z):
        return pl.ds(half * 8 + x % 8 + 16 * second_z, 4, stride=32)

    @pl.when(odd == 1)
    def _():
        pack_edge(parts, True, rows, even_y, first)

    @pl.when(odd == 0)
    def _():
        pack_edge(parts, False, rows, even_y, first)


def parity(odd):
    return ((iota((8, 256), 1) + odd + 1) & 1) == 0


def nsum_packed(lv, v, xa, xb, ya, yb, i, p):
    here = v[i]
    t = xa[i] * v[i + 1] + xb[i - 1] * v[i - 1]
    t = t + (ya[i] * up(here, 1) + down(yb[i] * here, 1))
    cross = lv["c"][i]
    z = jnp.where(p, down(cross * here, 0), cross * up(here, 0))
    return t + (lv["s"][i] * here + z)


def sweep_packed(lv, red, first, last):
    def step(i, odd, carry):
        p = parity(odd)
        if red:
            n = nsum_packed(lv, lv["vB"], lv["xR"], lv["xB"], lv["yR"], lv["yB"], i, p)
            lv["vR"][i] = (lv["fR"][i] + n) * lv["iR"][i]
        else:
            p = jnp.logical_not(p)
            n = nsum_packed(lv, lv["vR"], lv["xB"], lv["xR"], lv["yB"], lv["yR"], i, p)
            lv["vB"][i] = (lv["fB"][i] + n) * lv["iB"][i]
        return carry

    planes(first, last, SWEEP, step)


def residual_packed(lv, i, odd):
    p = parity(odd)
    n = nsum_packed(lv, lv["vB"], lv["xR"], lv["xB"], lv["yR"], lv["yB"], i, p)
    r_red = lv["fR"][i] - (lv["cR"][i] * lv["vR"][i] - n)
    q = jnp.logical_not(p)
    n = nsum_packed(lv, lv["vR"], lv["xB"], lv["xR"], lv["yB"], lv["yR"], i, q)
    r_black = lv["fB"][i] - (lv["cB"][i] * lv["vB"][i] - n)
    return r_red, r_black, p


PACKED = ("vB", "fR", "fB", "xR", "xB", "yR", "yB", "s", "c", "iR", "iB", "cR", "cB")


def fine_kernel(boxes, lo, hi, halo, *refs):
    outs = dict(zip(PACKED, refs))
    own, first, second, bottom = refs[len(PACKED) : len(PACKED) + 4]
    vR, bE, bO, pair_r, pair_b, tmp = refs[len(PACKED) + 4 :]
    lv = dict(outs, vR=vR)
    box = my_place()[1]
    odd = box & 1
    row, lane = iota((8, 256), 0), iota((8, 256), 1)
    low_half = row < 4

    def merge(parts, at, i, low, high):
        a, b = (part[at : at + 8, :] for part in parts)
        low[i] = jnp.where(low_half, a, pltpu.roll(b, 4, 0))
        high[i] = jnp.where(low_half, pltpu.roll(a, 4, 0), b)

    def stack(parts, at, i, out):
        for t in range(2):
            out[i, 4 * t : 4 * t + 4, :] = parts[t][at : at + 4, :]

    for x in range(32):
        source, base = (lo, x * ROWS) if x < 16 else (hi, (x - 16) * ROWS)
        parts = source.at[0], source.at[1]
        merge(parts, base, H0 + x, bE, bO)
        merge(parts, base + 8, H0 + x, lv["fR"], lv["fB"])
        stack(parts, base + 16, H0 + x, lv["vB"])
    for side, at in ((odd, 0), (1 - odd, H0 + 32)):
        parts = halo.at[0, side], halo.at[1, side]
        for k in range(H0):
            merge(parts, 8 * k, at + k, bE, bO)
            stack(parts, EDGE_V + 4 * k, at + k, lv["vB"])
        for k in range(H0 - 1):
            merge(parts, EDGE_F + 8 * k, (1 if at == 0 else at) + k, lv["fR"], lv["fB"])

    top, bot = row == 7, row == 0
    end, begin = lane == 255, lane == 0

    def x_faces(i, p):
        fxe, fxo = 0.5 * (bE[i] + bE[i + 1]), 0.5 * (bO[i] + bO[i + 1])
        lv["xR"][i] = jnp.where(p, fxe, fxo)
        lv["xB"][i] = jnp.where(p, fxo, fxe)
        return fxe, fxo

    def faces(i, odd, before):
        p = parity(odd)
        e, o = bE[i], bO[i]
        fxe, fxo = x_faces(i, p)
        fye = 0.5 * (e + jnp.where(end, 0.0, up(e, 1)))
        fyo = 0.5 * (o + jnp.where(end, 0.0, up(o, 1)))
        gye = 0.5 * (e + jnp.where(begin, 0.0, down(e, 1)))
        gyo = 0.5 * (o + jnp.where(begin, 0.0, down(o, 1)))
        yr, yb = jnp.where(p, fye, fyo), jnp.where(p, fyo, fye)
        lv["yR"][i] = jnp.where(end, 0.0, yr)
        lv["yB"][i] = jnp.where(end, 0.0, yb)
        s = 0.5 * (e + o)
        above = 0.5 * (o + jnp.where(top, 0.0, up(e, 0)))
        below = 0.5 * (e + jnp.where(bot, 0.0, down(o, 0)))
        lv["s"][i] = s
        lv["c"][i] = jnp.where(top, 0.0, above)
        ce = fye + gye + (s + below) + (fxe + before[0])
        co = fyo + gyo + (s + above) + (fxo + before[1])
        cr, cb = jnp.where(p, ce, co), jnp.where(p, co, ce)
        lv["cR"][i] = cr
        lv["cB"][i] = cb
        x = box * 32 - H0 + i
        inside = jnp.logical_and(x >= 0, x < boxes * 32)
        lv["iR"][i] = jnp.where(inside, 1.0 / cr, 0.0)
        lv["iB"][i] = jnp.where(inside, 1.0 / cb, 0.0)
        return fxe, fxo

    planes(1, N0 - 1, FACES, faces, x_faces(0, parity(0)))

    for k in range(2):
        sweep_packed(lv, True, 1 + 2 * k, N0 - 1 - 2 * k)
        sweep_packed(lv, False, 2 + 2 * k, N0 - 2 - 2 * k)

    def restrict(j, carry):
        i = H0 + 2 * j
        a, b, _ = residual_packed(lv, i, H0 % 2)
        c, d, _ = residual_packed(lv, i + 1, (H0 + 1) % 2)
        pair_r[j] = (a + b) + (c + d)
        pair_b[j] = (bE[i] + bO[i]) + (bE[i + 1] + bO[i + 1])
        return carry

    lax.fori_loop(0, 16, restrict, 0, unroll=RESTRICT)

    halve = one_hot((256, 128), lambda i, j: (i >> 1) == j)
    f1 = 0.125 * matmul(pair_r[...].reshape(128, 256), halve)
    b1 = 0.125 * matmul(pair_b[...].reshape(128, 256), halve)
    own[0:16] = f1.reshape(16, 8, 128)
    own[16:32] = b1.reshape(16, 8, 128)

    for k in range(8):
        tmp[8 * k : 8 * k + 8, :] = own[16 + 2 * k] + own[17 + 2 * k]
    summed = tmp[pl.ds(0, 32, stride=2), :] + tmp[pl.ds(1, 32, stride=2), :]
    halve = one_hot((128, 128), lambda i, j: (i >> 1) == j)
    own[32:36] = (0.125 * matmul(summed, halve)).reshape(4, 8, 128)
    bottom[...] = bottom_row([own[32 + k] + pltpu.roll(own[32 + k], 4, 0) for k in range(4)])

    for out, right in ((first, odd), (second, 1 - odd)):
        out[0:H1] = own[pl.ds(right * (16 - H1), H1)]
        out[H1 : 2 * H1 + 1] = own[pl.ds(16 + right * (15 - H1), H1 + 1)]
        out[2 * H1 + 1 :] = own[32:36]


def bottom_row(pairs):
    total = None
    for k, plane in enumerate(pairs):
        spread = one_hot((128, 128), lambda i, j, k=k: jnp.logical_and((i >> 1) + 32 * k == j, i < 64))
        part = matmul(plane, spread)
        total = part if total is None else total + part
    low, high = total[0:1] + total[1:2], total[2:3] + total[3:4]
    row = 0.125 * jnp.where(my_place()[0] == 0, low, high)
    return jnp.broadcast_to(row, (8, 128))


def level_faces(b, ax, ay, az, inv, n, factor, depth, width, inside):
    row, lane = iota((8, 128), 0), iota((8, 128), 1)
    top, bot = row == depth - 1, row == 0
    end, begin = lane == width - 1, lane == 0
    cell = jnp.logical_and(row < depth, lane < width)
    ax[0] = factor * (b[0] + b[1])

    def step(i, odd, before):
        v = b[i]
        fx = factor * (v + b[i + 1])
        ax[i] = fx
        fy = factor * (v + jnp.where(end, 0.0, up(v, 1)))
        gy = factor * (v + jnp.where(begin, 0.0, down(v, 1)))
        fz = factor * (v + jnp.where(top, 0.0, up(v, 0)))
        gz = factor * (v + jnp.where(bot, 0.0, down(v, 0)))
        ay[i] = jnp.where(end, 0.0, fy)
        az[i] = jnp.where(top, 0.0, fz)
        center = (fz + gz) + (fx + before) + (fy + gy)
        inv[i] = jnp.where(jnp.logical_and(cell, inside(i)), 1.0 / center, 0.0)
        return fx

    planes(1, n - 1, 99, step, ax[0])


def nsum_plain(v, ax, ay, az, i):
    here = v[i]
    t = ax[i] * v[i + 1] + ax[i - 1] * v[i - 1]
    t = t + (ay[i] * up(here, 1) + down(ay[i] * here, 1))
    return t + (az[i] * up(here, 0) + down(az[i] * here, 0))


def colour(odd):
    return ((iota((8, 128), 0) + iota((8, 128), 1) + odd) & 1) == 0


def sweep_plain(v, f, ax, ay, az, inv, odd, shift, first, last):
    def step(i, plane_odd, carry):
        cells = colour((plane_odd + shift + odd) % 2)
        v[i] = jnp.where(cells, (f[i] + nsum_plain(v, ax, ay, az, i)) * inv[i], v[i])
        return carry

    planes(first, last, 99, step)


def first_plain(v, f, inv, shift, first, last):
    def step(i, plane_odd, carry):
        v[i] = jnp.where(colour((plane_odd + shift) % 2), f[i] * inv[i], 0.0)
        return carry

    planes(first, last, 99, step)


def residual_plain(v, f, ax, ay, az, center, i):
    return f[i] - (center * v[i] - nsum_plain(v, ax, ay, az, i))


def center_plain(b, ax, i, factor, depth, width):
    row, lane = iota((8, 128), 0), iota((8, 128), 1)
    v = b[i]
    fy = jnp.where(lane == width - 1, 0.0, up(v, 1)) + jnp.where(lane == 0, 0.0, down(v, 1))
    fz = jnp.where(row == depth - 1, 0.0, up(v, 0)) + jnp.where(row == 0, 0.0, down(v, 0))
    return factor * (4.0 * v + fy + fz) + (ax[i] + ax[i - 1])


def middle_kernel(boxes, own, first, second, bottom, v1, f1, ax1, ay1, az1, inv1, ax2, ay2, az2, inv2, send, compact, message, v2, f2, b2, b1, tmp):
    box = my_place()[1]
    w = H1 + 1
    swapped = (box & 1) == 1

    def received(k, count):
        one, two = first[k : k + count], second[k : k + count]
        return jnp.where(swapped, two, one), jnp.where(swapped, one, two)

    left, right = received(H1, w)
    b1[0:w] = left
    b1[w : w + 16] = own[16:32]
    b1[w + 16 :] = right
    left, right = received(0, H1)
    f1[0:1] = jnp.zeros((1, 8, 128), F32)
    f1[1 : 1 + H1] = left
    f1[w : w + 16] = own[0:16]
    f1[w + 16 : w + 16 + H1] = right
    f1[N1 - 1 :] = jnp.zeros((1, 8, 128), F32)
    left, right = received(H1 + w, 4)
    b2[...] = jnp.zeros(b2.shape, F32)
    for at, part in ((0, left), (8, own[32:36]), (16, right)):
        for k in range(8):
            b2[at + k, 0:4, :] = part[k // 2, 4 * (k % 2) : 4 * (k % 2) + 4]
    v1[...] = jnp.zeros(v1.shape, F32)
    v2[...] = jnp.zeros(v2.shape, F32)
    f2[...] = jnp.zeros(f2.shape, F32)

    def within(size, width):
        def inside(i):
            x = box * size - width + i
            return jnp.logical_and(x >= 0, x < boxes * size)

        return inside

    k1, k2 = 0.5 * 0.25, 0.5 * 0.25**2
    level_faces(b1, ax1, ay1, az1, inv1, N1, k1, 8, 128, within(16, w))
    level_faces(b2, ax2, ay2, az2, inv2, N2, k2, 4, 64, within(8, 8))

    one = (f1, ax1, ay1, az1, inv1)
    first_plain(v1, f1, inv1, 1, 1, N1 - 1)
    sweep_plain(v1, *one, 1, 1, 2, N1 - 2)
    sweep_plain(v1, *one, 0, 1, 3, N1 - 3)
    sweep_plain(v1, *one, 1, 1, 4, N1 - 4)

    def restrict(j, carry):
        i = 5 + 2 * j
        parts = [residual_plain(v1, *one[:4], center_plain(b1, ax1, k, k1, 8, 128), k) for k in (i, i + 1)]
        tmp[8 * j : 8 * j + 8, :] = parts[0] + parts[1]
        return carry

    for j in range(16):
        restrict(j, 0)
    summed = tmp[pl.ds(0, 64, stride=2), :] + tmp[pl.ds(1, 64, stride=2), :]
    coarse = 0.125 * matmul(summed, one_hot((128, 128), lambda i, j: (i >> 1) == j))
    for j in range(16):
        f2[4 + j, 0:4, :] = coarse[4 * j : 4 * j + 4]

    two = (f2, ax2, ay2, az2, inv2)
    first_plain(v2, f2, inv2, 0, 4, 20)
    sweep_plain(v2, *two, 1, 0, 5, 19)
    sweep_plain(v2, *two, 0, 0, 6, 18)
    sweep_plain(v2, *two, 1, 0, 7, 17)
    send[0:8] = v2[8:16]
    send[8:16] = f2[8:16]
    for k in range(4):
        both = [pltpu.roll(ref[9 + 2 * k], 4, 0) + ref[8 + 2 * k] for ref in (v2, f2)]
        compact[k] = both[0] + pltpu.roll(both[1], 64, 1)

    pairs = []
    for k in range(4):
        parts = [
            residual_plain(v2, *two[:4], center_plain(b2, ax2, i, k2, 4, 64), i)
            for i in (8 + 2 * k, 9 + 2 * k)
        ]
        pairs.append(parts[0] + parts[1])
    source = bottom_row(pairs)
    rows = jnp.where((iota((8, 128), 0) & 1) == 0, source, bottom[...])
    for k in range(message.shape[0] // 8):
        message[8 * k : 8 * k + 8, :] = rows


def coarse_solve(n, source, coefficient, dref, qref, eref):
    row, lane = iota((n, 128), 0), iota((n, 128), 1)
    factor = 0.5 * 0.25**3
    last = jnp.logical_and(row == n - 1, lane >= 96)
    first = jnp.logical_and(row == 0, lane < 32)
    inner_hi, inner_lo = lane < 96, lane >= 32
    end, begin = (lane & 31) == 31, (lane & 31) == 0

    def xp(v):
        a = pltpu.roll(v, 96, 1)
        return jnp.where(inner_hi, a, up(a, 0))

    def xm(v):
        a = pltpu.roll(v, 32, 1)
        return jnp.where(inner_lo, a, down(a, 0))

    ax, ay, center = [], [], []
    az = factor * (coefficient[0] + coefficient[1])
    for b in coefficient:
        fx = factor * (b + jnp.where(last, 0.0, xp(b)))
        gx = factor * (b + jnp.where(first, 0.0, xm(b)))
        fy = factor * (b + jnp.where(end, 0.0, up(b, 1)))
        gy = factor * (b + jnp.where(begin, 0.0, down(b, 1)))
        ax.append(jnp.where(last, 0.0, fx))
        ay.append(jnp.where(end, 0.0, fy))
        center.append((factor * b + az) + (fx + gx) + (fy + gy))

    def total(u, w):
        s = u[0] * w[0] + u[1] * w[1]
        return jnp.sum(jnp.sum(s, axis=0, keepdims=True), axis=1, keepdims=True)

    for t in range(2):
        dref[t] = source[t]
        qref[t] = source[t]
        eref[t, 8 : 8 + n] = jnp.zeros((n, 128), F32)
        eref[t, 0:8] = jnp.zeros((8, 128), F32)
        eref[t, 8 + n :] = jnp.zeros((8, 128), F32)

    def iterate(k, now):
        d = (dref[0], dref[1])
        w = []
        for t in range(2):
            v = d[t]
            s = ax[t] * xp(v) + xm(ax[t] * v)
            s = s + (ay[t] * up(v, 1) + down(ay[t] * v, 1))
            w.append(center[t] * v - (s + az * d[1 - t]))
        alpha = now / total(d, w)
        q = []
        for t in range(2):
            eref[t, 8 : 8 + n] = eref[t, 8 : 8 + n] + alpha * d[t]
            q.append(qref[t] - alpha * w[t])
            qref[t] = q[t]
        later = total(q, q)
        beta = later / now
        for t in range(2):
            dref[t] = q[t] + beta * d[t]
        return later

    lax.fori_loop(0, ITERS, iterate, total(source, source), unroll=True)


def coarse_kernel(boxes, gathered, e2, dref, qref, eref):
    box = my_place()[1]
    source = [gathered[t, pl.ds(0, boxes, stride=2), :] for t in range(2)]
    coefficient = [gathered[t, pl.ds(1, boxes, stride=2), :] for t in range(2)]
    coarse_solve(boxes, source, coefficient, dref, qref, eref)
    near = [eref[t, pl.ds(7 + box, 8), :] for t in range(2)]
    spread = one_hot((128, 512), lambda i, j: jnp.logical_and(((j >> 7) * 32) + ((j & 127) >> 1) == i, (j & 127) < 64))
    fine = [matmul(e, spread) for e in near]
    row = iota((8, 128), 0)
    for i in range(N2):
        cell, k = (i // 2) // 4, (i // 2) % 4
        low, high = (f[cell : cell + 1, 128 * k : 128 * k + 128] for f in fine)
        e2[i] = jnp.where(row < 2, low, jnp.where(row < 4, high, 0.0))


def after_kernel(compact, black, gathered, first, second):
    del gathered
    odd = my_place()[1] & 1
    for out, right in ((first, odd), (second, 1 - odd)):
        out[0:4] = compact[...]
        start = H0 + right * (32 - H0)
        for k in range(H0):
            for half in range(2):
                out[4 + 2 * k + half] = black[start + k, :, 128 * half : 128 * half + 128]


def last_kernel(*refs):
    names = ("e2", "first", "second", "own2", "v1", "f1", "ax1", "ay1", "az1", "inv1", "ax2", "ay2", "az2", "inv2")
    given = dict(zip(names, refs))
    refs = refs[len(names) :]
    level0 = dict(zip(PACKED, refs))
    refs = refs[len(PACKED) :]
    out_v, out_r, vR, vB, v1, v2, f2, wide, e0 = refs
    slab, box = my_place()
    e2, first, second, own2 = given["e2"], given["first"], given["second"], given["own2"]
    swapped = (box & 1) == 1

    def received(side, k, count):
        one, two = (first, second) if side == 0 else (second, first)
        return jnp.where(swapped, two[k : k + count], one[k : k + count])

    v2[8:16] = own2[0:8]
    f2[8:16] = own2[8:16]
    quarter = jnp.logical_and(iota((8, 128), 0) < 4, iota((8, 128), 1) < 64)
    for side, at in ((0, 0), (1, 16)):
        four = received(side, 0, 4)
        for k in range(4):
            for ref, plane in ((v2, four[k]), (f2, pltpu.roll(four[k], 64, 1))):
                ref[at + 2 * k] = jnp.where(quarter, plane, 0.0)
                ref[at + 2 * k + 1] = jnp.where(quarter, pltpu.roll(plane, 4, 0), 0.0)
    for i in range(N2):
        v2[i] = v2[i] + e2[i]
    two = (f2, given["ax2"], given["ay2"], given["az2"], given["inv2"])
    for k in range(2):
        sweep_plain(v2, *two, 0, 0, 1 + 2 * k, N2 - 1 - 2 * k)
        sweep_plain(v2, *two, 1, 0, 2 + 2 * k, N2 - 2 - 2 * k)

    packed = jnp.concatenate([v2[4 + j, 0:4, :] for j in range(16)], axis=0)
    fine = matmul(packed, one_hot((128, 128), lambda i, j: (j >> 1) == i))
    wide[pl.ds(0, 64, stride=2), :] = fine
    wide[pl.ds(1, 64, stride=2), :] = fine
    for i in range(6, N1 - 6):
        j = (i + 3) // 2 - 4
        v1[i] = given["v1"][i] + wide[8 * j : 8 * j + 8, :]
    one = (given["f1"], given["ax1"], given["ay1"], given["az1"], given["inv1"])
    for k in range(2):
        sweep_plain(v1, *one, 0, 1, 7 + 2 * k, N1 - 7 - 2 * k)
        sweep_plain(v1, *one, 1, 1, 8 + 2 * k, N1 - 8 - 2 * k)

    double = one_hot((128, 256), lambda i, j: (j >> 1) == i)
    e0[...] = matmul(v1[10:32].reshape(176, 128), double).reshape(22, 8, 256)
    lv = dict(level0, vR=vR, vB=vB)

    black = level0["vB"]

    def correct(j, carry):
        e = e0[j]
        vB[2 * j - 1] = black[2 * j - 1] + e
        vB[2 * j] = black[2 * j] + e
        return carry

    lax.fori_loop(3, 19, correct, 0, unroll=4)
    for side, at in ((0, 0), (1, H0 + 32)):
        for k in range(H0):
            for half in range(2):
                lanes = slice(128 * half, 128 * half + 128)
                vB[at + k, :, lanes] = received(side, 4 + 2 * k + half, 1)[0] + e0[(at + k + 1) // 2, :, lanes]
    for k in range(2):
        sweep_packed(lv, True, 1 + 2 * k, N0 - 1 - 2 * k)
        sweep_packed(lv, False, 2 + 2 * k, N0 - 2 - 2 * k)


    def finish(i, odd, carry):
        x = i - H0
        red, black, p = residual_packed(lv, i, odd)
        for out, a, b in ((out_v, vR[i], vB[i]), (out_r, red, black)):
            for at, whole in ((0, jnp.where(p, a, b)), (1, jnp.where(p, b, a))):
                part = jnp.where(slab == 0, whole[0:4], whole[4:8])
                for half in range(2):
                    out[slab_rows(x, half, at), :] = part[:, 128 * half : 128 * half + 128]
        return carry

    planes(H0, H0 + 32, FINISH, finish)


def call(kernel, outs, scratch, *args, limit=12):
    vmem = pl.BlockSpec(memory_space=pltpu.VMEM)
    return pl.pallas_call(
        kernel,
        out_shape=[jax.ShapeDtypeStruct(s, F32) for s in outs],
        in_specs=[vmem] * len(args),
        out_specs=[vmem] * len(outs),
        scratch_shapes=[pltpu.VMEM(s, F32) for s in scratch],
        compiler_params=pltpu.CompilerParams(vmem_limit_bytes=limit * 1024 * 1024),
    )(*args)


def edges(*args):
    return pl.pallas_call(
        edge_kernel,
        out_shape=jax.ShapeDtypeStruct((EDGE, 256), F32),
        in_specs=[pl.BlockSpec(memory_space=pl.ANY)] * 3,
        out_specs=pl.BlockSpec(memory_space=pltpu.VMEM),
        scratch_shapes=[pltpu.VMEM((128, 128), F32)] * 3 + [pltpu.SemaphoreType.DMA((3,))],
        compiler_params=pltpu.CompilerParams(vmem_limit_bytes=60 * 1024 * 1024),
    )(*[a.reshape(8, 64, 128) for a in args])


def by_tiles(a):
    return a.reshape(8, 4, 8, 2, 128).transpose(0, 1, 3, 2, 4).reshape(512, 128)


def from_tiles(a):
    return a.reshape(8, 4, 2, 8, 128).transpose(0, 1, 3, 2, 4).reshape(8, 32, 256)


def exchange(first, second):
    boxes = lax.axis_size("box")
    odd = [(i, i + 1) for i in range(1, boxes - 1, 2)]
    even = [(i, i + 1) for i in range(0, boxes - 1, 2)]
    return [lax.ppermute(x, "box", p + [(j, i) for i, j in p]) for x, p in ((first, odd), (second, even))]


def body(pressure_guess, right_side, coefficient):
    boxes = lax.axis_size("box")
    flat = [by_tiles(a) for a in (pressure_guess, right_side, coefficient)]
    first = edges(*flat)
    low, high, second = call(pack_kernel, [(16 * ROWS, 256)] * 2 + [(EDGE, 256)], [], *flat)
    first, second = exchange(first, second)
    low, high = lax.all_gather(low, "slab"), lax.all_gather(high, "slab")
    halo = lax.all_gather(jnp.stack([first, second]), "slab")

    plane = (N0, 8, 256)
    fine = call(
        functools.partial(fine_kernel, boxes),
        [plane] * len(PACKED) + [(36, 8, 128), (SEND1, 8, 128), (SEND1, 8, 128), (8, 128)],
        [plane] * 3 + [(16, 8, 256)] * 2 + [(64, 128)],
        low,
        high,
        halo,
    )
    level0 = fine[: len(PACKED)]
    own, first, second, bottom = fine[len(PACKED) :]
    first, second = exchange(first, second)

    one, two = (N1, 8, 128), (N2, 8, 128)
    *levels, send, compact, message = call(
        functools.partial(middle_kernel, boxes),
        [one] * 6 + [two] * 4 + [(16, 8, 128), (4, 8, 128), (2 * boxes, 128)],
        [two] * 3 + [one, (128, 128)],
        own,
        first,
        second,
        bottom,
    )
    spread = lax.all_to_all(message.reshape(boxes, 2, 128), "box", 0, 0).reshape(2 * boxes, 128)
    first, second = exchange(*call(after_kernel, [(SEND2, 8, 128)] * 2, [], compact, level0[0], spread))
    gathered = lax.all_gather(spread, "slab")
    (e2,) = call(
        functools.partial(coarse_kernel, boxes),
        [two],
        [(2, boxes, 128), (2, boxes, 128), (2, boxes + 16, 128)],
        gathered,
    )
    pressure, residual = call(
        last_kernel,
        [(512, 128)] * 2,
        [plane, plane, one, two, two, (128, 128), (22, 8, 256)],
        e2,
        first,
        second,
        send,
        *levels,
        *level0,
    )
    return from_tiles(pressure), from_tiles(residual)


def solution(mesh):
    split = P("slab", "box", None)
    return jax.shard_map(body, mesh=mesh, in_specs=(split,) * 3, out_specs=(split,) * 2, check_vma=False)
```

```python
import functools

import jax
import jax.numpy as jnp
from jax import lax
from jax.experimental import pallas as pl
from jax.experimental.pallas import tpu as pltpu
from jax.sharding import PartitionSpec as P

ITERS = 8
F32 = jnp.float32
BF16 = jnp.bfloat16

H0 = 5
H1 = 12
N0 = 32 + 2 * H0
N1 = 16 + 2 * (H1 + 1)
N2 = 24
ROWS = 20
EDGE = 96
EDGE_F, EDGE_V = 8 * H0, 16 * H0 - 8
SWEEP, FACES, RESTRICT, FINISH = 99, 99, 16, 99
SEND1 = H1 + (H1 + 1) + 4
SEND2 = 4 + 2 * H0


def matmul(x, m):
    high = x.astype(BF16)
    rest = x - high.astype(F32)
    mid = rest.astype(BF16)
    low = (rest - mid.astype(F32)).astype(BF16)
    dot = functools.partial(jnp.dot, preferred_element_type=F32)
    return dot(high, m) + (dot(mid, m) + dot(low, m))


def one_hot(shape, rule):
    i = lax.broadcasted_iota(jnp.int32, shape, 0)
    j = lax.broadcasted_iota(jnp.int32, shape, 1)
    return rule(i, j).astype(F32).astype(BF16)


def iota(shape, axis):
    return lax.broadcasted_iota(jnp.int32, shape, axis)


def up(v, axis):
    return pltpu.roll(v, v.shape[axis] - 1, axis)


def down(v, axis):
    return pltpu.roll(v, 1, axis)


def planes(first, last, unroll, step, carry=0):
    def pair(k, carry):
        i = first + 2 * k
        return step(i + 1, (first + 1) % 2, step(i, first % 2, carry))

    count = (last - first) // 2
    if unroll < count:
        return lax.fori_loop(0, count, pair, carry, unroll=unroll)
    for k in range(count):
        carry = pair(k, carry)
    return carry


def my_place():
    return lax.axis_index("slab"), lax.axis_index("box")


def slab_rows(x, half, odd):
    return pl.ds((x // 8) * 16 + half * 8 + x % 8 + 64 * odd, 4, stride=128)


def pack_plane(g, r, c, x, rows, even_y, out, b_at, f_at, v_at):
    p0 = even_y if x % 2 == 0 else jnp.logical_not(even_y)
    for half in range(2):
        lanes = slice(128 * half, 128 * half + 128)
        even, odd = rows(half, 0), rows(half, 1)
        out[b_at : b_at + 4, lanes] = c[even, :]
        out[b_at + 4 : b_at + 8, lanes] = c[odd, :]
        if f_at is not None:
            fe, fo = r[even, :], r[odd, :]
            out[f_at : f_at + 4, lanes] = jnp.where(p0, fe, fo)
            out[f_at + 4 : f_at + 8, lanes] = jnp.where(p0, fo, fe)
        out[v_at : v_at + 4, lanes] = jnp.where(p0, g[odd, :], g[even, :])


def pack_edge(parts, right, rows, even_y, out):
    for k in range(H0):
        x = 32 - H0 + k if right else k
        f_at = k - 1 if right else k
        f_at = EDGE_F + 8 * f_at if 0 <= f_at < H0 - 1 else None
        pack_plane(*parts, x, functools.partial(rows, x), even_y, out, 8 * k, f_at, EDGE_V + 4 * k)
    out[EDGE_V + 4 * H0 :, :] = jnp.zeros((EDGE - EDGE_V - 4 * H0, 256), F32)


def pack_kernel(g, r, c, low, high, second):
    even_y = (iota((4, 128), 1) & 1) == 0
    swapped = (my_place()[1] & 1) == 1

    @pl.when(swapped)
    def _():
        pack_edge((g, r, c), False, slab_rows, even_y, second)

    @pl.when(jnp.logical_not(swapped))
    def _():
        pack_edge((g, r, c), True, slab_rows, even_y, second)

    for x in range(32):
        out, base = (low, x * ROWS) if x < 16 else (high, (x - 16) * ROWS)
        pack_plane(g, r, c, x, functools.partial(slab_rows, x), even_y, out, base, base + 8, base + 16)


def edge_kernel(g_hbm, r_hbm, c_hbm, first, *scratch):
    parts, sem = scratch[0:3], scratch[3]
    odd = my_place()[1] & 1
    at = pl.multiple_of(48 * odd, 16)
    copies = [
        pltpu.make_async_copy(source.at[:, pl.ds(at, 16), :], target.reshape(8, 16, 128), sem.at[k])
        for k, (source, target) in enumerate(zip((g_hbm, r_hbm, c_hbm), parts))
    ]
    for copy in copies:
        copy.start()
    for copy in copies:
        copy.wait()
    even_y = (iota((4, 128), 1) & 1) == 0

    def rows(x, half, second_z):
        return pl.ds(half * 8 + x % 8 + 16 * second_z, 4, stride=32)

    @pl.when(odd == 1)
    def _():
        pack_edge(parts, True, rows, even_y, first)

    @pl.when(odd == 0)
    def _():
        pack_edge(parts, False, rows, even_y, first)


def parity(odd):
    return ((iota((8, 256), 1) + odd + 1) & 1) == 0


def nsum_packed(lv, v, xa, xb, ya, yb, i, p):
    here = v[i]
    t = xa[i] * v[i + 1] + xb[i - 1] * v[i - 1]
    t = t + (ya[i] * up(here, 1) + down(yb[i] * here, 1))
    cross = lv["c"][i]
    z = jnp.where(p, down(cross * here, 0), cross * up(here, 0))
    return t + (lv["s"][i] * here + z)


def sweep_packed(lv, red, first, last):
    def step(i, odd, carry):
        p = parity(odd)
        if red:
            n = nsum_packed(lv, lv["vB"], lv["xR"], lv["xB"], lv["yR"], lv["yB"], i, p)
            lv["vR"][i] = (lv["fR"][i] + n) * lv["iR"][i]
        else:
            p = jnp.logical_not(p)
            n = nsum_packed(lv, lv["vR"], lv["xB"], lv["xR"], lv["yB"], lv["yR"], i, p)
            lv["vB"][i] = (lv["fB"][i] + n) * lv["iB"][i]
        return carry

    planes(first, last, SWEEP, step)


def residual_packed(lv, i, odd):
    p = parity(odd)
    n = nsum_packed(lv, lv["vB"], lv["xR"], lv["xB"], lv["yR"], lv["yB"], i, p)
    r_red = lv["fR"][i] - (lv["cR"][i] * lv["vR"][i] - n)
    q = jnp.logical_not(p)
    n = nsum_packed(lv, lv["vR"], lv["xB"], lv["xR"], lv["yB"], lv["yR"], i, q)
    r_black = lv["fB"][i] - (lv["cB"][i] * lv["vB"][i] - n)
    return r_red, r_black, p


PACKED = ("vB", "fR", "fB", "xR", "xB", "yR", "yB", "s", "c", "iR", "iB", "cR", "cB")


def fine_kernel(boxes, lo, hi, halo, *refs):
    outs = dict(zip(PACKED, refs))
    own, first, second, bottom = refs[len(PACKED) : len(PACKED) + 4]
    vR, bE, bO, pair_r, pair_b, tmp = refs[len(PACKED) + 4 :]
    lv = dict(outs, vR=vR)
    box = my_place()[1]
    odd = box & 1
    row, lane = iota((8, 256), 0), iota((8, 256), 1)
    low_half = row < 4

    def merge(parts, at, i, low, high):
        a, b = (part[at : at + 8, :] for part in parts)
        low[i] = jnp.where(low_half, a, pltpu.roll(b, 4, 0))
        high[i] = jnp.where(low_half, pltpu.roll(a, 4, 0), b)

    def stack(parts, at, i, out):
        for t in range(2):
            out[i, 4 * t : 4 * t + 4, :] = parts[t][at : at + 4, :]

    for x in range(32):
        source, base = (lo, x * ROWS) if x < 16 else (hi, (x - 16) * ROWS)
        parts = source.at[0], source.at[1]
        merge(parts, base, H0 + x, bE, bO)
        merge(parts, base + 8, H0 + x, lv["fR"], lv["fB"])
        stack(parts, base + 16, H0 + x, lv["vB"])
    for side, at in ((odd, 0), (1 - odd, H0 + 32)):
        parts = halo.at[0, side], halo.at[1, side]
        for k in range(H0):
            merge(parts, 8 * k, at + k, bE, bO)
            stack(parts, EDGE_V + 4 * k, at + k, lv["vB"])
        for k in range(H0 - 1):
            merge(parts, EDGE_F + 8 * k, (1 if at == 0 else at) + k, lv["fR"], lv["fB"])

    top, bot = row == 7, row == 0
    end, begin = lane == 255, lane == 0

    def x_faces(i, p):
        fxe, fxo = 0.5 * (bE[i] + bE[i + 1]), 0.5 * (bO[i] + bO[i + 1])
        lv["xR"][i] = jnp.where(p, fxe, fxo)
        lv["xB"][i] = jnp.where(p, fxo, fxe)
        return fxe, fxo

    def faces(i, odd, before):
        p = parity(odd)
        e, o = bE[i], bO[i]
        fxe, fxo = x_faces(i, p)
        fye = 0.5 * (e + jnp.where(end, 0.0, up(e, 1)))
        fyo = 0.5 * (o + jnp.where(end, 0.0, up(o, 1)))
        gye = 0.5 * (e + jnp.where(begin, 0.0, down(e, 1)))
        gyo = 0.5 * (o + jnp.where(begin, 0.0, down(o, 1)))
        yr, yb = jnp.where(p, fye, fyo), jnp.where(p, fyo, fye)
        lv["yR"][i] = jnp.where(end, 0.0, yr)
        lv["yB"][i] = jnp.where(end, 0.0, yb)
        s = 0.5 * (e + o)
        above = 0.5 * (o + jnp.where(top, 0.0, up(e, 0)))
        below = 0.5 * (e + jnp.where(bot, 0.0, down(o, 0)))
        lv["s"][i] = s
        lv["c"][i] = jnp.where(top, 0.0, above)
        ce = fye + gye + (s + below) + (fxe + before[0])
        co = fyo + gyo + (s + above) + (fxo + before[1])
        cr, cb = jnp.where(p, ce, co), jnp.where(p, co, ce)
        lv["cR"][i] = cr
        lv["cB"][i] = cb
        x = box * 32 - H0 + i
        inside = jnp.logical_and(x >= 0, x < boxes * 32)
        lv["iR"][i] = jnp.where(inside, 1.0 / cr, 0.0)
        lv["iB"][i] = jnp.where(inside, 1.0 / cb, 0.0)
        return fxe, fxo

    planes(1, N0 - 1, FACES, faces, x_faces(0, parity(0)))

    for k in range(2):
        sweep_packed(lv, True, 1 + 2 * k, N0 - 1 - 2 * k)
        sweep_packed(lv, False, 2 + 2 * k, N0 - 2 - 2 * k)

    def restrict(j, carry):
        i = H0 + 2 * j
        a, b, _ = residual_packed(lv, i, H0 % 2)
        c, d, _ = residual_packed(lv, i + 1, (H0 + 1) % 2)
        pair_r[j] = (a + b) + (c + d)
        pair_b[j] = (bE[i] + bO[i]) + (bE[i + 1] + bO[i + 1])
        return carry

    lax.fori_loop(0, 16, restrict, 0, unroll=RESTRICT)

    halve = one_hot((256, 128), lambda i, j: (i >> 1) == j)
    f1 = 0.125 * matmul(pair_r[...].reshape(128, 256), halve)
    b1 = 0.125 * matmul(pair_b[...].reshape(128, 256), halve)
    own[0:16] = f1.reshape(16, 8, 128)
    own[16:32] = b1.reshape(16, 8, 128)

    for k in range(8):
        tmp[8 * k : 8 * k + 8, :] = own[16 + 2 * k] + own[17 + 2 * k]
    summed = tmp[pl.ds(0, 32, stride=2), :] + tmp[pl.ds(1, 32, stride=2), :]
    halve = one_hot((128, 128), lambda i, j: (i >> 1) == j)
    own[32:36] = (0.125 * matmul(summed, halve)).reshape(4, 8, 128)
    bottom[...] = bottom_row([own[32 + k] + pltpu.roll(own[32 + k], 4, 0) for k in range(4)])

    for out, right in ((first, odd), (second, 1 - odd)):
        out[0:H1] = own[pl.ds(right * (16 - H1), H1)]
        out[H1 : 2 * H1 + 1] = own[pl.ds(16 + right * (15 - H1), H1 + 1)]
        out[2 * H1 + 1 :] = own[32:36]


def bottom_row(pairs):
    total = None
    for k, plane in enumerate(pairs):
        spread = one_hot((128, 128), lambda i, j, k=k: jnp.logical_and((i >> 1) + 32 * k == j, i < 64))
        part = matmul(plane, spread)
        total = part if total is None else total + part
    low, high = total[0:1] + total[1:2], total[2:3] + total[3:4]
    row = 0.125 * jnp.where(my_place()[0] == 0, low, high)
    return jnp.broadcast_to(row, (8, 128))


def level_faces(b, ax, ay, az, inv, n, factor, depth, width, inside):
    row, lane = iota((8, 128), 0), iota((8, 128), 1)
    top, bot = row == depth - 1, row == 0
    end, begin = lane == width - 1, lane == 0
    cell = jnp.logical_and(row < depth, lane < width)
    ax[0] = factor * (b[0] + b[1])

    def step(i, odd, before):
        v = b[i]
        fx = factor * (v + b[i + 1])
        ax[i] = fx
        fy = factor * (v + jnp.where(end, 0.0, up(v, 1)))
        gy = factor * (v + jnp.where(begin, 0.0, down(v, 1)))
        fz = factor * (v + jnp.where(top, 0.0, up(v, 0)))
        gz = factor * (v + jnp.where(bot, 0.0, down(v, 0)))
        ay[i] = jnp.where(end, 0.0, fy)
        az[i] = jnp.where(top, 0.0, fz)
        center = (fz + gz) + (fx + before) + (fy + gy)
        inv[i] = jnp.where(jnp.logical_and(cell, inside(i)), 1.0 / center, 0.0)
        return fx

    planes(1, n - 1, 99, step, ax[0])


def nsum_plain(v, ax, ay, az, i):
    here = v[i]
    t = ax[i] * v[i + 1] + ax[i - 1] * v[i - 1]
    t = t + (ay[i] * up(here, 1) + down(ay[i] * here, 1))
    return t + (az[i] * up(here, 0) + down(az[i] * here, 0))


def colour(odd):
    return ((iota((8, 128), 0) + iota((8, 128), 1) + odd) & 1) == 0


def sweep_plain(v, f, ax, ay, az, inv, odd, shift, first, last):
    def step(i, plane_odd, carry):
        cells = colour((plane_odd + shift + odd) % 2)
        v[i] = jnp.where(cells, (f[i] + nsum_plain(v, ax, ay, az, i)) * inv[i], v[i])
        return carry

    planes(first, last, 99, step)


def first_plain(v, f, inv, shift, first, last):
    def step(i, plane_odd, carry):
        v[i] = jnp.where(colour((plane_odd + shift) % 2), f[i] * inv[i], 0.0)
        return carry

    planes(first, last, 99, step)


def residual_plain(v, f, ax, ay, az, center, i):
    return f[i] - (center * v[i] - nsum_plain(v, ax, ay, az, i))


def center_plain(b, ax, i, factor, depth, width):
    row, lane = iota((8, 128), 0), iota((8, 128), 1)
    v = b[i]
    fy = jnp.where(lane == width - 1, 0.0, up(v, 1)) + jnp.where(lane == 0, 0.0, down(v, 1))
    fz = jnp.where(row == depth - 1, 0.0, up(v, 0)) + jnp.where(row == 0, 0.0, down(v, 0))
    return factor * (4.0 * v + fy + fz) + (ax[i] + ax[i - 1])


def middle_kernel(boxes, own, first, second, bottom, v1, f1, ax1, ay1, az1, inv1, ax2, ay2, az2, inv2, send, compact, message, v2, f2, b2, b1, tmp):
    box = my_place()[1]
    w = H1 + 1
    swapped = (box & 1) == 1

    def received(k, count):
        one, two = first[k : k + count], second[k : k + count]
        return jnp.where(swapped, two, one), jnp.where(swapped, one, two)

    left, right = received(H1, w)
    b1[0:w] = left
    b1[w : w + 16] = own[16:32]
    b1[w + 16 :] = right
    left, right = received(0, H1)
    f1[0:1] = jnp.zeros((1, 8, 128), F32)
    f1[1 : 1 + H1] = left
    f1[w : w + 16] = own[0:16]
    f1[w + 16 : w + 16 + H1] = right
    f1[N1 - 1 :] = jnp.zeros((1, 8, 128), F32)
    left, right = received(H1 + w, 4)
    b2[...] = jnp.zeros(b2.shape, F32)
    for at, part in ((0, left), (8, own[32:36]), (16, right)):
        for k in range(8):
            b2[at + k, 0:4, :] = part[k // 2, 4 * (k % 2) : 4 * (k % 2) + 4]
    v1[...] = jnp.zeros(v1.shape, F32)
    v2[...] = jnp.zeros(v2.shape, F32)
    f2[...] = jnp.zeros(f2.shape, F32)

    def within(size, width):
        def inside(i):
            x = box * size - width + i
            return jnp.logical_and(x >= 0, x < boxes * size)

        return inside

    k1, k2 = 0.5 * 0.25, 0.5 * 0.25**2
    level_faces(b1, ax1, ay1, az1, inv1, N1, k1, 8, 128, within(16, w))
    level_faces(b2, ax2, ay2, az2, inv2, N2, k2, 4, 64, within(8, 8))

    one = (f1, ax1, ay1, az1, inv1)
    first_plain(v1, f1, inv1, 1, 1, N1 - 1)
    sweep_plain(v1, *one, 1, 1, 2, N1 - 2)
    sweep_plain(v1, *one, 0, 1, 3, N1 - 3)
    sweep_plain(v1, *one, 1, 1, 4, N1 - 4)

    def restrict(j, carry):
        i = 5 + 2 * j
        parts = [residual_plain(v1, *one[:4], center_plain(b1, ax1, k, k1, 8, 128), k) for k in (i, i + 1)]
        tmp[8 * j : 8 * j + 8, :] = parts[0] + parts[1]
        return carry

    for j in range(16):
        restrict(j, 0)
    summed = tmp[pl.ds(0, 64, stride=2), :] + tmp[pl.ds(1, 64, stride=2), :]
    coarse = 0.125 * matmul(summed, one_hot((128, 128), lambda i, j: (i >> 1) == j))
    for j in range(16):
        f2[4 + j, 0:4, :] = coarse[4 * j : 4 * j + 4]

    two = (f2, ax2, ay2, az2, inv2)
    first_plain(v2, f2, inv2, 0, 4, 20)
    sweep_plain(v2, *two, 1, 0, 5, 19)
    sweep_plain(v2, *two, 0, 0, 6, 18)
    sweep_plain(v2, *two, 1, 0, 7, 17)
    send[0:8] = v2[8:16]
    send[8:16] = f2[8:16]
    for k in range(4):
        both = [pltpu.roll(ref[9 + 2 * k], 4, 0) + ref[8 + 2 * k] for ref in (v2, f2)]
        compact[k] = both[0] + pltpu.roll(both[1], 64, 1)

    pairs = []
    for k in range(4):
        parts = [
            residual_plain(v2, *two[:4], center_plain(b2, ax2, i, k2, 4, 64), i)
            for i in (8 + 2 * k, 9 + 2 * k)
        ]
        pairs.append(parts[0] + parts[1])
    source = bottom_row(pairs)
    rows = jnp.where((iota((8, 128), 0) & 1) == 0, source, bottom[...])
    for k in range(message.shape[0] // 8):
        message[8 * k : 8 * k + 8, :] = rows


def coarse_solve(source, coefficient, dref, sref, rref, eref):
    shape = source[0].shape
    groups = shape[0]
    group, row, lane = (iota(shape, k) for k in range(3))
    factor = 0.5 * 0.25**3
    last = jnp.logical_and(jnp.logical_and(group == groups - 1, row == 7), lane >= 96)
    first = jnp.logical_and(jnp.logical_and(group == 0, row == 0), lane < 32)
    inner_hi, inner_lo = lane < 96, lane >= 32
    end, begin = (lane & 31) == 31, (lane & 31) == 0

    def lanes(v, shift):
        return pltpu.roll(v.reshape(8 * groups, 128), shift, 1).reshape(shape)

    def xp(v):
        a = lanes(v, 96)
        return jnp.where(inner_hi, a, jnp.concatenate([a[1:], up(a[0], 0)[None]], axis=0))

    def xm(v):
        a = lanes(v, 32)
        return jnp.where(inner_lo, a, jnp.concatenate([down(a[groups - 1], 0)[None], a[:-1]], axis=0))

    ax, ay, center = [], [], []
    az = factor * (coefficient[0] + coefficient[1])
    for b in coefficient:
        fx = factor * (b + jnp.where(last, 0.0, xp(b)))
        gx = factor * (b + jnp.where(first, 0.0, xm(b)))
        fy = factor * (b + jnp.where(end, 0.0, lanes(b, 127)))
        gy = factor * (b + jnp.where(begin, 0.0, lanes(b, 1)))
        ax.append(jnp.where(last, 0.0, fx))
        ay.append(jnp.where(end, 0.0, fy))
        center.append((factor * b + az) + (fx + gx) + (fy + gy))

    def total(u, w):
        s = jnp.sum(u[0] * w[0] + u[1] * w[1], axis=0)
        return jnp.sum(jnp.sum(s, axis=0, keepdims=True), axis=1, keepdims=True)

    before = alpha = None
    for k in range(ITERS):
        r = [source[t] if k == 0 else rref[t] for t in range(2)]
        w = []
        for t in range(2):
            v = r[t]
            n = ax[t] * xp(v) + xm(ax[t] * v)
            n = n + (ay[t] * lanes(v, 127) + lanes(ay[t] * v, 1))
            w.append(center[t] * v - (n + az * r[1 - t]))
        rr, below = total(r, r), total(r, w)
        if k > 0:
            beta = rr / before
            below = below - beta * (rr / alpha)
        alpha = rr / below
        before = rr
        for t in range(2):
            d, image = (r[t], w[t]) if k == 0 else (r[t] + beta * dref[t], w[t] + beta * sref[t])
            eref[t] = alpha * d if k == 0 else eref[t] + alpha * d
            if k < ITERS - 1:
                dref[t] = d
                sref[t] = image
                rref[t] = r[t] - alpha * image


def coarse_kernel(boxes, gathered, e2, dref, sref, rref, eref, ordered):
    box = my_place()[1]
    groups = boxes // 8

    def load(t, at):
        return jnp.stack([gathered[t, pl.ds(2 * g + at, 8, stride=2 * groups), :] for g in range(groups)])

    coarse_solve([load(t, 0) for t in range(2)], [load(t, 1) for t in range(2)], dref, sref, rref, eref)
    for t in range(2):
        ordered[t, 0:8] = jnp.zeros((8, 128), F32)
        ordered[t, 8 + boxes :] = jnp.zeros((8, 128), F32)
        for g in range(groups):
            ordered[t, pl.ds(8 + g, 8, stride=groups), :] = eref[t, g]
    near = [ordered[t, pl.ds(7 + box, 8), :] for t in range(2)]
    spread = one_hot((128, 512), lambda i, j: jnp.logical_and(((j >> 7) * 32) + ((j & 127) >> 1) == i, (j & 127) < 64))
    fine = [matmul(e, spread) for e in near]
    row = iota((8, 128), 0)
    for i in range(N2):
        cell, k = (i // 2) // 4, (i // 2) % 4
        low, high = (f[cell : cell + 1, 128 * k : 128 * k + 128] for f in fine)
        e2[i] = jnp.where(row < 2, low, jnp.where(row < 4, high, 0.0))


def after_kernel(compact, black, gathered, first, second):
    del gathered
    odd = my_place()[1] & 1
    for out, right in ((first, odd), (second, 1 - odd)):
        out[0:4] = compact[...]
        start = H0 + right * (32 - H0)
        for k in range(H0):
            for half in range(2):
                out[4 + 2 * k + half] = black[start + k, :, 128 * half : 128 * half + 128]


def last_kernel(*refs):
    names = ("e2", "first", "second", "own2", "v1", "f1", "ax1", "ay1", "az1", "inv1", "ax2", "ay2", "az2", "inv2")
    given = dict(zip(names, refs))
    refs = refs[len(names) :]
    level0 = dict(zip(PACKED, refs))
    refs = refs[len(PACKED) :]
    out_v, out_r, vR, vB, v1, v2, f2, wide, e0 = refs
    slab, box = my_place()
    e2, first, second, own2 = given["e2"], given["first"], given["second"], given["own2"]
    swapped = (box & 1) == 1

    def received(side, k, count):
        one, two = (first, second) if side == 0 else (second, first)
        return jnp.where(swapped, two[k : k + count], one[k : k + count])

    v2[8:16] = own2[0:8]
    f2[8:16] = own2[8:16]
    quarter = jnp.logical_and(iota((8, 128), 0) < 4, iota((8, 128), 1) < 64)
    for side, at in ((0, 0), (1, 16)):
        four = received(side, 0, 4)
        for k in range(4):
            for ref, plane in ((v2, four[k]), (f2, pltpu.roll(four[k], 64, 1))):
                ref[at + 2 * k] = jnp.where(quarter, plane, 0.0)
                ref[at + 2 * k + 1] = jnp.where(quarter, pltpu.roll(plane, 4, 0), 0.0)
    for i in range(N2):
        v2[i] = v2[i] + e2[i]
    two = (f2, given["ax2"], given["ay2"], given["az2"], given["inv2"])
    for k in range(2):
        sweep_plain(v2, *two, 0, 0, 1 + 2 * k, N2 - 1 - 2 * k)
        sweep_plain(v2, *two, 1, 0, 2 + 2 * k, N2 - 2 - 2 * k)

    packed = jnp.concatenate([v2[4 + j, 0:4, :] for j in range(16)], axis=0)
    fine = matmul(packed, one_hot((128, 128), lambda i, j: (j >> 1) == i))
    wide[pl.ds(0, 64, stride=2), :] = fine
    wide[pl.ds(1, 64, stride=2), :] = fine
    for i in range(6, N1 - 6):
        j = (i + 3) // 2 - 4
        v1[i] = given["v1"][i] + wide[8 * j : 8 * j + 8, :]
    one = (given["f1"], given["ax1"], given["ay1"], given["az1"], given["inv1"])
    for k in range(2):
        sweep_plain(v1, *one, 0, 1, 7 + 2 * k, N1 - 7 - 2 * k)
        sweep_plain(v1, *one, 1, 1, 8 + 2 * k, N1 - 8 - 2 * k)

    double = one_hot((128, 256), lambda i, j: (j >> 1) == i)
    e0[...] = matmul(v1[10:32].reshape(176, 128), double).reshape(22, 8, 256)
    lv = dict(level0, vR=vR, vB=vB)

    black = level0["vB"]

    def correct(j, carry):
        e = e0[j]
        vB[2 * j - 1] = black[2 * j - 1] + e
        vB[2 * j] = black[2 * j] + e
        return carry

    lax.fori_loop(3, 19, correct, 0, unroll=4)
    for side, at in ((0, 0), (1, H0 + 32)):
        for k in range(H0):
            for half in range(2):
                lanes = slice(128 * half, 128 * half + 128)
                vB[at + k, :, lanes] = received(side, 4 + 2 * k + half, 1)[0] + e0[(at + k + 1) // 2, :, lanes]
    for k in range(2):
        sweep_packed(lv, True, 1 + 2 * k, N0 - 1 - 2 * k)
        sweep_packed(lv, False, 2 + 2 * k, N0 - 2 - 2 * k)


    def finish(i, odd, carry):
        x = i - H0
        red, black, p = residual_packed(lv, i, odd)
        for out, a, b in ((out_v, vR[i], vB[i]), (out_r, red, black)):
            for at, whole in ((0, jnp.where(p, a, b)), (1, jnp.where(p, b, a))):
                part = jnp.where(slab == 0, whole[0:4], whole[4:8])
                for half in range(2):
                    out[slab_rows(x, half, at), :] = part[:, 128 * half : 128 * half + 128]
        return carry

    planes(H0, H0 + 32, FINISH, finish)


def call(kernel, outs, scratch, *args, limit=12):
    vmem = pl.BlockSpec(memory_space=pltpu.VMEM)
    return pl.pallas_call(
        kernel,
        out_shape=[jax.ShapeDtypeStruct(s, F32) for s in outs],
        in_specs=[vmem] * len(args),
        out_specs=[vmem] * len(outs),
        scratch_shapes=[pltpu.VMEM(s, F32) for s in scratch],
        compiler_params=pltpu.CompilerParams(vmem_limit_bytes=limit * 1024 * 1024),
    )(*args)


def edges(*args):
    return pl.pallas_call(
        edge_kernel,
        out_shape=jax.ShapeDtypeStruct((EDGE, 256), F32),
        in_specs=[pl.BlockSpec(memory_space=pl.ANY)] * 3,
        out_specs=pl.BlockSpec(memory_space=pltpu.VMEM),
        scratch_shapes=[pltpu.VMEM((128, 128), F32)] * 3 + [pltpu.SemaphoreType.DMA((3,))],
        compiler_params=pltpu.CompilerParams(vmem_limit_bytes=60 * 1024 * 1024),
    )(*[a.reshape(8, 64, 128) for a in args])


def by_tiles(a):
    return a.reshape(8, 4, 8, 2, 128).transpose(0, 1, 3, 2, 4).reshape(512, 128)


def from_tiles(a):
    return a.reshape(8, 4, 2, 8, 128).transpose(0, 1, 3, 2, 4).reshape(8, 32, 256)


def exchange(first, second):
    boxes = lax.axis_size("box")
    odd = [(i, i + 1) for i in range(1, boxes - 1, 2)]
    even = [(i, i + 1) for i in range(0, boxes - 1, 2)]
    return [lax.ppermute(x, "box", p + [(j, i) for i, j in p]) for x, p in ((first, odd), (second, even))]


def body(pressure_guess, right_side, coefficient):
    boxes = lax.axis_size("box")
    flat = [by_tiles(a) for a in (pressure_guess, right_side, coefficient)]
    first = edges(*flat)
    low, high, second = call(pack_kernel, [(16 * ROWS, 256)] * 2 + [(EDGE, 256)], [], *flat)
    first, second = exchange(first, second)
    low, high = lax.all_gather(low, "slab"), lax.all_gather(high, "slab")
    halo = lax.all_gather(jnp.stack([first, second]), "slab")

    plane = (N0, 8, 256)
    fine = call(
        functools.partial(fine_kernel, boxes),
        [plane] * len(PACKED) + [(36, 8, 128), (SEND1, 8, 128), (SEND1, 8, 128), (8, 128)],
        [plane] * 3 + [(16, 8, 256)] * 2 + [(64, 128)],
        low,
        high,
        halo,
    )
    level0 = fine[: len(PACKED)]
    own, first, second, bottom = fine[len(PACKED) :]
    first, second = exchange(first, second)

    one, two = (N1, 8, 128), (N2, 8, 128)
    *levels, send, compact, message = call(
        functools.partial(middle_kernel, boxes),
        [one] * 6 + [two] * 4 + [(16, 8, 128), (4, 8, 128), (2 * boxes, 128)],
        [two] * 3 + [one, (128, 128)],
        own,
        first,
        second,
        bottom,
    )
    spread = lax.all_to_all(message.reshape(boxes, 2, 128), "box", 0, 0).reshape(2 * boxes, 128)
    first, second = exchange(*call(after_kernel, [(SEND2, 8, 128)] * 2, [], compact, level0[0], spread))
    gathered = lax.all_gather(spread, "slab")
    (e2,) = call(
        functools.partial(coarse_kernel, boxes),
        [two],
        [(2, boxes // 8, 8, 128)] * 4 + [(2, boxes + 16, 128)],
        gathered,
    )
    pressure, residual = call(
        last_kernel,
        [(512, 128)] * 2,
        [plane, plane, one, two, two, (128, 128), (22, 8, 256)],
        e2,
        first,
        second,
        send,
        *levels,
        *level0,
    )
    return from_tiles(pressure), from_tiles(residual)


def solution(mesh):
    split = P("slab", "box", None)
    return jax.shard_map(body, mesh=mesh, in_specs=(split,) * 3, out_specs=(split,) * 2, check_vma=False)
```

```python
import functools

import jax
import jax.numpy as jnp
from jax import lax
from jax.experimental import pallas as pl
from jax.experimental.pallas import tpu as pltpu
from jax.sharding import PartitionSpec as P

ITERS = 8
F32 = jnp.float32
BF16 = jnp.bfloat16

H0 = 5
H1 = 12
N0 = 32 + 2 * H0
N1 = 16 + 2 * (H1 + 1)
N2 = 24
ROWS = 20
EDGE = 96
EDGE_F, EDGE_V = 8 * H0, 16 * H0 - 8
SWEEP, FACES, RESTRICT, FINISH = 99, 99, 16, 99
SEND1 = H1 + (H1 + 1) + 4
SEND2 = 4 + 2 * H0


def matmul(x, m):
    high = x.astype(BF16)
    rest = x - high.astype(F32)
    mid = rest.astype(BF16)
    low = (rest - mid.astype(F32)).astype(BF16)
    dot = functools.partial(jnp.dot, preferred_element_type=F32)
    return dot(high, m) + (dot(mid, m) + dot(low, m))


def one_hot(shape, rule):
    i = lax.broadcasted_iota(jnp.int32, shape, 0)
    j = lax.broadcasted_iota(jnp.int32, shape, 1)
    return rule(i, j).astype(F32).astype(BF16)


def iota(shape, axis):
    return lax.broadcasted_iota(jnp.int32, shape, axis)


def up(v, axis):
    return pltpu.roll(v, v.shape[axis] - 1, axis)


def down(v, axis):
    return pltpu.roll(v, 1, axis)


def planes(first, last, unroll, step, carry=0):
    def pair(k, carry):
        i = first + 2 * k
        return step(i + 1, (first + 1) % 2, step(i, first % 2, carry))

    count = (last - first) // 2
    if unroll < count:
        return lax.fori_loop(0, count, pair, carry, unroll=unroll)
    for k in range(count):
        carry = pair(k, carry)
    return carry


def my_place():
    return lax.axis_index("slab"), lax.axis_index("box")


def slab_rows(x, half, odd):
    return pl.ds((x // 8) * 16 + half * 8 + x % 8 + 64 * odd, 4, stride=128)


def pack_plane(g, r, c, x, rows, even_y, out, b_at, f_at, v_at):
    p0 = even_y if x % 2 == 0 else jnp.logical_not(even_y)
    for half in range(2):
        lanes = slice(128 * half, 128 * half + 128)
        even, odd = rows(half, 0), rows(half, 1)
        out[b_at : b_at + 4, lanes] = c[even, :]
        out[b_at + 4 : b_at + 8, lanes] = c[odd, :]
        if f_at is not None:
            fe, fo = r[even, :], r[odd, :]
            out[f_at : f_at + 4, lanes] = jnp.where(p0, fe, fo)
            out[f_at + 4 : f_at + 8, lanes] = jnp.where(p0, fo, fe)
        out[v_at : v_at + 4, lanes] = jnp.where(p0, g[odd, :], g[even, :])


def pack_edge(parts, right, rows, even_y, out):
    for k in range(H0):
        x = 32 - H0 + k if right else k
        f_at = k - 1 if right else k
        f_at = EDGE_F + 8 * f_at if 0 <= f_at < H0 - 1 else None
        pack_plane(*parts, x, functools.partial(rows, x), even_y, out, 8 * k, f_at, EDGE_V + 4 * k)
    out[EDGE_V + 4 * H0 :, :] = jnp.zeros((EDGE - EDGE_V - 4 * H0, 256), F32)


def pack_kernel(g, r, c, low, high, second):
    even_y = (iota((4, 128), 1) & 1) == 0
    swapped = (my_place()[1] & 1) == 1

    @pl.when(swapped)
    def _():
        pack_edge((g, r, c), False, slab_rows, even_y, second)

    @pl.when(jnp.logical_not(swapped))
    def _():
        pack_edge((g, r, c), True, slab_rows, even_y, second)

    for x in range(32):
        out, base = (low, x * ROWS) if x < 16 else (high, (x - 16) * ROWS)
        pack_plane(g, r, c, x, functools.partial(slab_rows, x), even_y, out, base, base + 8, base + 16)


def edge_kernel(g_hbm, r_hbm, c_hbm, first, *scratch):
    parts, sem = scratch[0:3], scratch[3]
    odd = my_place()[1] & 1
    at = pl.multiple_of(48 * odd, 16)
    copies = [
        pltpu.make_async_copy(source.at[:, pl.ds(at, 16), :], target.reshape(8, 16, 128), sem.at[k])
        for k, (source, target) in enumerate(zip((g_hbm, r_hbm, c_hbm), parts))
    ]
    for copy in copies:
        copy.start()
    for copy in copies:
        copy.wait()
    even_y = (iota((4, 128), 1) & 1) == 0

    def rows(x, half, second_z):
        return pl.ds(half * 8 + x % 8 + 16 * second_z, 4, stride=32)

    @pl.when(odd == 1)
    def _():
        pack_edge(parts, True, rows, even_y, first)

    @pl.when(odd == 0)
    def _():
        pack_edge(parts, False, rows, even_y, first)


def parity(odd):
    return ((iota((8, 256), 1) + odd + 1) & 1) == 0


def nsum_packed(lv, v, xa, xb, ya, yb, i, p):
    here = v[i]
    t = xa[i] * v[i + 1] + xb[i - 1] * v[i - 1]
    t = t + (ya[i] * up(here, 1) + down(yb[i] * here, 1))
    cross = lv["c"][i]
    z = jnp.where(p, down(cross * here, 0), cross * up(here, 0))
    return t + (lv["s"][i] * here + z)


def sweep_packed(lv, red, first, last):
    def step(i, odd, carry):
        p = parity(odd)
        if red:
            n = nsum_packed(lv, lv["vB"], lv["xR"], lv["xB"], lv["yR"], lv["yB"], i, p)
            lv["vR"][i] = (lv["fR"][i] + n) * lv["iR"][i]
        else:
            p = jnp.logical_not(p)
            n = nsum_packed(lv, lv["vR"], lv["xB"], lv["xR"], lv["yB"], lv["yR"], i, p)
            lv["vB"][i] = (lv["fB"][i] + n) * lv["iB"][i]
        return carry

    planes(first, last, SWEEP, step)


def residual_packed(lv, i, odd):
    p = parity(odd)
    n = nsum_packed(lv, lv["vB"], lv["xR"], lv["xB"], lv["yR"], lv["yB"], i, p)
    r_red = lv["fR"][i] - (lv["cR"][i] * lv["vR"][i] - n)
    q = jnp.logical_not(p)
    n = nsum_packed(lv, lv["vR"], lv["xB"], lv["xR"], lv["yB"], lv["yR"], i, q)
    r_black = lv["fB"][i] - (lv["cB"][i] * lv["vB"][i] - n)
    return r_red, r_black, p


PACKED = ("vB", "fR", "fB", "xR", "xB", "yR", "yB", "s", "c", "iR", "iB", "cR", "cB")


FINE = PACKED + ("bE", "bO")


def stack(parts, at, i, out):
    for t in range(2):
        out[i, 4 * t : 4 * t + 4, :] = parts[t][at : at + 4, :]


def merge(parts, at, i, low, high):
    low_half = iota((8, 256), 0) < 4
    a, b = (part[at : at + 8, :] for part in parts)
    low[i] = jnp.where(low_half, a, pltpu.roll(b, 4, 0))
    high[i] = jnp.where(low_half, pltpu.roll(a, 4, 0), b)


def x_values(lv, i):
    return 0.5 * (lv["bE"][i] + lv["bE"][i + 1]), 0.5 * (lv["bO"][i] + lv["bO"][i + 1])


def x_faces(lv, i, p):
    fxe, fxo = x_values(lv, i)
    lv["xR"][i] = jnp.where(p, fxe, fxo)
    lv["xB"][i] = jnp.where(p, fxo, fxe)
    return fxe, fxo


def faces(lv, i, before, inside=None):
    row, lane = iota((8, 256), 0), iota((8, 256), 1)
    top, bot = row == 7, row == 0
    end, begin = lane == 255, lane == 0
    p = parity(i % 2)
    e, o = lv["bE"][i], lv["bO"][i]
    fxe, fxo = x_faces(lv, i, p)
    fye = 0.5 * (e + jnp.where(end, 0.0, up(e, 1)))
    fyo = 0.5 * (o + jnp.where(end, 0.0, up(o, 1)))
    gye = 0.5 * (e + jnp.where(begin, 0.0, down(e, 1)))
    gyo = 0.5 * (o + jnp.where(begin, 0.0, down(o, 1)))
    yr, yb = jnp.where(p, fye, fyo), jnp.where(p, fyo, fye)
    lv["yR"][i] = jnp.where(end, 0.0, yr)
    lv["yB"][i] = jnp.where(end, 0.0, yb)
    s = 0.5 * (e + o)
    above = 0.5 * (o + jnp.where(top, 0.0, up(e, 0)))
    below = 0.5 * (e + jnp.where(bot, 0.0, down(o, 0)))
    lv["s"][i] = s
    lv["c"][i] = jnp.where(top, 0.0, above)
    ce = fye + gye + (s + below) + (fxe + before[0])
    co = fyo + gyo + (s + above) + (fxo + before[1])
    cr, cb = jnp.where(p, ce, co), jnp.where(p, co, ce)
    lv["cR"][i] = cr
    lv["cB"][i] = cb
    ir, ib = 1.0 / cr, 1.0 / cb
    lv["iR"][i] = ir if inside is None else jnp.where(inside, ir, 0.0)
    lv["iB"][i] = ib if inside is None else jnp.where(inside, ib, 0.0)
    return fxe, fxo


def own_kernel(lo, hi, *refs):
    lv = dict(zip(FINE, refs))
    coarse, bottom, pair_b, tmp = refs[len(FINE) :]
    for x in range(32):
        source, base = (lo, x * ROWS) if x < 16 else (hi, (x - 16) * ROWS)
        parts = source.at[0], source.at[1]
        merge(parts, base, H0 + x, lv["bE"], lv["bO"])
        merge(parts, base + 8, H0 + x, lv["fR"], lv["fB"])
        stack(parts, base + 16, H0 + x, lv["vB"])
    before = x_values(lv, H0)
    for i in range(H0 + 1, H0 + 31):
        before = faces(lv, i, before)

    bE, bO = lv["bE"], lv["bO"]
    for j in range(16):
        i = H0 + 2 * j
        pair_b[j] = (bE[i] + bO[i]) + (bE[i + 1] + bO[i + 1])
    halve = one_hot((256, 128), lambda i, j: (i >> 1) == j)
    coarse[0:16] = (0.125 * matmul(pair_b[...].reshape(128, 256), halve)).reshape(16, 8, 128)
    for k in range(8):
        tmp[8 * k : 8 * k + 8, :] = coarse[2 * k] + coarse[2 * k + 1]
    summed = tmp[pl.ds(0, 32, stride=2), :] + tmp[pl.ds(1, 32, stride=2), :]
    halve = one_hot((128, 128), lambda i, j: (i >> 1) == j)
    coarse[16:20] = (0.125 * matmul(summed, halve)).reshape(4, 8, 128)
    bottom[...] = bottom_row([coarse[16 + k] + pltpu.roll(coarse[16 + k], 4, 0) for k in range(4)])


def fine_kernel(boxes, halo, coarse, *refs):
    refs = refs[len(FINE) :]
    lv = dict(zip(FINE, refs))
    f1, first, second, vR, pair_r = refs[len(FINE) :]
    lv["vR"] = vR
    box = my_place()[1]
    odd = box & 1
    for side, at in ((odd, 0), (1 - odd, H0 + 32)):
        parts = halo.at[0, side], halo.at[1, side]
        for k in range(H0):
            merge(parts, 8 * k, at + k, lv["bE"], lv["bO"])
            stack(parts, EDGE_V + 4 * k, at + k, lv["vB"])
        for k in range(H0 - 1):
            merge(parts, EDGE_F + 8 * k, (1 if at == 0 else at) + k, lv["fR"], lv["fB"])
    before = x_faces(lv, 0, parity(0))
    for i in range(1, H0 + 1):
        before = faces(lv, i, before, None if i == H0 else box > 0)
    before = x_values(lv, H0 + 30)
    for i in range(H0 + 31, N0 - 1):
        before = faces(lv, i, before, None if i == H0 + 31 else box < boxes - 1)

    for k in range(2):
        sweep_packed(lv, True, 1 + 2 * k, N0 - 1 - 2 * k)
        sweep_packed(lv, False, 2 + 2 * k, N0 - 2 - 2 * k)
    for j in range(16):
        i = H0 + 2 * j
        a, b, _ = residual_packed(lv, i, H0 % 2)
        c, d, _ = residual_packed(lv, i + 1, (H0 + 1) % 2)
        pair_r[j] = (a + b) + (c + d)
    halve = one_hot((256, 128), lambda i, j: (i >> 1) == j)
    f1[...] = (0.125 * matmul(pair_r[...].reshape(128, 256), halve)).reshape(16, 8, 128)

    for out, right in ((first, odd), (second, 1 - odd)):
        out[0:H1] = f1[pl.ds(right * (16 - H1), H1)]
        out[H1 : 2 * H1 + 1] = coarse[pl.ds(right * (15 - H1), H1 + 1)]
        out[2 * H1 + 1 :] = coarse[16:20]


def bottom_row(pairs):
    total = None
    for k, plane in enumerate(pairs):
        spread = one_hot((128, 128), lambda i, j, k=k: jnp.logical_and((i >> 1) + 32 * k == j, i < 64))
        part = matmul(plane, spread)
        total = part if total is None else total + part
    low, high = total[0:1] + total[1:2], total[2:3] + total[3:4]
    row = 0.125 * jnp.where(my_place()[0] == 0, low, high)
    return jnp.broadcast_to(row, (8, 128))


def level_faces(b, ax, ay, az, inv, n, factor, depth, width, inside):
    row, lane = iota((8, 128), 0), iota((8, 128), 1)
    top, bot = row == depth - 1, row == 0
    end, begin = lane == width - 1, lane == 0
    cell = jnp.logical_and(row < depth, lane < width)
    ax[0] = factor * (b[0] + b[1])

    def step(i, odd, before):
        v = b[i]
        fx = factor * (v + b[i + 1])
        ax[i] = fx
        fy = factor * (v + jnp.where(end, 0.0, up(v, 1)))
        gy = factor * (v + jnp.where(begin, 0.0, down(v, 1)))
        fz = factor * (v + jnp.where(top, 0.0, up(v, 0)))
        gz = factor * (v + jnp.where(bot, 0.0, down(v, 0)))
        ay[i] = jnp.where(end, 0.0, fy)
        az[i] = jnp.where(top, 0.0, fz)
        center = (fz + gz) + (fx + before) + (fy + gy)
        inv[i] = jnp.where(jnp.logical_and(cell, inside(i)), 1.0 / center, 0.0)
        return fx

    planes(1, n - 1, 99, step, ax[0])


def nsum_plain(v, ax, ay, az, i):
    here = v[i]
    t = ax[i] * v[i + 1] + ax[i - 1] * v[i - 1]
    t = t + (ay[i] * up(here, 1) + down(ay[i] * here, 1))
    return t + (az[i] * up(here, 0) + down(az[i] * here, 0))


def colour(odd):
    return ((iota((8, 128), 0) + iota((8, 128), 1) + odd) & 1) == 0


def sweep_plain(v, f, ax, ay, az, inv, odd, shift, first, last):
    def step(i, plane_odd, carry):
        cells = colour((plane_odd + shift + odd) % 2)
        v[i] = jnp.where(cells, (f[i] + nsum_plain(v, ax, ay, az, i)) * inv[i], v[i])
        return carry

    planes(first, last, 99, step)


def first_plain(v, f, inv, shift, first, last):
    def step(i, plane_odd, carry):
        v[i] = jnp.where(colour((plane_odd + shift) % 2), f[i] * inv[i], 0.0)
        return carry

    planes(first, last, 99, step)


def residual_plain(v, f, ax, ay, az, center, i):
    return f[i] - (center * v[i] - nsum_plain(v, ax, ay, az, i))


def center_plain(b, ax, i, factor, depth, width):
    row, lane = iota((8, 128), 0), iota((8, 128), 1)
    v = b[i]
    fy = jnp.where(lane == width - 1, 0.0, up(v, 1)) + jnp.where(lane == 0, 0.0, down(v, 1))
    fz = jnp.where(row == depth - 1, 0.0, up(v, 0)) + jnp.where(row == 0, 0.0, down(v, 0))
    return factor * (4.0 * v + fy + fz) + (ax[i] + ax[i - 1])


def middle_kernel(boxes, source, coarse, first, second, bottom, v1, f1, ax1, ay1, az1, inv1, ax2, ay2, az2, inv2, send, compact, message, v2, f2, b2, b1, tmp):
    box = my_place()[1]
    w = H1 + 1
    swapped = (box & 1) == 1

    def received(k, count):
        one, two = first[k : k + count], second[k : k + count]
        return jnp.where(swapped, two, one), jnp.where(swapped, one, two)

    left, right = received(H1, w)
    b1[0:w] = left
    b1[w : w + 16] = coarse[0:16]
    b1[w + 16 :] = right
    left, right = received(0, H1)
    f1[0:1] = jnp.zeros((1, 8, 128), F32)
    f1[1 : 1 + H1] = left
    f1[w : w + 16] = source[...]
    f1[w + 16 : w + 16 + H1] = right
    f1[N1 - 1 :] = jnp.zeros((1, 8, 128), F32)
    left, right = received(H1 + w, 4)
    b2[...] = jnp.zeros(b2.shape, F32)
    for at, part in ((0, left), (8, coarse[16:20]), (16, right)):
        for k in range(8):
            b2[at + k, 0:4, :] = part[k // 2, 4 * (k % 2) : 4 * (k % 2) + 4]
    v1[...] = jnp.zeros(v1.shape, F32)
    v2[...] = jnp.zeros(v2.shape, F32)
    f2[...] = jnp.zeros(f2.shape, F32)

    def within(size, width):
        def inside(i):
            x = box * size - width + i
            return jnp.logical_and(x >= 0, x < boxes * size)

        return inside

    k1, k2 = 0.5 * 0.25, 0.5 * 0.25**2
    level_faces(b1, ax1, ay1, az1, inv1, N1, k1, 8, 128, within(16, w))
    level_faces(b2, ax2, ay2, az2, inv2, N2, k2, 4, 64, within(8, 8))

    one = (f1, ax1, ay1, az1, inv1)
    first_plain(v1, f1, inv1, 1, 1, N1 - 1)
    sweep_plain(v1, *one, 1, 1, 2, N1 - 2)
    sweep_plain(v1, *one, 0, 1, 3, N1 - 3)
    sweep_plain(v1, *one, 1, 1, 4, N1 - 4)

    def restrict(j, carry):
        i = 5 + 2 * j
        parts = [residual_plain(v1, *one[:4], center_plain(b1, ax1, k, k1, 8, 128), k) for k in (i, i + 1)]
        tmp[8 * j : 8 * j + 8, :] = parts[0] + parts[1]
        return carry

    for j in range(16):
        restrict(j, 0)
    summed = tmp[pl.ds(0, 64, stride=2), :] + tmp[pl.ds(1, 64, stride=2), :]
    restricted = 0.125 * matmul(summed, one_hot((128, 128), lambda i, j: (i >> 1) == j))
    for j in range(16):
        f2[4 + j, 0:4, :] = restricted[4 * j : 4 * j + 4]

    two = (f2, ax2, ay2, az2, inv2)
    first_plain(v2, f2, inv2, 0, 4, 20)
    sweep_plain(v2, *two, 1, 0, 5, 19)
    sweep_plain(v2, *two, 0, 0, 6, 18)
    sweep_plain(v2, *two, 1, 0, 7, 17)
    send[0:8] = v2[8:16]
    send[8:16] = f2[8:16]
    for k in range(4):
        both = [pltpu.roll(ref[9 + 2 * k], 4, 0) + ref[8 + 2 * k] for ref in (v2, f2)]
        compact[k] = both[0] + pltpu.roll(both[1], 64, 1)

    pairs = []
    for k in range(4):
        parts = [
            residual_plain(v2, *two[:4], center_plain(b2, ax2, i, k2, 4, 64), i)
            for i in (8 + 2 * k, 9 + 2 * k)
        ]
        pairs.append(parts[0] + parts[1])
    rows = jnp.where((iota((8, 128), 0) & 1) == 0, bottom_row(pairs), bottom[...])
    for k in range(message.shape[0] // 8):
        message[8 * k : 8 * k + 8, :] = rows


def coarse_solve(source, coefficient, dref, sref, rref, eref):
    shape = source[0].shape
    groups = shape[0]
    group, row, lane = (iota(shape, k) for k in range(3))
    factor = 0.5 * 0.25**3
    last = jnp.logical_and(jnp.logical_and(group == groups - 1, row == 7), lane >= 96)
    first = jnp.logical_and(jnp.logical_and(group == 0, row == 0), lane < 32)
    inner_hi, inner_lo = lane < 96, lane >= 32
    end, begin = (lane & 31) == 31, (lane & 31) == 0

    def lanes(v, shift):
        return pltpu.roll(v.reshape(8 * groups, 128), shift, 1).reshape(shape)

    def xp(v):
        a = lanes(v, 96)
        return jnp.where(inner_hi, a, jnp.concatenate([a[1:], up(a[0], 0)[None]], axis=0))

    def xm(v):
        a = lanes(v, 32)
        return jnp.where(inner_lo, a, jnp.concatenate([down(a[groups - 1], 0)[None], a[:-1]], axis=0))

    ax, ay, center = [], [], []
    az = factor * (coefficient[0] + coefficient[1])
    for b in coefficient:
        fx = factor * (b + jnp.where(last, 0.0, xp(b)))
        gx = factor * (b + jnp.where(first, 0.0, xm(b)))
        fy = factor * (b + jnp.where(end, 0.0, lanes(b, 127)))
        gy = factor * (b + jnp.where(begin, 0.0, lanes(b, 1)))
        ax.append(jnp.where(last, 0.0, fx))
        ay.append(jnp.where(end, 0.0, fy))
        center.append((factor * b + az) + (fx + gx) + (fy + gy))

    def total(u, w):
        s = jnp.sum(u[0] * w[0] + u[1] * w[1], axis=0)
        return jnp.sum(jnp.sum(s, axis=0, keepdims=True), axis=1, keepdims=True)

    before = alpha = None
    for k in range(ITERS):
        r = [source[t] if k == 0 else rref[t] for t in range(2)]
        w = []
        for t in range(2):
            v = r[t]
            n = ax[t] * xp(v) + xm(ax[t] * v)
            n = n + (ay[t] * lanes(v, 127) + lanes(ay[t] * v, 1))
            w.append(center[t] * v - (n + az * r[1 - t]))
        rr, below = total(r, r), total(r, w)
        if k > 0:
            beta = rr / before
            below = below - beta * (rr / alpha)
        alpha = rr / below
        before = rr
        for t in range(2):
            d, image = (r[t], w[t]) if k == 0 else (r[t] + beta * dref[t], w[t] + beta * sref[t])
            eref[t] = alpha * d if k == 0 else eref[t] + alpha * d
            if k < ITERS - 1:
                dref[t] = d
                sref[t] = image
                rref[t] = r[t] - alpha * image


def coarse_kernel(boxes, gathered, e2, dref, sref, rref, eref, ordered):
    box = my_place()[1]
    groups = boxes // 8

    def load(t, at):
        return jnp.stack([gathered[t, pl.ds(2 * g + at, 8, stride=2 * groups), :] for g in range(groups)])

    coarse_solve([load(t, 0) for t in range(2)], [load(t, 1) for t in range(2)], dref, sref, rref, eref)
    for t in range(2):
        ordered[t, 0:8] = jnp.zeros((8, 128), F32)
        ordered[t, 8 + boxes :] = jnp.zeros((8, 128), F32)
        for g in range(groups):
            ordered[t, pl.ds(8 + g, 8, stride=groups), :] = eref[t, g]
    near = [ordered[t, pl.ds(7 + box, 8), :] for t in range(2)]
    spread = one_hot((128, 512), lambda i, j: jnp.logical_and(((j >> 7) * 32) + ((j & 127) >> 1) == i, (j & 127) < 64))
    fine = [matmul(e, spread) for e in near]
    row = iota((8, 128), 0)
    for i in range(N2):
        cell, k = (i // 2) // 4, (i // 2) % 4
        low, high = (f[cell : cell + 1, 128 * k : 128 * k + 128] for f in fine)
        e2[i] = jnp.where(row < 2, low, jnp.where(row < 4, high, 0.0))


def after_kernel(compact, black, gathered, first, second):
    del gathered
    odd = my_place()[1] & 1
    for out, right in ((first, odd), (second, 1 - odd)):
        out[0:4] = compact[...]
        start = H0 + right * (32 - H0)
        for k in range(H0):
            for half in range(2):
                out[4 + 2 * k + half] = black[start + k, :, 128 * half : 128 * half + 128]


def last_kernel(*refs):
    names = ("e2", "first", "second", "own2", "v1", "f1", "ax1", "ay1", "az1", "inv1", "ax2", "ay2", "az2", "inv2")
    given = dict(zip(names, refs))
    refs = refs[len(names) :]
    level0 = dict(zip(PACKED, refs))
    refs = refs[len(PACKED) :]
    out_v, out_r, vR, vB, v1, v2, f2, wide, e0 = refs
    slab, box = my_place()
    e2, first, second, own2 = given["e2"], given["first"], given["second"], given["own2"]
    swapped = (box & 1) == 1

    def received(side, k, count):
        one, two = (first, second) if side == 0 else (second, first)
        return jnp.where(swapped, two[k : k + count], one[k : k + count])

    v2[8:16] = own2[0:8]
    f2[8:16] = own2[8:16]
    quarter = jnp.logical_and(iota((8, 128), 0) < 4, iota((8, 128), 1) < 64)
    for side, at in ((0, 0), (1, 16)):
        four = received(side, 0, 4)
        for k in range(4):
            for ref, plane in ((v2, four[k]), (f2, pltpu.roll(four[k], 64, 1))):
                ref[at + 2 * k] = jnp.where(quarter, plane, 0.0)
                ref[at + 2 * k + 1] = jnp.where(quarter, pltpu.roll(plane, 4, 0), 0.0)
    for i in range(N2):
        v2[i] = v2[i] + e2[i]
    two = (f2, given["ax2"], given["ay2"], given["az2"], given["inv2"])
    for k in range(2):
        sweep_plain(v2, *two, 0, 0, 1 + 2 * k, N2 - 1 - 2 * k)
        sweep_plain(v2, *two, 1, 0, 2 + 2 * k, N2 - 2 - 2 * k)

    packed = jnp.concatenate([v2[4 + j, 0:4, :] for j in range(16)], axis=0)
    fine = matmul(packed, one_hot((128, 128), lambda i, j: (j >> 1) == i))
    wide[pl.ds(0, 64, stride=2), :] = fine
    wide[pl.ds(1, 64, stride=2), :] = fine
    for i in range(6, N1 - 6):
        j = (i + 3) // 2 - 4
        v1[i] = given["v1"][i] + wide[8 * j : 8 * j + 8, :]
    one = (given["f1"], given["ax1"], given["ay1"], given["az1"], given["inv1"])
    for k in range(2):
        sweep_plain(v1, *one, 0, 1, 7 + 2 * k, N1 - 7 - 2 * k)
        sweep_plain(v1, *one, 1, 1, 8 + 2 * k, N1 - 8 - 2 * k)

    double = one_hot((128, 256), lambda i, j: (j >> 1) == i)
    e0[...] = matmul(v1[10:32].reshape(176, 128), double).reshape(22, 8, 256)
    lv = dict(level0, vR=vR, vB=vB)

    black = level0["vB"]

    def correct(j, carry):
        e = e0[j]
        vB[2 * j - 1] = black[2 * j - 1] + e
        vB[2 * j] = black[2 * j] + e
        return carry

    lax.fori_loop(3, 19, correct, 0, unroll=4)
    for side, at in ((0, 0), (1, H0 + 32)):
        for k in range(H0):
            for half in range(2):
                lanes = slice(128 * half, 128 * half + 128)
                vB[at + k, :, lanes] = received(side, 4 + 2 * k + half, 1)[0] + e0[(at + k + 1) // 2, :, lanes]
    for k in range(2):
        sweep_packed(lv, True, 1 + 2 * k, N0 - 1 - 2 * k)
        sweep_packed(lv, False, 2 + 2 * k, N0 - 2 - 2 * k)


    def finish(i, odd, carry):
        x = i - H0
        red, black, p = residual_packed(lv, i, odd)
        for out, a, b in ((out_v, vR[i], vB[i]), (out_r, red, black)):
            for at, whole in ((0, jnp.where(p, a, b)), (1, jnp.where(p, b, a))):
                part = jnp.where(slab == 0, whole[0:4], whole[4:8])
                for half in range(2):
                    out[slab_rows(x, half, at), :] = part[:, 128 * half : 128 * half + 128]
        return carry

    planes(H0, H0 + 32, FINISH, finish)


def call(kernel, outs, scratch, *args, limit=12, aliases=()):
    vmem = pl.BlockSpec(memory_space=pltpu.VMEM)
    return pl.pallas_call(
        kernel,
        out_shape=[jax.ShapeDtypeStruct(s, F32) for s in outs],
        in_specs=[vmem] * len(args),
        out_specs=[vmem] * len(outs),
        input_output_aliases=dict(aliases),
        scratch_shapes=[pltpu.VMEM(s, F32) for s in scratch],
        compiler_params=pltpu.CompilerParams(vmem_limit_bytes=limit * 1024 * 1024),
    )(*args)


def edges(*args):
    return pl.pallas_call(
        edge_kernel,
        out_shape=jax.ShapeDtypeStruct((EDGE, 256), F32),
        in_specs=[pl.BlockSpec(memory_space=pl.ANY)] * 3,
        out_specs=pl.BlockSpec(memory_space=pltpu.VMEM),
        scratch_shapes=[pltpu.VMEM((128, 128), F32)] * 3 + [pltpu.SemaphoreType.DMA((3,))],
        compiler_params=pltpu.CompilerParams(vmem_limit_bytes=60 * 1024 * 1024),
    )(*[a.reshape(8, 64, 128) for a in args])


def by_tiles(a):
    return a.reshape(8, 4, 8, 2, 128).transpose(0, 1, 3, 2, 4).reshape(512, 128)


def from_tiles(a):
    return a.reshape(8, 4, 2, 8, 128).transpose(0, 1, 3, 2, 4).reshape(8, 32, 256)


def exchange(first, second):
    boxes = lax.axis_size("box")
    odd = [(i, i + 1) for i in range(1, boxes - 1, 2)]
    even = [(i, i + 1) for i in range(0, boxes - 1, 2)]
    return [lax.ppermute(x, "box", p + [(j, i) for i, j in p]) for x, p in ((first, odd), (second, even))]


def body(pressure_guess, right_side, coefficient):
    boxes = lax.axis_size("box")
    flat = [by_tiles(a) for a in (pressure_guess, right_side, coefficient)]
    first = edges(*flat)
    low, high, second = call(pack_kernel, [(16 * ROWS, 256)] * 2 + [(EDGE, 256)], [], *flat)
    first, second = exchange(first, second)
    low, high = lax.all_gather(low, "slab"), lax.all_gather(high, "slab")
    halo = lax.all_gather(jnp.stack([first, second]), "slab")

    plane = (N0, 8, 256)
    *arrays, coarse, bottom = call(
        own_kernel,
        [plane] * len(FINE) + [(20, 8, 128), (8, 128)],
        [(16, 8, 256), (64, 128)],
        low,
        high,
    )
    fine = call(
        functools.partial(fine_kernel, boxes),
        [plane] * len(FINE) + [(16, 8, 128), (SEND1, 8, 128), (SEND1, 8, 128)],
        [plane, (16, 8, 256)],
        halo,
        coarse,
        *arrays,
        aliases=[(2 + k, k) for k in range(len(FINE))],
    )
    level0 = fine[: len(PACKED)]
    source, first, second = fine[len(FINE) :]
    first, second = exchange(first, second)

    one, two = (N1, 8, 128), (N2, 8, 128)
    *levels, send, compact, message = call(
        functools.partial(middle_kernel, boxes),
        [one] * 6 + [two] * 4 + [(16, 8, 128), (4, 8, 128), (2 * boxes, 128)],
        [two] * 3 + [one, (128, 128)],
        source,
        coarse,
        first,
        second,
        bottom,
    )
    spread = lax.all_to_all(message.reshape(boxes, 2, 128), "box", 0, 0).reshape(2 * boxes, 128)
    first, second = exchange(*call(after_kernel, [(SEND2, 8, 128)] * 2, [], compact, level0[0], spread))
    gathered = lax.all_gather(spread, "slab")
    (e2,) = call(
        functools.partial(coarse_kernel, boxes),
        [two],
        [(2, boxes // 8, 8, 128)] * 4 + [(2, boxes + 16, 128)],
        gathered,
    )
    pressure, residual = call(
        last_kernel,
        [(512, 128)] * 2,
        [plane, plane, one, two, two, (128, 128), (22, 8, 256)],
        e2,
        first,
        second,
        send,
        *levels,
        *level0,
    )
    return from_tiles(pressure), from_tiles(residual)


def solution(mesh):
    split = P("slab", "box", None)
    return jax.shard_map(body, mesh=mesh, in_specs=(split,) * 3, out_specs=(split,) * 2, check_vma=False)
```

```python
import functools

import jax
import jax.numpy as jnp
from jax import lax
from jax.experimental import pallas as pl
from jax.experimental.pallas import tpu as pltpu
from jax.sharding import PartitionSpec as P

ITERS = 8
F32 = jnp.float32
BF16 = jnp.bfloat16

H0 = 5
H1 = 12
N0 = 32 + 2 * H0
N1 = 16 + 2 * (H1 + 1)
N2 = 24
ROWS = 20
EDGE = 96
EDGE_F, EDGE_V = 8 * H0, 16 * H0 - 8
SWEEP, FACES, RESTRICT, FINISH = 99, 99, 16, 99
SEND1 = H1 + (H1 + 1) + 4
SEND2 = 4 + 2 * H0


def matmul(x, m):
    high = x.astype(BF16)
    rest = x - high.astype(F32)
    mid = rest.astype(BF16)
    low = (rest - mid.astype(F32)).astype(BF16)
    dot = functools.partial(jnp.dot, preferred_element_type=F32)
    return dot(high, m) + (dot(mid, m) + dot(low, m))


def one_hot(shape, rule):
    i = lax.broadcasted_iota(jnp.int32, shape, 0)
    j = lax.broadcasted_iota(jnp.int32, shape, 1)
    return rule(i, j).astype(F32).astype(BF16)


def iota(shape, axis):
    return lax.broadcasted_iota(jnp.int32, shape, axis)


def up(v, axis):
    return pltpu.roll(v, v.shape[axis] - 1, axis)


def down(v, axis):
    return pltpu.roll(v, 1, axis)


def planes(first, last, unroll, step, carry=0):
    def pair(k, carry):
        i = first + 2 * k
        return step(i + 1, (first + 1) % 2, step(i, first % 2, carry))

    count = (last - first) // 2
    if unroll < count:
        return lax.fori_loop(0, count, pair, carry, unroll=unroll)
    for k in range(count):
        carry = pair(k, carry)
    return carry


def my_place():
    return lax.axis_index("slab"), lax.axis_index("box")


def slab_rows(x, half, odd):
    return pl.ds((x // 8) * 16 + half * 8 + x % 8 + 64 * odd, 4, stride=128)


def pack_plane(g, r, c, x, rows, even_y, out, b_at, f_at, v_at):
    p0 = even_y if x % 2 == 0 else jnp.logical_not(even_y)
    for half in range(2):
        lanes = slice(128 * half, 128 * half + 128)
        even, odd = rows(half, 0), rows(half, 1)
        out[b_at : b_at + 4, lanes] = c[even, :]
        out[b_at + 4 : b_at + 8, lanes] = c[odd, :]
        if f_at is not None:
            fe, fo = r[even, :], r[odd, :]
            out[f_at : f_at + 4, lanes] = jnp.where(p0, fe, fo)
            out[f_at + 4 : f_at + 8, lanes] = jnp.where(p0, fo, fe)
        out[v_at : v_at + 4, lanes] = jnp.where(p0, g[odd, :], g[even, :])


def pack_edge(parts, right, rows, even_y, out):
    for k in range(H0):
        x = 32 - H0 + k if right else k
        f_at = k - 1 if right else k
        f_at = EDGE_F + 8 * f_at if 0 <= f_at < H0 - 1 else None
        pack_plane(*parts, x, functools.partial(rows, x), even_y, out, 8 * k, f_at, EDGE_V + 4 * k)
    out[EDGE_V + 4 * H0 :, :] = jnp.zeros((EDGE - EDGE_V - 4 * H0, 256), F32)


def pack_kernel(g, r, c, low, high, second):
    even_y = (iota((4, 128), 1) & 1) == 0
    swapped = (my_place()[1] & 1) == 1

    @pl.when(swapped)
    def _():
        pack_edge((g, r, c), False, slab_rows, even_y, second)

    @pl.when(jnp.logical_not(swapped))
    def _():
        pack_edge((g, r, c), True, slab_rows, even_y, second)

    for x in range(32):
        out, base = (low, x * ROWS) if x < 16 else (high, (x - 16) * ROWS)
        pack_plane(g, r, c, x, functools.partial(slab_rows, x), even_y, out, base, base + 8, base + 16)


def edge_kernel(g_hbm, r_hbm, c_hbm, first, *scratch):
    parts, sem = scratch[0:3], scratch[3]
    odd = my_place()[1] & 1
    at = pl.multiple_of(48 * odd, 16)
    copies = [
        pltpu.make_async_copy(source.at[:, pl.ds(at, 16), :], target.reshape(8, 16, 128), sem.at[k])
        for k, (source, target) in enumerate(zip((g_hbm, r_hbm, c_hbm), parts))
    ]
    for copy in copies:
        copy.start()
    for copy in copies:
        copy.wait()
    even_y = (iota((4, 128), 1) & 1) == 0

    def rows(x, half, second_z):
        return pl.ds(half * 8 + x % 8 + 16 * second_z, 4, stride=32)

    @pl.when(odd == 1)
    def _():
        pack_edge(parts, True, rows, even_y, first)

    @pl.when(odd == 0)
    def _():
        pack_edge(parts, False, rows, even_y, first)


def parity(odd):
    return ((iota((8, 256), 1) + odd + 1) & 1) == 0


def nsum_packed(lv, v, xa, xb, ya, yb, i, p):
    here = v[i]
    t = xa[i] * v[i + 1] + xb[i - 1] * v[i - 1]
    t = t + (ya[i] * up(here, 1) + down(yb[i] * here, 1))
    cross = lv["c"][i]
    z = jnp.where(p, down(cross * here, 0), cross * up(here, 0))
    return t + (lv["s"][i] * here + z)


def sweep_packed(lv, red, first, last):
    def step(i, odd, carry):
        p = parity(odd)
        if red:
            n = nsum_packed(lv, lv["vB"], lv["xR"], lv["xB"], lv["yR"], lv["yB"], i, p)
            lv["vR"][i] = (lv["fR"][i] + n) * lv["iR"][i]
        else:
            p = jnp.logical_not(p)
            n = nsum_packed(lv, lv["vR"], lv["xB"], lv["xR"], lv["yB"], lv["yR"], i, p)
            lv["vB"][i] = (lv["fB"][i] + n) * lv["iB"][i]
        return carry

    planes(first, last, SWEEP, step)


def residual_packed(lv, i, odd):
    p = parity(odd)
    n = nsum_packed(lv, lv["vB"], lv["xR"], lv["xB"], lv["yR"], lv["yB"], i, p)
    r_red = lv["fR"][i] - (lv["cR"][i] * lv["vR"][i] - n)
    q = jnp.logical_not(p)
    n = nsum_packed(lv, lv["vR"], lv["xB"], lv["xR"], lv["yB"], lv["yR"], i, q)
    r_black = lv["fB"][i] - (lv["cB"][i] * lv["vB"][i] - n)
    return r_red, r_black, p


PACKED = ("vB", "fR", "fB", "xR", "xB", "yR", "yB", "s", "c", "iR", "iB", "cR", "cB")


FINE = PACKED + ("bE", "bO")


def stack(parts, at, i, out):
    for t in range(2):
        out[i, 4 * t : 4 * t + 4, :] = parts[t][at : at + 4, :]


def merge(parts, at, i, low, high):
    low_half = iota((8, 256), 0) < 4
    a, b = (part[at : at + 8, :] for part in parts)
    low[i] = jnp.where(low_half, a, pltpu.roll(b, 4, 0))
    high[i] = jnp.where(low_half, pltpu.roll(a, 4, 0), b)


def x_values(lv, i):
    return 0.5 * (lv["bE"][i] + lv["bE"][i + 1]), 0.5 * (lv["bO"][i] + lv["bO"][i + 1])


def x_faces(lv, i, p):
    fxe, fxo = x_values(lv, i)
    lv["xR"][i] = jnp.where(p, fxe, fxo)
    lv["xB"][i] = jnp.where(p, fxo, fxe)
    return fxe, fxo


def faces(lv, i, before, inside=None):
    row, lane = iota((8, 256), 0), iota((8, 256), 1)
    top, bot = row == 7, row == 0
    end, begin = lane == 255, lane == 0
    p = parity(i % 2)
    e, o = lv["bE"][i], lv["bO"][i]
    fxe, fxo = x_faces(lv, i, p)
    fye = 0.5 * (e + jnp.where(end, 0.0, up(e, 1)))
    fyo = 0.5 * (o + jnp.where(end, 0.0, up(o, 1)))
    gye = 0.5 * (e + jnp.where(begin, 0.0, down(e, 1)))
    gyo = 0.5 * (o + jnp.where(begin, 0.0, down(o, 1)))
    yr, yb = jnp.where(p, fye, fyo), jnp.where(p, fyo, fye)
    lv["yR"][i] = jnp.where(end, 0.0, yr)
    lv["yB"][i] = jnp.where(end, 0.0, yb)
    s = 0.5 * (e + o)
    above = 0.5 * (o + jnp.where(top, 0.0, up(e, 0)))
    below = 0.5 * (e + jnp.where(bot, 0.0, down(o, 0)))
    lv["s"][i] = s
    lv["c"][i] = jnp.where(top, 0.0, above)
    ce = fye + gye + (s + below) + (fxe + before[0])
    co = fyo + gyo + (s + above) + (fxo + before[1])
    cr, cb = jnp.where(p, ce, co), jnp.where(p, co, ce)
    lv["cR"][i] = cr
    lv["cB"][i] = cb
    ir, ib = 1.0 / cr, 1.0 / cb
    lv["iR"][i] = ir if inside is None else jnp.where(inside, ir, 0.0)
    lv["iB"][i] = ib if inside is None else jnp.where(inside, ib, 0.0)
    return fxe, fxo


def own_kernel(lo, hi, *refs):
    lv = dict(zip(FINE, refs))
    coarse, bottom, pair_b, tmp = refs[len(FINE) :]
    for x in range(32):
        source, base = (lo, x * ROWS) if x < 16 else (hi, (x - 16) * ROWS)
        parts = source.at[0], source.at[1]
        merge(parts, base, H0 + x, lv["bE"], lv["bO"])
        merge(parts, base + 8, H0 + x, lv["fR"], lv["fB"])
        stack(parts, base + 16, H0 + x, lv["vB"])
    before = x_values(lv, H0)
    for i in range(H0 + 1, H0 + 31):
        before = faces(lv, i, before)

    bE, bO = lv["bE"], lv["bO"]
    for j in range(16):
        i = H0 + 2 * j
        pair_b[j] = (bE[i] + bO[i]) + (bE[i + 1] + bO[i + 1])
    halve = one_hot((256, 128), lambda i, j: (i >> 1) == j)
    coarse[0:16] = (0.125 * matmul(pair_b[...].reshape(128, 256), halve)).reshape(16, 8, 128)
    for k in range(8):
        tmp[8 * k : 8 * k + 8, :] = coarse[2 * k] + coarse[2 * k + 1]
    summed = tmp[pl.ds(0, 32, stride=2), :] + tmp[pl.ds(1, 32, stride=2), :]
    halve = one_hot((128, 128), lambda i, j: (i >> 1) == j)
    coarse[16:20] = (0.125 * matmul(summed, halve)).reshape(4, 8, 128)
    bottom[...] = bottom_row([coarse[16 + k] + pltpu.roll(coarse[16 + k], 4, 0) for k in range(4)])


def fine_kernel(boxes, halo, coarse, *refs):
    refs = refs[len(FINE) :]
    lv = dict(zip(FINE, refs))
    f1, first, second, vR, pair_r = refs[len(FINE) :]
    lv["vR"] = vR
    box = my_place()[1]
    odd = box & 1
    for side, at in ((odd, 0), (1 - odd, H0 + 32)):
        parts = halo.at[0, side], halo.at[1, side]
        for k in range(H0):
            merge(parts, 8 * k, at + k, lv["bE"], lv["bO"])
            stack(parts, EDGE_V + 4 * k, at + k, lv["vB"])
        for k in range(H0 - 1):
            merge(parts, EDGE_F + 8 * k, (1 if at == 0 else at) + k, lv["fR"], lv["fB"])
    before = x_faces(lv, 0, parity(0))
    for i in range(1, H0 + 1):
        before = faces(lv, i, before, None if i == H0 else box > 0)
    before = x_values(lv, H0 + 30)
    for i in range(H0 + 31, N0 - 1):
        before = faces(lv, i, before, None if i == H0 + 31 else box < boxes - 1)

    for k in range(2):
        sweep_packed(lv, True, 1 + 2 * k, N0 - 1 - 2 * k)
        sweep_packed(lv, False, 2 + 2 * k, N0 - 2 - 2 * k)
    for j in range(16):
        i = H0 + 2 * j
        a, b, _ = residual_packed(lv, i, H0 % 2)
        c, d, _ = residual_packed(lv, i + 1, (H0 + 1) % 2)
        pair_r[j] = (a + b) + (c + d)
    halve = one_hot((256, 128), lambda i, j: (i >> 1) == j)
    f1[...] = (0.125 * matmul(pair_r[...].reshape(128, 256), halve)).reshape(16, 8, 128)

    for out, right in ((first, odd), (second, 1 - odd)):
        out[0:H1] = f1[pl.ds(right * (16 - H1), H1)]
        out[H1 : 2 * H1 + 1] = coarse[pl.ds(right * (15 - H1), H1 + 1)]
        out[2 * H1 + 1 :] = coarse[16:20]


def bottom_row(pairs):
    total = None
    for k, plane in enumerate(pairs):
        spread = one_hot((128, 128), lambda i, j, k=k: jnp.logical_and((i >> 1) + 32 * k == j, i < 64))
        part = matmul(plane, spread)
        total = part if total is None else total + part
    low, high = total[0:1] + total[1:2], total[2:3] + total[3:4]
    row = 0.125 * jnp.where(my_place()[0] == 0, low, high)
    return jnp.broadcast_to(row, (8, 128))


def level_faces(b, ax, ay, az, inv, n, factor, depth, width, inside):
    row, lane = iota((8, 128), 0), iota((8, 128), 1)
    top, bot = row == depth - 1, row == 0
    end, begin = lane == width - 1, lane == 0
    cell = jnp.logical_and(row < depth, lane < width)
    ax[0] = factor * (b[0] + b[1])

    def step(i, odd, before):
        v = b[i]
        fx = factor * (v + b[i + 1])
        ax[i] = fx
        fy = factor * (v + jnp.where(end, 0.0, up(v, 1)))
        gy = factor * (v + jnp.where(begin, 0.0, down(v, 1)))
        fz = factor * (v + jnp.where(top, 0.0, up(v, 0)))
        gz = factor * (v + jnp.where(bot, 0.0, down(v, 0)))
        ay[i] = jnp.where(end, 0.0, fy)
        az[i] = jnp.where(top, 0.0, fz)
        center = (fz + gz) + (fx + before) + (fy + gy)
        inv[i] = jnp.where(jnp.logical_and(cell, inside(i)), 1.0 / center, 0.0)
        return fx

    planes(1, n - 1, 99, step, ax[0])


def nsum_values(before, here, after, ax, ay, az, i):
    t = ax[i] * after + ax[i - 1] * before
    t = t + (ay[i] * up(here, 1) + down(ay[i] * here, 1))
    return t + (az[i] * up(here, 0) + down(az[i] * here, 0))


def nsum_plain(v, ax, ay, az, i):
    return nsum_values(v[i - 1], v[i], v[i + 1], ax, ay, az, i)


def colour(odd):
    return ((iota((8, 128), 0) + iota((8, 128), 1) + odd) & 1) == 0


def sweep_plain(v, f, ax, ay, az, inv, odd, shift, first, last):
    before, here = v[first - 1], v[first]
    for i in range(first, last):
        after = v[i + 1]
        n = nsum_values(before, here, after, ax, ay, az, i)
        v[i] = jnp.where(colour((i + shift + odd) % 2), (f[i] + n) * inv[i], here)
        before, here = here, after


def first_plain(v, f, inv, shift, first, last):
    def step(i, plane_odd, carry):
        v[i] = jnp.where(colour((plane_odd + shift) % 2), f[i] * inv[i], 0.0)
        return carry

    planes(first, last, 99, step)


def residual_plain(v, f, ax, ay, az, center, i):
    return f[i] - (center * v[i] - nsum_plain(v, ax, ay, az, i))


def center_plain(b, ax, i, factor, depth, width):
    row, lane = iota((8, 128), 0), iota((8, 128), 1)
    v = b[i]
    fy = jnp.where(lane == width - 1, 0.0, up(v, 1)) + jnp.where(lane == 0, 0.0, down(v, 1))
    fz = jnp.where(row == depth - 1, 0.0, up(v, 0)) + jnp.where(row == 0, 0.0, down(v, 0))
    return factor * (4.0 * v + fy + fz) + (ax[i] + ax[i - 1])


def middle_kernel(boxes, source, coarse, first, second, bottom, v1, f1, ax1, ay1, az1, inv1, ax2, ay2, az2, inv2, send, compact, message, v2, f2, b2, b1, tmp):
    box = my_place()[1]
    w = H1 + 1
    swapped = (box & 1) == 1

    def received(k, count):
        one, two = first[k : k + count], second[k : k + count]
        return jnp.where(swapped, two, one), jnp.where(swapped, one, two)

    left, right = received(H1, w)
    b1[0:w] = left
    b1[w : w + 16] = coarse[0:16]
    b1[w + 16 :] = right
    left, right = received(0, H1)
    f1[0:1] = jnp.zeros((1, 8, 128), F32)
    f1[1 : 1 + H1] = left
    f1[w : w + 16] = source[...]
    f1[w + 16 : w + 16 + H1] = right
    f1[N1 - 1 :] = jnp.zeros((1, 8, 128), F32)
    left, right = received(H1 + w, 4)
    b2[...] = jnp.zeros(b2.shape, F32)
    for at, part in ((0, left), (8, coarse[16:20]), (16, right)):
        for k in range(8):
            b2[at + k, 0:4, :] = part[k // 2, 4 * (k % 2) : 4 * (k % 2) + 4]
    v1[...] = jnp.zeros(v1.shape, F32)
    v2[...] = jnp.zeros(v2.shape, F32)
    f2[...] = jnp.zeros(f2.shape, F32)

    def within(size, width):
        def inside(i):
            x = box * size - width + i
            return jnp.logical_and(x >= 0, x < boxes * size)

        return inside

    k1, k2 = 0.5 * 0.25, 0.5 * 0.25**2
    level_faces(b1, ax1, ay1, az1, inv1, N1, k1, 8, 128, within(16, w))
    level_faces(b2, ax2, ay2, az2, inv2, N2, k2, 4, 64, within(8, 8))

    one = (f1, ax1, ay1, az1, inv1)
    first_plain(v1, f1, inv1, 1, 1, N1 - 1)
    sweep_plain(v1, *one, 1, 1, 2, N1 - 2)
    sweep_plain(v1, *one, 0, 1, 3, N1 - 3)
    sweep_plain(v1, *one, 1, 1, 4, N1 - 4)

    def restrict(j, carry):
        i = 5 + 2 * j
        parts = [residual_plain(v1, *one[:4], center_plain(b1, ax1, k, k1, 8, 128), k) for k in (i, i + 1)]
        tmp[8 * j : 8 * j + 8, :] = parts[0] + parts[1]
        return carry

    for j in range(16):
        restrict(j, 0)
    summed = tmp[pl.ds(0, 64, stride=2), :] + tmp[pl.ds(1, 64, stride=2), :]
    restricted = 0.125 * matmul(summed, one_hot((128, 128), lambda i, j: (i >> 1) == j))
    for j in range(16):
        f2[4 + j, 0:4, :] = restricted[4 * j : 4 * j + 4]

    two = (f2, ax2, ay2, az2, inv2)
    first_plain(v2, f2, inv2, 0, 4, 20)
    sweep_plain(v2, *two, 1, 0, 5, 19)
    sweep_plain(v2, *two, 0, 0, 6, 18)
    sweep_plain(v2, *two, 1, 0, 7, 17)
    send[0:8] = v2[8:16]
    send[8:16] = f2[8:16]
    for k in range(4):
        both = [pltpu.roll(ref[9 + 2 * k], 4, 0) + ref[8 + 2 * k] for ref in (v2, f2)]
        compact[k] = both[0] + pltpu.roll(both[1], 64, 1)

    pairs = []
    for k in range(4):
        parts = [
            residual_plain(v2, *two[:4], center_plain(b2, ax2, i, k2, 4, 64), i)
            for i in (8 + 2 * k, 9 + 2 * k)
        ]
        pairs.append(parts[0] + parts[1])
    rows = jnp.where((iota((8, 128), 0) & 1) == 0, bottom_row(pairs), bottom[...])
    for k in range(message.shape[0] // 8):
        message[8 * k : 8 * k + 8, :] = rows


def coarse_solve(source, coefficient, dref, sref, rref, eref):
    shape = source[0].shape
    groups = shape[0]
    group, row, lane = (iota(shape, k) for k in range(3))
    factor = 0.5 * 0.25**3
    last = jnp.logical_and(jnp.logical_and(group == groups - 1, row == 7), lane >= 96)
    first = jnp.logical_and(jnp.logical_and(group == 0, row == 0), lane < 32)
    inner_hi, inner_lo = lane < 96, lane >= 32
    end, begin = (lane & 31) == 31, (lane & 31) == 0

    def lanes(v, shift):
        return pltpu.roll(v.reshape(8 * groups, 128), shift, 1).reshape(shape)

    def xp(v):
        a = lanes(v, 96)
        return jnp.where(inner_hi, a, jnp.concatenate([a[1:], up(a[0], 0)[None]], axis=0))

    def xm(v):
        a = lanes(v, 32)
        return jnp.where(inner_lo, a, jnp.concatenate([down(a[groups - 1], 0)[None], a[:-1]], axis=0))

    ax, ay, center = [], [], []
    az = factor * (coefficient[0] + coefficient[1])
    for b in coefficient:
        fx = factor * (b + jnp.where(last, 0.0, xp(b)))
        gx = factor * (b + jnp.where(first, 0.0, xm(b)))
        fy = factor * (b + jnp.where(end, 0.0, lanes(b, 127)))
        gy = factor * (b + jnp.where(begin, 0.0, lanes(b, 1)))
        ax.append(jnp.where(last, 0.0, fx))
        ay.append(jnp.where(end, 0.0, fy))
        center.append((factor * b + az) + (fx + gx) + (fy + gy))

    def total(u, w):
        s = jnp.sum(u[0] * w[0] + u[1] * w[1], axis=0)
        return jnp.sum(jnp.sum(s, axis=0, keepdims=True), axis=1, keepdims=True)

    before = alpha = None
    for k in range(ITERS):
        r = [source[t] if k == 0 else rref[t] for t in range(2)]
        w = []
        for t in range(2):
            v = r[t]
            n = ax[t] * xp(v) + xm(ax[t] * v)
            n = n + (ay[t] * lanes(v, 127) + lanes(ay[t] * v, 1))
            w.append(center[t] * v - (n + az * r[1 - t]))
        rr, below = total(r, r), total(r, w)
        if k > 0:
            beta = rr / before
            below = below - beta * (rr / alpha)
        alpha = rr / below
        before = rr
        for t in range(2):
            d, image = (r[t], w[t]) if k == 0 else (r[t] + beta * dref[t], w[t] + beta * sref[t])
            eref[t] = alpha * d if k == 0 else eref[t] + alpha * d
            if k < ITERS - 1:
                dref[t] = d
                sref[t] = image
                rref[t] = r[t] - alpha * image


def coarse_kernel(boxes, gathered, e2, dref, sref, rref, eref, ordered):
    box = my_place()[1]
    groups = boxes // 8

    def load(t, at):
        return jnp.stack([gathered[t, pl.ds(2 * g + at, 8, stride=2 * groups), :] for g in range(groups)])

    coarse_solve([load(t, 0) for t in range(2)], [load(t, 1) for t in range(2)], dref, sref, rref, eref)
    for t in range(2):
        ordered[t, 0:8] = jnp.zeros((8, 128), F32)
        ordered[t, 8 + boxes :] = jnp.zeros((8, 128), F32)
        for g in range(groups):
            ordered[t, pl.ds(8 + g, 8, stride=groups), :] = eref[t, g]
    near = [ordered[t, pl.ds(7 + box, 8), :] for t in range(2)]
    spread = one_hot((128, 512), lambda i, j: jnp.logical_and(((j >> 7) * 32) + ((j & 127) >> 1) == i, (j & 127) < 64))
    fine = [matmul(e, spread) for e in near]
    row = iota((8, 128), 0)
    for i in range(N2):
        cell, k = (i // 2) // 4, (i // 2) % 4
        low, high = (f[cell : cell + 1, 128 * k : 128 * k + 128] for f in fine)
        e2[i] = jnp.where(row < 2, low, jnp.where(row < 4, high, 0.0))


def after_kernel(compact, black, gathered, first, second):
    del gathered
    odd = my_place()[1] & 1
    for out, right in ((first, odd), (second, 1 - odd)):
        out[0:4] = compact[...]
        start = H0 + right * (32 - H0)
        for k in range(H0):
            for half in range(2):
                out[4 + 2 * k + half] = black[start + k, :, 128 * half : 128 * half + 128]


def last_kernel(*refs):
    names = ("e2", "first", "second", "own2", "v1", "f1", "ax1", "ay1", "az1", "inv1", "ax2", "ay2", "az2", "inv2")
    given = dict(zip(names, refs))
    refs = refs[len(names) :]
    level0 = dict(zip(PACKED, refs))
    refs = refs[len(PACKED) :]
    out_v, out_r, vR, vB, v1, v2, f2, wide, e0 = refs
    slab, box = my_place()
    e2, first, second, own2 = given["e2"], given["first"], given["second"], given["own2"]
    swapped = (box & 1) == 1

    def received(side, k, count):
        one, two = (first, second) if side == 0 else (second, first)
        return jnp.where(swapped, two[k : k + count], one[k : k + count])

    v2[8:16] = own2[0:8]
    f2[8:16] = own2[8:16]
    quarter = jnp.logical_and(iota((8, 128), 0) < 4, iota((8, 128), 1) < 64)
    for side, at in ((0, 0), (1, 16)):
        four = received(side, 0, 4)
        for k in range(4):
            for ref, plane in ((v2, four[k]), (f2, pltpu.roll(four[k], 64, 1))):
                ref[at + 2 * k] = jnp.where(quarter, plane, 0.0)
                ref[at + 2 * k + 1] = jnp.where(quarter, pltpu.roll(plane, 4, 0), 0.0)
    for i in range(N2):
        v2[i] = v2[i] + e2[i]
    two = (f2, given["ax2"], given["ay2"], given["az2"], given["inv2"])
    for k in range(2):
        sweep_plain(v2, *two, 0, 0, 1 + 2 * k, N2 - 1 - 2 * k)
        sweep_plain(v2, *two, 1, 0, 2 + 2 * k, N2 - 2 - 2 * k)

    packed = jnp.concatenate([v2[4 + j, 0:4, :] for j in range(16)], axis=0)
    fine = matmul(packed, one_hot((128, 128), lambda i, j: (j >> 1) == i))
    wide[pl.ds(0, 64, stride=2), :] = fine
    wide[pl.ds(1, 64, stride=2), :] = fine
    for i in range(6, N1 - 6):
        j = (i + 3) // 2 - 4
        v1[i] = given["v1"][i] + wide[8 * j : 8 * j + 8, :]
    one = (given["f1"], given["ax1"], given["ay1"], given["az1"], given["inv1"])
    for k in range(2):
        sweep_plain(v1, *one, 0, 1, 7 + 2 * k, N1 - 7 - 2 * k)
        sweep_plain(v1, *one, 1, 1, 8 + 2 * k, N1 - 8 - 2 * k)

    double = one_hot((128, 256), lambda i, j: (j >> 1) == i)
    e0[...] = matmul(v1[10:32].reshape(176, 128), double).reshape(22, 8, 256)
    lv = dict(level0, vR=vR, vB=vB)

    black = level0["vB"]

    def correct(j, carry):
        e = e0[j]
        vB[2 * j - 1] = black[2 * j - 1] + e
        vB[2 * j] = black[2 * j] + e
        return carry

    lax.fori_loop(3, 19, correct, 0, unroll=4)
    for side, at in ((0, 0), (1, H0 + 32)):
        for k in range(H0):
            for half in range(2):
                lanes = slice(128 * half, 128 * half + 128)
                vB[at + k, :, lanes] = received(side, 4 + 2 * k + half, 1)[0] + e0[(at + k + 1) // 2, :, lanes]
    for k in range(2):
        sweep_packed(lv, True, 1 + 2 * k, N0 - 1 - 2 * k)
        sweep_packed(lv, False, 2 + 2 * k, N0 - 2 - 2 * k)


    def finish(i, odd, carry):
        x = i - H0
        red, black, p = residual_packed(lv, i, odd)
        for out, a, b in ((out_v, vR[i], vB[i]), (out_r, red, black)):
            for at, whole in ((0, jnp.where(p, a, b)), (1, jnp.where(p, b, a))):
                part = jnp.where(slab == 0, whole[0:4], whole[4:8])
                for half in range(2):
                    out[slab_rows(x, half, at), :] = part[:, 128 * half : 128 * half + 128]
        return carry

    planes(H0, H0 + 32, FINISH, finish)


def call(kernel, outs, scratch, *args, limit=12, aliases=()):
    vmem = pl.BlockSpec(memory_space=pltpu.VMEM)
    return pl.pallas_call(
        kernel,
        out_shape=[jax.ShapeDtypeStruct(s, F32) for s in outs],
        in_specs=[vmem] * len(args),
        out_specs=[vmem] * len(outs),
        input_output_aliases=dict(aliases),
        scratch_shapes=[pltpu.VMEM(s, F32) for s in scratch],
        compiler_params=pltpu.CompilerParams(vmem_limit_bytes=limit * 1024 * 1024),
    )(*args)


def edges(*args):
    return pl.pallas_call(
        edge_kernel,
        out_shape=jax.ShapeDtypeStruct((EDGE, 256), F32),
        in_specs=[pl.BlockSpec(memory_space=pl.ANY)] * 3,
        out_specs=pl.BlockSpec(memory_space=pltpu.VMEM),
        scratch_shapes=[pltpu.VMEM((128, 128), F32)] * 3 + [pltpu.SemaphoreType.DMA((3,))],
        compiler_params=pltpu.CompilerParams(vmem_limit_bytes=60 * 1024 * 1024),
    )(*[a.reshape(8, 64, 128) for a in args])


def by_tiles(a):
    return a.reshape(8, 4, 8, 2, 128).transpose(0, 1, 3, 2, 4).reshape(512, 128)


def from_tiles(a):
    return a.reshape(8, 4, 2, 8, 128).transpose(0, 1, 3, 2, 4).reshape(8, 32, 256)


def exchange(first, second):
    boxes = lax.axis_size("box")
    odd = [(i, i + 1) for i in range(1, boxes - 1, 2)]
    even = [(i, i + 1) for i in range(0, boxes - 1, 2)]
    return [lax.ppermute(x, "box", p + [(j, i) for i, j in p]) for x, p in ((first, odd), (second, even))]


def body(pressure_guess, right_side, coefficient):
    boxes = lax.axis_size("box")
    flat = [by_tiles(a) for a in (pressure_guess, right_side, coefficient)]
    first = edges(*flat)
    low, high, second = call(pack_kernel, [(16 * ROWS, 256)] * 2 + [(EDGE, 256)], [], *flat)
    first, second = exchange(first, second)
    low, high = lax.all_gather(low, "slab"), lax.all_gather(high, "slab")
    halo = lax.all_gather(jnp.stack([first, second]), "slab")

    plane = (N0, 8, 256)
    *arrays, coarse, bottom = call(
        own_kernel,
        [plane] * len(FINE) + [(20, 8, 128), (8, 128)],
        [(16, 8, 256), (64, 128)],
        low,
        high,
    )
    fine = call(
        functools.partial(fine_kernel, boxes),
        [plane] * len(FINE) + [(16, 8, 128), (SEND1, 8, 128), (SEND1, 8, 128)],
        [plane, (16, 8, 256)],
        halo,
        coarse,
        *arrays,
        aliases=[(2 + k, k) for k in range(len(FINE))],
    )
    level0 = fine[: len(PACKED)]
    source, first, second = fine[len(FINE) :]
    first, second = exchange(first, second)

    one, two = (N1, 8, 128), (N2, 8, 128)
    *levels, send, compact, message = call(
        functools.partial(middle_kernel, boxes),
        [one] * 6 + [two] * 4 + [(16, 8, 128), (4, 8, 128), (2 * boxes, 128)],
        [two] * 3 + [one, (128, 128)],
        source,
        coarse,
        first,
        second,
        bottom,
    )
    spread = lax.all_to_all(message.reshape(boxes, 2, 128), "box", 0, 0).reshape(2 * boxes, 128)
    first, second = exchange(*call(after_kernel, [(SEND2, 8, 128)] * 2, [], compact, level0[0], spread))
    gathered = lax.all_gather(spread, "slab")
    (e2,) = call(
        functools.partial(coarse_kernel, boxes),
        [two],
        [(2, boxes // 8, 8, 128)] * 4 + [(2, boxes + 16, 128)],
        gathered,
    )
    pressure, residual = call(
        last_kernel,
        [(512, 128)] * 2,
        [plane, plane, one, two, two, (128, 128), (22, 8, 256)],
        e2,
        first,
        second,
        send,
        *levels,
        *level0,
    )
    return from_tiles(pressure), from_tiles(residual)


def solution(mesh):
    split = P("slab", "box", None)
    return jax.shard_map(body, mesh=mesh, in_specs=(split,) * 3, out_specs=(split,) * 2, check_vma=False)
```

```python
import functools

import jax
import jax.numpy as jnp
from jax import lax
from jax.experimental import pallas as pl
from jax.experimental.pallas import tpu as pltpu
from jax.sharding import PartitionSpec as P

ITERS = 8
F32 = jnp.float32
BF16 = jnp.bfloat16

H0 = 5
H1 = 12
N0 = 32 + 2 * H0
N1 = 16 + 2 * (H1 + 1)
N2 = 24
ROWS = 20
EDGE = 96
EDGE_F, EDGE_V = 8 * H0, 16 * H0 - 8
SWEEP, FACES, RESTRICT, FINISH = 99, 99, 16, 99
SEND1 = H1 + (H1 + 1) + 4
SEND2 = 4 + 2 * H0


def matmul(x, m):
    high = x.astype(BF16)
    rest = x - high.astype(F32)
    mid = rest.astype(BF16)
    low = (rest - mid.astype(F32)).astype(BF16)
    dot = functools.partial(jnp.dot, preferred_element_type=F32)
    return dot(high, m) + (dot(mid, m) + dot(low, m))


def one_hot(shape, rule):
    i = lax.broadcasted_iota(jnp.int32, shape, 0)
    j = lax.broadcasted_iota(jnp.int32, shape, 1)
    return rule(i, j).astype(F32).astype(BF16)


def iota(shape, axis):
    return lax.broadcasted_iota(jnp.int32, shape, axis)


def up(v, axis):
    return pltpu.roll(v, v.shape[axis] - 1, axis)


def down(v, axis):
    return pltpu.roll(v, 1, axis)


def planes(first, last, unroll, step, carry=0):
    def pair(k, carry):
        i = first + 2 * k
        return step(i + 1, (first + 1) % 2, step(i, first % 2, carry))

    count = (last - first) // 2
    if unroll < count:
        return lax.fori_loop(0, count, pair, carry, unroll=unroll)
    for k in range(count):
        carry = pair(k, carry)
    return carry


def my_place():
    return lax.axis_index("slab"), lax.axis_index("box")


def slab_rows(x, half, odd):
    return pl.ds((x // 8) * 16 + half * 8 + x % 8 + 64 * odd, 4, stride=128)


def pack_plane(g, r, c, x, rows, even_y, out, b_at, f_at, v_at):
    p0 = even_y if x % 2 == 0 else jnp.logical_not(even_y)
    for half in range(2):
        lanes = slice(128 * half, 128 * half + 128)
        even, odd = rows(half, 0), rows(half, 1)
        out[b_at : b_at + 4, lanes] = c[even, :]
        out[b_at + 4 : b_at + 8, lanes] = c[odd, :]
        if f_at is not None:
            fe, fo = r[even, :], r[odd, :]
            out[f_at : f_at + 4, lanes] = jnp.where(p0, fe, fo)
            out[f_at + 4 : f_at + 8, lanes] = jnp.where(p0, fo, fe)
        out[v_at : v_at + 4, lanes] = jnp.where(p0, g[odd, :], g[even, :])


def pack_edge(parts, right, rows, even_y, out):
    for k in range(H0):
        x = 32 - H0 + k if right else k
        f_at = k - 1 if right else k
        f_at = EDGE_F + 8 * f_at if 0 <= f_at < H0 - 1 else None
        pack_plane(*parts, x, functools.partial(rows, x), even_y, out, 8 * k, f_at, EDGE_V + 4 * k)
    out[EDGE_V + 4 * H0 :, :] = jnp.zeros((EDGE - EDGE_V - 4 * H0, 256), F32)


def pack_kernel(g, r, c, low, high, second):
    even_y = (iota((4, 128), 1) & 1) == 0
    swapped = (my_place()[1] & 1) == 1

    @pl.when(swapped)
    def _():
        pack_edge((g, r, c), False, slab_rows, even_y, second)

    @pl.when(jnp.logical_not(swapped))
    def _():
        pack_edge((g, r, c), True, slab_rows, even_y, second)

    for x in range(32):
        out, base = (low, x * ROWS) if x < 16 else (high, (x - 16) * ROWS)
        pack_plane(g, r, c, x, functools.partial(slab_rows, x), even_y, out, base, base + 8, base + 16)


def edge_kernel(g_hbm, r_hbm, c_hbm, first, *scratch):
    parts, sem = scratch[0:3], scratch[3]
    odd = my_place()[1] & 1
    at = pl.multiple_of(48 * odd, 16)
    copies = [
        pltpu.make_async_copy(source.at[:, pl.ds(at, 16), :], target.reshape(8, 16, 128), sem.at[k])
        for k, (source, target) in enumerate(zip((g_hbm, r_hbm, c_hbm), parts))
    ]
    for copy in copies:
        copy.start()
    for copy in copies:
        copy.wait()
    even_y = (iota((4, 128), 1) & 1) == 0

    def rows(x, half, second_z):
        return pl.ds(half * 8 + x % 8 + 16 * second_z, 4, stride=32)

    @pl.when(odd == 1)
    def _():
        pack_edge(parts, True, rows, even_y, first)

    @pl.when(odd == 0)
    def _():
        pack_edge(parts, False, rows, even_y, first)


def parity(odd):
    return ((iota((8, 256), 1) + odd + 1) & 1) == 0


def nsum_packed(lv, v, xa, xb, ya, yb, i, p):
    here = v[i]
    t = xa[i] * v[i + 1] + xb[i - 1] * v[i - 1]
    t = t + (ya[i] * up(here, 1) + down(yb[i] * here, 1))
    cross = lv["c"][i]
    z = jnp.where(p, down(cross * here, 0), cross * up(here, 0))
    return t + (lv["s"][i] * here + z)


def sweep_packed(lv, red, first, last):
    def step(i, odd, carry):
        p = parity(odd)
        if red:
            n = nsum_packed(lv, lv["vB"], lv["xR"], lv["xB"], lv["yR"], lv["yB"], i, p)
            lv["vR"][i] = (lv["fR"][i] + n) * lv["iR"][i]
        else:
            p = jnp.logical_not(p)
            n = nsum_packed(lv, lv["vR"], lv["xB"], lv["xR"], lv["yB"], lv["yR"], i, p)
            lv["vB"][i] = (lv["fB"][i] + n) * lv["iB"][i]
        return carry

    planes(first, last, SWEEP, step)


def residual_packed(lv, i, odd):
    p = parity(odd)
    n = nsum_packed(lv, lv["vB"], lv["xR"], lv["xB"], lv["yR"], lv["yB"], i, p)
    r_red = lv["fR"][i] - (lv["cR"][i] * lv["vR"][i] - n)
    q = jnp.logical_not(p)
    n = nsum_packed(lv, lv["vR"], lv["xB"], lv["xR"], lv["yB"], lv["yR"], i, q)
    r_black = lv["fB"][i] - (lv["cB"][i] * lv["vB"][i] - n)
    return r_red, r_black, p


PACKED = ("vB", "fR", "fB", "xR", "xB", "yR", "yB", "s", "c", "iR", "iB", "cR", "cB")


FINE = PACKED + ("bE", "bO")


def stack(parts, at, i, out):
    for t in range(2):
        out[i, 4 * t : 4 * t + 4, :] = parts[t][at : at + 4, :]


def merge(parts, at, i, low, high):
    low_half = iota((8, 256), 0) < 4
    a, b = (part[at : at + 8, :] for part in parts)
    low[i] = jnp.where(low_half, a, pltpu.roll(b, 4, 0))
    high[i] = jnp.where(low_half, pltpu.roll(a, 4, 0), b)


def x_values(lv, i):
    return 0.5 * (lv["bE"][i] + lv["bE"][i + 1]), 0.5 * (lv["bO"][i] + lv["bO"][i + 1])


def x_faces(lv, i, p):
    fxe, fxo = x_values(lv, i)
    lv["xR"][i] = jnp.where(p, fxe, fxo)
    lv["xB"][i] = jnp.where(p, fxo, fxe)
    return fxe, fxo


def faces(lv, i, before, inside=None):
    row, lane = iota((8, 256), 0), iota((8, 256), 1)
    top, bot = row == 7, row == 0
    end, begin = lane == 255, lane == 0
    p = parity(i % 2)
    e, o = lv["bE"][i], lv["bO"][i]
    fxe, fxo = x_faces(lv, i, p)
    fye = 0.5 * (e + jnp.where(end, 0.0, up(e, 1)))
    fyo = 0.5 * (o + jnp.where(end, 0.0, up(o, 1)))
    gye = 0.5 * (e + jnp.where(begin, 0.0, down(e, 1)))
    gyo = 0.5 * (o + jnp.where(begin, 0.0, down(o, 1)))
    yr, yb = jnp.where(p, fye, fyo), jnp.where(p, fyo, fye)
    lv["yR"][i] = jnp.where(end, 0.0, yr)
    lv["yB"][i] = jnp.where(end, 0.0, yb)
    s = 0.5 * (e + o)
    above = 0.5 * (o + jnp.where(top, 0.0, up(e, 0)))
    below = 0.5 * (e + jnp.where(bot, 0.0, down(o, 0)))
    lv["s"][i] = s
    lv["c"][i] = jnp.where(top, 0.0, above)
    ce = fye + gye + (s + below) + (fxe + before[0])
    co = fyo + gyo + (s + above) + (fxo + before[1])
    cr, cb = jnp.where(p, ce, co), jnp.where(p, co, ce)
    lv["cR"][i] = cr
    lv["cB"][i] = cb
    ir, ib = 1.0 / cr, 1.0 / cb
    lv["iR"][i] = ir if inside is None else jnp.where(inside, ir, 0.0)
    lv["iB"][i] = ib if inside is None else jnp.where(inside, ib, 0.0)
    return fxe, fxo


def own_kernel(lo, hi, *refs):
    lv = dict(zip(FINE, refs))
    coarse, bottom, pair_b, tmp = refs[len(FINE) :]
    for x in range(32):
        source, base = (lo, x * ROWS) if x < 16 else (hi, (x - 16) * ROWS)
        parts = source.at[0], source.at[1]
        merge(parts, base, H0 + x, lv["bE"], lv["bO"])
        merge(parts, base + 8, H0 + x, lv["fR"], lv["fB"])
        stack(parts, base + 16, H0 + x, lv["vB"])
    before = x_values(lv, H0)
    for i in range(H0 + 1, H0 + 31):
        before = faces(lv, i, before)

    bE, bO = lv["bE"], lv["bO"]
    for j in range(16):
        i = H0 + 2 * j
        pair_b[j] = (bE[i] + bO[i]) + (bE[i + 1] + bO[i + 1])
    halve = one_hot((256, 128), lambda i, j: (i >> 1) == j)
    coarse[0:16] = (0.125 * matmul(pair_b[...].reshape(128, 256), halve)).reshape(16, 8, 128)
    for k in range(8):
        tmp[8 * k : 8 * k + 8, :] = coarse[2 * k] + coarse[2 * k + 1]
    summed = tmp[pl.ds(0, 32, stride=2), :] + tmp[pl.ds(1, 32, stride=2), :]
    halve = one_hot((128, 128), lambda i, j: (i >> 1) == j)
    coarse[16:20] = (0.125 * matmul(summed, halve)).reshape(4, 8, 128)
    bottom[...] = bottom_row([coarse[16 + k] + pltpu.roll(coarse[16 + k], 4, 0) for k in range(4)])


def fine_kernel(boxes, halo, coarse, *refs):
    refs = refs[len(FINE) :]
    lv = dict(zip(FINE, refs))
    f1, first, second, vR, pair_r = refs[len(FINE) :]
    lv["vR"] = vR
    box = my_place()[1]
    odd = box & 1
    for side, at in ((odd, 0), (1 - odd, H0 + 32)):
        parts = halo.at[0, side], halo.at[1, side]
        for k in range(H0):
            merge(parts, 8 * k, at + k, lv["bE"], lv["bO"])
            stack(parts, EDGE_V + 4 * k, at + k, lv["vB"])
        for k in range(H0 - 1):
            merge(parts, EDGE_F + 8 * k, (1 if at == 0 else at) + k, lv["fR"], lv["fB"])
    before = x_faces(lv, 0, parity(0))
    for i in range(1, H0 + 1):
        before = faces(lv, i, before, None if i == H0 else box > 0)
    before = x_values(lv, H0 + 30)
    for i in range(H0 + 31, N0 - 1):
        before = faces(lv, i, before, None if i == H0 + 31 else box < boxes - 1)

    for k in range(2):
        sweep_packed(lv, True, 1 + 2 * k, N0 - 1 - 2 * k)
        sweep_packed(lv, False, 2 + 2 * k, N0 - 2 - 2 * k)
    for j in range(16):
        i = H0 + 2 * j
        a, b, _ = residual_packed(lv, i, H0 % 2)
        c, d, _ = residual_packed(lv, i + 1, (H0 + 1) % 2)
        pair_r[j] = (a + b) + (c + d)
    halve = one_hot((256, 128), lambda i, j: (i >> 1) == j)
    f1[...] = (0.125 * matmul(pair_r[...].reshape(128, 256), halve)).reshape(16, 8, 128)

    for out, right in ((first, odd), (second, 1 - odd)):
        out[0:H1] = f1[pl.ds(right * (16 - H1), H1)]
        out[H1 : 2 * H1 + 1] = coarse[pl.ds(right * (15 - H1), H1 + 1)]
        out[2 * H1 + 1 :] = coarse[16:20]


def bottom_row(pairs):
    total = None
    for k, plane in enumerate(pairs):
        spread = one_hot((128, 128), lambda i, j, k=k: jnp.logical_and((i >> 1) + 32 * k == j, i < 64))
        part = matmul(plane, spread)
        total = part if total is None else total + part
    low, high = total[0:1] + total[1:2], total[2:3] + total[3:4]
    row = 0.125 * jnp.where(my_place()[0] == 0, low, high)
    return jnp.broadcast_to(row, (8, 128))


def level_faces(b, ax, ay, az, inv, centers, n, factor, depth, width, inside):
    row, lane = iota((8, 128), 0), iota((8, 128), 1)
    top, bot = row == depth - 1, row == 0
    end, begin = lane == width - 1, lane == 0
    cell = jnp.logical_and(row < depth, lane < width)
    ax[0] = factor * (b[0] + b[1])

    def step(i, odd, before):
        v = b[i]
        fx = factor * (v + b[i + 1])
        ax[i] = fx
        fy = factor * (v + jnp.where(end, 0.0, up(v, 1)))
        gy = factor * (v + jnp.where(begin, 0.0, down(v, 1)))
        fz = factor * (v + jnp.where(top, 0.0, up(v, 0)))
        gz = factor * (v + jnp.where(bot, 0.0, down(v, 0)))
        ay[i] = jnp.where(end, 0.0, fy)
        az[i] = jnp.where(top, 0.0, fz)
        center = (fz + gz) + (fx + before) + (fy + gy)
        centers[i] = center
        inv[i] = jnp.where(jnp.logical_and(cell, inside(i)), 1.0 / center, 0.0)
        return fx

    planes(1, n - 1, 99, step, ax[0])


def nsum_values(before, here, after, ax, ay, az, i):
    t = ax[i] * after + ax[i - 1] * before
    t = t + (ay[i] * up(here, 1) + down(ay[i] * here, 1))
    return t + (az[i] * up(here, 0) + down(az[i] * here, 0))


def nsum_plain(v, ax, ay, az, i):
    return nsum_values(v[i - 1], v[i], v[i + 1], ax, ay, az, i)


def colour(odd):
    return ((iota((8, 128), 0) + iota((8, 128), 1) + odd) & 1) == 0


def sweep_plain(v, f, ax, ay, az, inv, odd, shift, first, last):
    before, here = v[first - 1], v[first]
    for i in range(first, last):
        after = v[i + 1]
        n = nsum_values(before, here, after, ax, ay, az, i)
        v[i] = jnp.where(colour((i + shift + odd) % 2), (f[i] + n) * inv[i], here)
        before, here = here, after


def first_plain(v, f, inv, shift, first, last):
    def step(i, plane_odd, carry):
        v[i] = jnp.where(colour((plane_odd + shift) % 2), f[i] * inv[i], 0.0)
        return carry

    planes(first, last, 99, step)


def residual_plain(v, f, ax, ay, az, center, i):
    return f[i] - (center * v[i] - nsum_plain(v, ax, ay, az, i))


def middle_kernel(boxes, source, coarse, first, second, bottom, v1, f1, ax1, ay1, az1, inv1, ax2, ay2, az2, inv2, send, compact, message, v2, f2, b2, c2, b1, c1, tmp):
    box = my_place()[1]
    w = H1 + 1
    swapped = (box & 1) == 1

    def received(k, count):
        one, two = first[k : k + count], second[k : k + count]
        return jnp.where(swapped, two, one), jnp.where(swapped, one, two)

    left, right = received(H1, w)
    b1[0:w] = left
    b1[w : w + 16] = coarse[0:16]
    b1[w + 16 :] = right
    left, right = received(0, H1)
    f1[0:1] = jnp.zeros((1, 8, 128), F32)
    f1[1 : 1 + H1] = left
    f1[w : w + 16] = source[...]
    f1[w + 16 : w + 16 + H1] = right
    f1[N1 - 1 :] = jnp.zeros((1, 8, 128), F32)
    left, right = received(H1 + w, 4)
    b2[...] = jnp.zeros(b2.shape, F32)
    for at, part in ((0, left), (8, coarse[16:20]), (16, right)):
        for k in range(8):
            b2[at + k, 0:4, :] = part[k // 2, 4 * (k % 2) : 4 * (k % 2) + 4]
    v1[...] = jnp.zeros(v1.shape, F32)
    v2[...] = jnp.zeros(v2.shape, F32)
    f2[...] = jnp.zeros(f2.shape, F32)

    def within(size, width):
        def inside(i):
            x = box * size - width + i
            return jnp.logical_and(x >= 0, x < boxes * size)

        return inside

    k1, k2 = 0.5 * 0.25, 0.5 * 0.25**2
    level_faces(b1, ax1, ay1, az1, inv1, c1, N1, k1, 8, 128, within(16, w))
    level_faces(b2, ax2, ay2, az2, inv2, c2, N2, k2, 4, 64, within(8, 8))

    one = (f1, ax1, ay1, az1, inv1)
    first_plain(v1, f1, inv1, 1, 1, N1 - 1)
    sweep_plain(v1, *one, 1, 1, 2, N1 - 2)
    sweep_plain(v1, *one, 0, 1, 3, N1 - 3)
    sweep_plain(v1, *one, 1, 1, 4, N1 - 4)

    def restrict(j, carry):
        i = 5 + 2 * j
        parts = [residual_plain(v1, *one[:4], c1[k], k) for k in (i, i + 1)]
        tmp[8 * j : 8 * j + 8, :] = parts[0] + parts[1]
        return carry

    for j in range(16):
        restrict(j, 0)
    summed = tmp[pl.ds(0, 64, stride=2), :] + tmp[pl.ds(1, 64, stride=2), :]
    restricted = 0.125 * matmul(summed, one_hot((128, 128), lambda i, j: (i >> 1) == j))
    for j in range(16):
        f2[4 + j, 0:4, :] = restricted[4 * j : 4 * j + 4]

    two = (f2, ax2, ay2, az2, inv2)
    first_plain(v2, f2, inv2, 0, 4, 20)
    sweep_plain(v2, *two, 1, 0, 5, 19)
    sweep_plain(v2, *two, 0, 0, 6, 18)
    sweep_plain(v2, *two, 1, 0, 7, 17)
    send[0:8] = v2[8:16]
    send[8:16] = f2[8:16]
    for k in range(4):
        both = [pltpu.roll(ref[9 + 2 * k], 4, 0) + ref[8 + 2 * k] for ref in (v2, f2)]
        compact[k] = both[0] + pltpu.roll(both[1], 64, 1)

    pairs = []
    for k in range(4):
        parts = [
            residual_plain(v2, *two[:4], c2[i], i)
            for i in (8 + 2 * k, 9 + 2 * k)
        ]
        pairs.append(parts[0] + parts[1])
    rows = jnp.where((iota((8, 128), 0) & 1) == 0, bottom_row(pairs), bottom[...])
    for k in range(message.shape[0] // 8):
        message[8 * k : 8 * k + 8, :] = rows


def coarse_solve(source, coefficient, dref, sref, rref, eref):
    shape = source[0].shape
    groups = shape[0]
    group, row, lane = (iota(shape, k) for k in range(3))
    factor = 0.5 * 0.25**3
    last = jnp.logical_and(jnp.logical_and(group == groups - 1, row == 7), lane >= 96)
    first = jnp.logical_and(jnp.logical_and(group == 0, row == 0), lane < 32)
    inner_hi, inner_lo = lane < 96, lane >= 32
    end, begin = (lane & 31) == 31, (lane & 31) == 0

    def lanes(v, shift):
        return pltpu.roll(v.reshape(8 * groups, 128), shift, 1).reshape(shape)

    def xp(v):
        a = lanes(v, 96)
        return jnp.where(inner_hi, a, jnp.concatenate([a[1:], up(a[0], 0)[None]], axis=0))

    def xm(v):
        a = lanes(v, 32)
        return jnp.where(inner_lo, a, jnp.concatenate([down(a[groups - 1], 0)[None], a[:-1]], axis=0))

    ax, ay, center = [], [], []
    az = factor * (coefficient[0] + coefficient[1])
    for b in coefficient:
        fx = factor * (b + jnp.where(last, 0.0, xp(b)))
        gx = factor * (b + jnp.where(first, 0.0, xm(b)))
        fy = factor * (b + jnp.where(end, 0.0, lanes(b, 127)))
        gy = factor * (b + jnp.where(begin, 0.0, lanes(b, 1)))
        ax.append(jnp.where(last, 0.0, fx))
        ay.append(jnp.where(end, 0.0, fy))
        center.append((factor * b + az) + (fx + gx) + (fy + gy))

    def total(u, w):
        s = jnp.sum(u[0] * w[0] + u[1] * w[1], axis=0)
        return jnp.sum(jnp.sum(s, axis=0, keepdims=True), axis=1, keepdims=True)

    before = alpha = None
    for k in range(ITERS):
        r = [source[t] if k == 0 else rref[t] for t in range(2)]
        w = []
        for t in range(2):
            v = r[t]
            n = ax[t] * xp(v) + xm(ax[t] * v)
            n = n + (ay[t] * lanes(v, 127) + lanes(ay[t] * v, 1))
            w.append(center[t] * v - (n + az * r[1 - t]))
        rr, below = total(r, r), total(r, w)
        if k > 0:
            beta = rr / before
            below = below - beta * (rr / alpha)
        alpha = rr / below
        before = rr
        for t in range(2):
            d, image = (r[t], w[t]) if k == 0 else (r[t] + beta * dref[t], w[t] + beta * sref[t])
            eref[t] = alpha * d if k == 0 else eref[t] + alpha * d
            if k < ITERS - 1:
                dref[t] = d
                sref[t] = image
                rref[t] = r[t] - alpha * image


def coarse_kernel(boxes, gathered, e2, dref, sref, rref, eref, ordered):
    box = my_place()[1]
    groups = boxes // 8

    def load(t, at):
        return jnp.stack([gathered[t, pl.ds(2 * g + at, 8, stride=2 * groups), :] for g in range(groups)])

    coarse_solve([load(t, 0) for t in range(2)], [load(t, 1) for t in range(2)], dref, sref, rref, eref)
    for t in range(2):
        ordered[t, 0:8] = jnp.zeros((8, 128), F32)
        ordered[t, 8 + boxes :] = jnp.zeros((8, 128), F32)
        for g in range(groups):
            ordered[t, pl.ds(8 + g, 8, stride=groups), :] = eref[t, g]
    near = [ordered[t, pl.ds(7 + box, 8), :] for t in range(2)]
    spread = one_hot((128, 512), lambda i, j: jnp.logical_and(((j >> 7) * 32) + ((j & 127) >> 1) == i, (j & 127) < 64))
    fine = [matmul(e, spread) for e in near]
    row = iota((8, 128), 0)
    for i in range(N2):
        cell, k = (i // 2) // 4, (i // 2) % 4
        low, high = (f[cell : cell + 1, 128 * k : 128 * k + 128] for f in fine)
        e2[i] = jnp.where(row < 2, low, jnp.where(row < 4, high, 0.0))


def after_kernel(compact, black, gathered, first, second):
    del gathered
    odd = my_place()[1] & 1
    for out, right in ((first, odd), (second, 1 - odd)):
        out[0:4] = compact[...]
        start = H0 + right * (32 - H0)
        for k in range(H0):
            for half in range(2):
                out[4 + 2 * k + half] = black[start + k, :, 128 * half : 128 * half + 128]


def last_kernel(*refs):
    names = ("e2", "first", "second", "own2", "v1", "f1", "ax1", "ay1", "az1", "inv1", "ax2", "ay2", "az2", "inv2")
    given = dict(zip(names, refs))
    refs = refs[len(names) :]
    level0 = dict(zip(PACKED, refs))
    refs = refs[len(PACKED) :]
    out_v, out_r, vR, vB, v1, v2, f2, wide, e0 = refs
    slab, box = my_place()
    e2, first, second, own2 = given["e2"], given["first"], given["second"], given["own2"]
    swapped = (box & 1) == 1

    def received(side, k, count):
        one, two = (first, second) if side == 0 else (second, first)
        return jnp.where(swapped, two[k : k + count], one[k : k + count])

    v2[8:16] = own2[0:8]
    f2[8:16] = own2[8:16]
    quarter = jnp.logical_and(iota((8, 128), 0) < 4, iota((8, 128), 1) < 64)
    for side, at in ((0, 0), (1, 16)):
        four = received(side, 0, 4)
        for k in range(4):
            for ref, plane in ((v2, four[k]), (f2, pltpu.roll(four[k], 64, 1))):
                ref[at + 2 * k] = jnp.where(quarter, plane, 0.0)
                ref[at + 2 * k + 1] = jnp.where(quarter, pltpu.roll(plane, 4, 0), 0.0)
    for i in range(N2):
        v2[i] = v2[i] + e2[i]
    two = (f2, given["ax2"], given["ay2"], given["az2"], given["inv2"])
    for k in range(2):
        sweep_plain(v2, *two, 0, 0, 1 + 2 * k, N2 - 1 - 2 * k)
        sweep_plain(v2, *two, 1, 0, 2 + 2 * k, N2 - 2 - 2 * k)

    packed = jnp.concatenate([v2[4 + j, 0:4, :] for j in range(16)], axis=0)
    fine = matmul(packed, one_hot((128, 128), lambda i, j: (j >> 1) == i))
    wide[pl.ds(0, 64, stride=2), :] = fine
    wide[pl.ds(1, 64, stride=2), :] = fine
    for i in range(6, N1 - 6):
        j = (i + 3) // 2 - 4
        v1[i] = given["v1"][i] + wide[8 * j : 8 * j + 8, :]
    one = (given["f1"], given["ax1"], given["ay1"], given["az1"], given["inv1"])
    for k in range(2):
        sweep_plain(v1, *one, 0, 1, 7 + 2 * k, N1 - 7 - 2 * k)
        sweep_plain(v1, *one, 1, 1, 8 + 2 * k, N1 - 8 - 2 * k)

    double = one_hot((128, 256), lambda i, j: (j >> 1) == i)
    e0[...] = matmul(v1[10:32].reshape(176, 128), double).reshape(22, 8, 256)
    lv = dict(level0, vR=vR, vB=vB)

    black = level0["vB"]

    def correct(j, carry):
        e = e0[j]
        vB[2 * j - 1] = black[2 * j - 1] + e
        vB[2 * j] = black[2 * j] + e
        return carry

    lax.fori_loop(3, 19, correct, 0, unroll=4)
    for side, at in ((0, 0), (1, H0 + 32)):
        for k in range(H0):
            for half in range(2):
                lanes = slice(128 * half, 128 * half + 128)
                vB[at + k, :, lanes] = received(side, 4 + 2 * k + half, 1)[0] + e0[(at + k + 1) // 2, :, lanes]
    for k in range(2):
        sweep_packed(lv, True, 1 + 2 * k, N0 - 1 - 2 * k)
        sweep_packed(lv, False, 2 + 2 * k, N0 - 2 - 2 * k)


    def finish(i, odd, carry):
        x = i - H0
        red, black, p = residual_packed(lv, i, odd)
        for out, a, b in ((out_v, vR[i], vB[i]), (out_r, red, black)):
            for at, whole in ((0, jnp.where(p, a, b)), (1, jnp.where(p, b, a))):
                part = jnp.where(slab == 0, whole[0:4], whole[4:8])
                for half in range(2):
                    out[slab_rows(x, half, at), :] = part[:, 128 * half : 128 * half + 128]
        return carry

    planes(H0, H0 + 32, FINISH, finish)


def call(kernel, outs, scratch, *args, limit=12, aliases=()):
    vmem = pl.BlockSpec(memory_space=pltpu.VMEM)
    return pl.pallas_call(
        kernel,
        out_shape=[jax.ShapeDtypeStruct(s, F32) for s in outs],
        in_specs=[vmem] * len(args),
        out_specs=[vmem] * len(outs),
        input_output_aliases=dict(aliases),
        scratch_shapes=[pltpu.VMEM(s, F32) for s in scratch],
        compiler_params=pltpu.CompilerParams(vmem_limit_bytes=limit * 1024 * 1024),
    )(*args)


def edges(*args):
    return pl.pallas_call(
        edge_kernel,
        out_shape=jax.ShapeDtypeStruct((EDGE, 256), F32),
        in_specs=[pl.BlockSpec(memory_space=pl.ANY)] * 3,
        out_specs=pl.BlockSpec(memory_space=pltpu.VMEM),
        scratch_shapes=[pltpu.VMEM((128, 128), F32)] * 3 + [pltpu.SemaphoreType.DMA((3,))],
        compiler_params=pltpu.CompilerParams(vmem_limit_bytes=60 * 1024 * 1024),
    )(*[a.reshape(8, 64, 128) for a in args])


def by_tiles(a):
    return a.reshape(8, 4, 8, 2, 128).transpose(0, 1, 3, 2, 4).reshape(512, 128)


def from_tiles(a):
    return a.reshape(8, 4, 2, 8, 128).transpose(0, 1, 3, 2, 4).reshape(8, 32, 256)


def exchange(first, second):
    boxes = lax.axis_size("box")
    odd = [(i, i + 1) for i in range(1, boxes - 1, 2)]
    even = [(i, i + 1) for i in range(0, boxes - 1, 2)]
    return [lax.ppermute(x, "box", p + [(j, i) for i, j in p]) for x, p in ((first, odd), (second, even))]


def body(pressure_guess, right_side, coefficient):
    boxes = lax.axis_size("box")
    flat = [by_tiles(a) for a in (pressure_guess, right_side, coefficient)]
    first = edges(*flat)
    low, high, second = call(pack_kernel, [(16 * ROWS, 256)] * 2 + [(EDGE, 256)], [], *flat)
    first, second = exchange(first, second)
    low, high = lax.all_gather(low, "slab"), lax.all_gather(high, "slab")
    halo = lax.all_gather(jnp.stack([first, second]), "slab")

    plane = (N0, 8, 256)
    *arrays, coarse, bottom = call(
        own_kernel,
        [plane] * len(FINE) + [(20, 8, 128), (8, 128)],
        [(16, 8, 256), (64, 128)],
        low,
        high,
    )
    fine = call(
        functools.partial(fine_kernel, boxes),
        [plane] * len(FINE) + [(16, 8, 128), (SEND1, 8, 128), (SEND1, 8, 128)],
        [plane, (16, 8, 256)],
        halo,
        coarse,
        *arrays,
        aliases=[(2 + k, k) for k in range(len(FINE))],
    )
    level0 = fine[: len(PACKED)]
    source, first, second = fine[len(FINE) :]
    first, second = exchange(first, second)

    one, two = (N1, 8, 128), (N2, 8, 128)
    *levels, send, compact, message = call(
        functools.partial(middle_kernel, boxes),
        [one] * 6 + [two] * 4 + [(16, 8, 128), (4, 8, 128), (2 * boxes, 128)],
        [two] * 4 + [one, one, (128, 128)],
        source,
        coarse,
        first,
        second,
        bottom,
    )
    spread = lax.all_to_all(message.reshape(boxes, 2, 128), "box", 0, 0).reshape(2 * boxes, 128)
    first, second = exchange(*call(after_kernel, [(SEND2, 8, 128)] * 2, [], compact, level0[0], spread))
    gathered = lax.all_gather(spread, "slab")
    (e2,) = call(
        functools.partial(coarse_kernel, boxes),
        [two],
        [(2, boxes // 8, 8, 128)] * 4 + [(2, boxes + 16, 128)],
        gathered,
    )
    pressure, residual = call(
        last_kernel,
        [(512, 128)] * 2,
        [plane, plane, one, two, two, (128, 128), (22, 8, 256)],
        e2,
        first,
        second,
        send,
        *levels,
        *level0,
    )
    return from_tiles(pressure), from_tiles(residual)


def solution(mesh):
    split = P("slab", "box", None)
    return jax.shard_map(body, mesh=mesh, in_specs=(split,) * 3, out_specs=(split,) * 2, check_vma=False)
```
